512 devices in a mesh: pair: 128 (over x, z, core), aux: 4 (over y).
Axes of the slice: x: 4, y: 4, z: 16, core: 2. Of those that a mesh axis runs over, the one named last changes fastest.
Arguments:
- integrals: bfloat16 [8192, 256, 256], P('pair', 'aux'), may hold values from -4 to 4
- amplitudes: bfloat16 [8192, 128, 128], P(('pair', 'aux')), may hold values from -4 to 4
- coeffs: bfloat16 [8192, 128, 128], P(('pair', 'aux')), may hold values from -0.5 to 0.5
- domains: int32 [8192, 128], P(('pair', 'aux')), may hold values from 0 to 4247, as said below
- neighbours: int32 [8192, 8], P(('pair', 'aux')), may hold values from 0 to 8191, as said below
- counts: int32 [8192], P(('pair', 'aux')), may hold values from 1 to 8, as said below
- couplings: float32 [8192, 8], P(('pair', 'aux')), may hold values from -1 to 1
- pno_energies: float32 [8192, 128], P(('pair', 'aux')), may hold values from 0.3 to 3
- occ_energies: float32 [8192], P(('pair', 'aux')), may hold values from 1 to 4
Outputs:
- residual: float32 [8192, 128, 128], P(('pair', 'aux'))
- updated_amplitudes: bfloat16 [8192, 128, 128], P(('pair', 'aux'))
The draws below stay inside these ranges and needn't reach their ends.
Inputs may be any that keep to these rules, and one draw needn't show every extreme that they name: `domains`: each row holds 128 distinct PAO numbers in rising order. `neighbours`: pairs are numbered device by device along pair+aux, 16 a device; every slot of pair p names a pair whose device differs from p's device by at most 1. Only the first counts[p] slots of pair p are active.
All inputs are finite; a program needn't handle non-finite values.
Results may differ from the reference program's by a relative error of at most 0.0034.
Values may be sent and summed in bfloat16 or wider, within the bound.
A program may use at most 128 MiB of HBM per device.

```python
import math
import jax
import jax.numpy as jnp
from jax import lax

NPNO = 128
DOM = 128
NAUX = 256
NB = 8
REACH = 1
PAIRS_DEV = 16
PAIRS = 8192


def draw_domains(key, part):
    key = jax.random.fold_in(key, 11)
    window = DOM + DOM // 4
    pair_keys = jax.random.split(key, PAIRS)

    def draw_row(row_key):
        subset = jax.random.permutation(row_key, window - 2)[:DOM - 2] + 1
        return jnp.sort(subset)
    middle = jax.vmap(draw_row)(pair_keys).astype(jnp.int32)
    lowest = jnp.zeros((PAIRS, 1), jnp.int32)
    highest = jnp.full((PAIRS, 1), window - 1, jnp.int32)
    rows_all = jnp.concatenate([lowest, middle, highest], axis=1)
    offsets = jnp.arange(PAIRS, dtype=jnp.int32) // PAIRS_DEV * (DOM // 16)
    return (rows_all + offsets[:, None]).astype(jnp.int32)


def draw_neighbours(key, part):
    key = jax.random.fold_in(key, 12)
    device_count = PAIRS // PAIRS_DEV
    owner = jnp.arange(PAIRS, dtype=jnp.int32) // PAIRS_DEV
    lowest = jnp.maximum(owner - REACH, 0) * PAIRS_DEV
    highest = jnp.minimum(owner + REACH + 1, device_count) * PAIRS_DEV
    chosen = jax.random.randint(key, (PAIRS, NB), lowest[:, None], highest[:, None], dtype=jnp.int32)
    far_device = jnp.where(owner + REACH < device_count, owner + REACH, owner - REACH)
    leading = jnp.arange(PAIRS, dtype=jnp.int32) % PAIRS_DEV == 0
    chosen = chosen.at[:, 0].set(jnp.where(leading, far_device * PAIRS_DEV, chosen[:, 0]))
    chosen = chosen.at[0, 1].set(0)
    chosen = chosen.at[PAIRS - 1, 1].set(PAIRS - 1)
    return chosen.astype(jnp.int32)


def draw_counts(key, part):
    key = jax.random.fold_in(key, 13)
    chosen = jax.random.randint(key, (PAIRS,), 1, NB + 1, dtype=jnp.int32)
    chosen = chosen.at[0].set(NB)
    chosen = chosen.at[1].set(1)
    return chosen.astype(jnp.int32)


def shard_levels(rng, dims, cuts, least, top_value):
    def one(dim, parts):
        steps = jax.random.uniform(jax.random.fold_in(jax.random.fold_in(rng, 6), dim), (parts,), jnp.float32, least / len(cuts), top_value / len(cuts))
        return jnp.repeat(jnp.exp(steps), dims[dim] // parts).reshape((-1,) + (1,) * (len(dims) - dim - 1))

    loudness = one(*cuts[0])
    for cut in cuts[1:]:
        loudness = loudness * one(*cut)
    return loudness


def normal_values(rng, extent, width, bound, cuts=(), kind=jnp.bfloat16):
    entries = width * jax.random.normal(rng, extent, jnp.float32)
    if cuts:
        entries = entries * shard_levels(rng, extent, cuts, -0.22, 0.18)
    return jnp.clip(entries, -bound, bound).astype(kind)


def setup_inputs(seed: int = 0) -> dict:
    streams_of = jax.random.split(jax.random.key(seed), 10)
    integrals = normal_values(streams_of[0], (PAIRS, NAUX, 2 * NPNO), 0.25, 4.0, ((0, 128), (1, 4)))
    amplitudes = normal_values(streams_of[1], (PAIRS, NPNO, NPNO), 0.3, 4.0, ((0, 512),))
    coeffs = normal_values(streams_of[2], (PAIRS, DOM, NPNO), NPNO ** -0.5, 0.5, ((0, 512),))
    domains = draw_domains(jax.random.fold_in(streams_of[9], 71), 0)
    neighbours = draw_neighbours(jax.random.fold_in(streams_of[9], 71), 0)
    counts = draw_counts(jax.random.fold_in(streams_of[9], 71), 0)
    couplings = jnp.clip(jax.random.uniform(streams_of[6], (PAIRS, NB), jnp.float32, -1.0, 1.0) * shard_levels(streams_of[6], (PAIRS, NB), ((0, 512),), -0.4, 0.0), -1.0, 1.0)
    pno_energies = jnp.clip(jnp.exp(math.log(3.0) - 2.3025851 * jax.random.uniform(streams_of[7], (PAIRS, NPNO), jnp.float32) ** shard_levels(streams_of[7], (PAIRS, NPNO), ((0, 512),), -0.2, 0.2)), 0.3, 3.0)
    occ_energies = jnp.clip(1.0 + 3.0 * jax.random.uniform(streams_of[8], (PAIRS,), jnp.float32) ** shard_levels(streams_of[8], (PAIRS,), ((0, 512),), -0.2, 0.2), 1.0, 4.0)
    return dict(integrals=integrals, amplitudes=amplitudes, coeffs=coeffs, domains=domains, neighbours=neighbours, counts=counts, couplings=couplings, pno_energies=pno_energies, occ_energies=occ_energies)


def pno_to_pao(amplitudes, coeffs):
    left_half = jnp.einsum("pdn,pnm->pdm", coeffs.astype(jnp.float32), amplitudes.astype(jnp.float32)).astype(jnp.bfloat16)
    return jnp.einsum("pdm,pem->pde", left_half.astype(jnp.float32), coeffs.astype(jnp.float32)).astype(jnp.bfloat16)


def reference(integrals, amplitudes, coeffs, domains, neighbours, counts, couplings, pno_energies, occ_energies):
    block_count = PAIRS // PAIRS_DEV
    pao_amps = lax.map(lambda blocks_in: pno_to_pao(blocks_in[0], blocks_in[1]),
                       (amplitudes.reshape(block_count, PAIRS_DEV, NPNO, NPNO),
                        coeffs.reshape(block_count, PAIRS_DEV, DOM, NPNO)))
    pao_amps = pao_amps.reshape(PAIRS, DOM, DOM)

    def one_block(blocks_in):
        ints_here, amps_here, coeffs_here, domains_here, nbr_here, counts_here, couplings_here, pno_here, occ_here = blocks_in
        exchange_part = jnp.einsum("pqa,pqb->pab", ints_here[:, :, :NPNO].astype(jnp.float32), ints_here[:, :, NPNO:].astype(jnp.float32))
        far_amps = pao_amps[nbr_here]
        far_domains = domains[nbr_here]
        matches = (domains_here[:, None, :, None] == far_domains[:, :, None, :]).astype(jnp.float32)
        select = jnp.einsum("pan,pkab->pknb", coeffs_here.astype(jnp.float32), matches).astype(jnp.bfloat16)
        half_done = jnp.einsum("pknb,pkbe->pkne", select.astype(jnp.float32), far_amps.astype(jnp.float32)).astype(jnp.bfloat16)
        projected = jnp.einsum("pkne,pkme->pknm", half_done.astype(jnp.float32), select.astype(jnp.float32))
        slots = lax.broadcasted_iota(jnp.int32, couplings_here.shape, 1)
        weights = jnp.where(slots < counts_here[:, None], couplings_here, jnp.zeros_like(couplings_here))
        coupled = jnp.einsum("pk,pknm->pnm", weights, projected, precision=lax.Precision.HIGHEST)
        denominator = pno_here[:, :, None] + pno_here[:, None, :] + occ_here[:, None, None]
        residual = exchange_part + denominator * amps_here.astype(jnp.float32) + coupled
        updated = (amps_here.astype(jnp.float32) - residual / denominator).astype(jnp.bfloat16)
        return residual, updated

    residual, updated = lax.map(one_block, (
        integrals.reshape(block_count, PAIRS_DEV, NAUX, 2 * NPNO),
        amplitudes.reshape(block_count, PAIRS_DEV, NPNO, NPNO),
        coeffs.reshape(block_count, PAIRS_DEV, DOM, NPNO),
        domains.reshape(block_count, PAIRS_DEV, DOM),
        neighbours.reshape(block_count, PAIRS_DEV, NB),
        counts.reshape(block_count, PAIRS_DEV),
        couplings.reshape(block_count, PAIRS_DEV, NB),
        pno_energies.reshape(block_count, PAIRS_DEV, NPNO),
        occ_energies.reshape(block_count, PAIRS_DEV)))
    return residual.reshape(PAIRS, NPNO, NPNO), updated.reshape(PAIRS, NPNO, NPNO)
```

```python
import jax
import jax.numpy as jnp
from jax import lax
from jax.experimental import pallas as pl
from jax.experimental.pallas import tpu as pltpu
from jax.sharding import PartitionSpec as P

MESH = pl.DeviceIdType.MESH
F32 = jnp.float32
BF16 = jnp.bfloat16
CHUNK = 4


def contract(a, b, dim_a, dim_b):
    return lax.dot_general(a, b, (((dim_a,), (dim_b,)), ((), ())), preferred_element_type=F32)


def kernel(
    ints, amps_in, coeffs_in, domains_in, neighbours, counts, couplings,
    out,
    amps, coeffs, pao, doms, own, via, summed, arrived, acc,
    load_sem, own_sem, via_sem, raw_send, raw_recv, near_send, near_recv,
    summed_send, summed_recv, halo_send, halo_recv, dom_send, dom_recv, out_sem,
):
    n_pair, n_aux = lax.axis_size("pair"), lax.axis_size("aux")
    pair, aux = lax.axis_index("pair"), lax.axis_index("aux")
    pairs = amps.shape[0]
    half = pairs // 2
    depth = ints.shape[1]
    width = amps.shape[1]
    slots = neighbours.shape[0]
    chunks = half // CHUNK

    up, down, far = (aux + 1) % n_aux, (aux + n_aux - 1) % n_aux, (aux + 2) % n_aux
    to_up, to_down = (pair, up), (pair, down)
    to_right = ((pair + (aux + 1) // n_aux) % n_pair, up)
    to_left = ((pair + n_pair - (n_aux - aux) // n_aux) % n_pair, down)

    barrier = pltpu.get_barrier_semaphore()
    for device in (to_up, to_down, to_right, to_left):
        pl.semaphore_signal(barrier, inc=1, device_id=device, device_id_type=MESH)

    def remote(src, dst, send, recv, device):
        return pltpu.make_async_remote_copy(
            src_ref=src, dst_ref=dst, send_sem=send, recv_sem=recv, device_id=device, device_id_type=MESH
        )

    def rows(first, count=CHUNK):
        return pl.ds(first, count)

    loads = [
        pltpu.make_async_copy(coeffs_in, coeffs, load_sem.at[0]),
        pltpu.make_async_copy(amps_in, amps, load_sem.at[1]),
        pltpu.make_async_copy(domains_in, doms.at[rows(pairs, pairs)], load_sem.at[2]),
    ]
    via_loads = [
        pltpu.make_async_copy(
            ints.at[rows(down * pairs, half)], via.at[0, :, pl.ds(0, depth)], via_sem.at[0]
        ),
        pltpu.make_async_copy(
            ints.at[rows(up * pairs + half, half)], via.at[1, :, pl.ds(0, depth)], via_sem.at[1]
        ),
    ]
    own_load = pltpu.make_async_copy(ints.at[rows(aux * pairs, pairs)], own.at[:, pl.ds(0, depth)], own_sem)
    for copy in loads + via_loads + [own_load]:
        copy.start()

    for copy in loads:
        copy.wait()

    def to_pao(p, carry):
        c = coeffs[p]
        left_half = contract(c, amps[p], 1, 0).astype(BF16)
        pao[pairs + p] = contract(left_half, c, 1, 1).astype(BF16)
        return carry

    lax.fori_loop(0, pairs, to_pao, 0)

    pl.semaphore_wait(barrier, 4)

    raw = []
    for c in range(chunks):
        for side, device in ((0, to_down), (1, to_up)):
            raw.append(
                remote(
                    ints.at[rows(far * pairs + side * half + c * CHUNK)],
                    via.at[side, rows(c * CHUNK), pl.ds(depth, depth)],
                    raw_send.at[side, c],
                    raw_recv.at[side, c],
                    device,
                )
            )
    halo = []
    for side, device in ((0, to_right), (1, to_left)):
        halo.append(
            remote(
                doms.at[rows(pairs, pairs)],
                doms.at[rows(side * 2 * pairs, pairs)],
                dom_send.at[side],
                dom_recv.at[side],
                device,
            )
        )
    for c in range(pairs // CHUNK):
        for side, device in ((0, to_right), (1, to_left)):
            halo.append(
                remote(
                    pao.at[rows(pairs + c * CHUNK)],
                    pao.at[rows(side * 2 * pairs + c * CHUNK)],
                    halo_send.at[side, c],
                    halo_recv.at[side, c],
                    device,
                )
            )
    for copy in raw + halo:
        copy.start()

    for copy in via_loads:
        copy.wait()
    sums = []
    for c in range(chunks):
        for side, device in ((0, to_down), (1, to_up)):
            raw[c * 2 + side].wait_recv()

            def add_up(i, carry, side=side, c=c):
                p = c * CHUNK + i
                block = via[side, p]
                summed[side, p] = contract(block[:, :width], block[:, width:], 0, 0).astype(BF16)
                return carry

            lax.fori_loop(0, CHUNK, add_up, 0)
            copy = remote(
                summed.at[side, rows(c * CHUNK)],
                arrived.at[rows(side * half + c * CHUNK)],
                summed_send.at[side, c],
                summed_recv.at[side, c],
                device,
            )
            copy.start()
            sums.append(copy)

    for copy in halo:
        copy.wait_send()

    near = []
    for c in range(chunks):
        for side, device, there in ((0, to_up, up), (1, to_down, down)):
            copy = remote(
                ints.at[rows(there * pairs + side * half + c * CHUNK)],
                own.at[rows(side * half + c * CHUNK), pl.ds(depth, depth)],
                near_send.at[side, c],
                near_recv.at[side, c],
                device,
            )
            copy.start()
            near.append(copy)

    for copy in halo:
        copy.wait_recv()

    first_row = ((pair * n_aux + aux) - 1) * pairs

    def couple(p, carry):
        mine = jnp.broadcast_to(doms[pl.ds(pairs + p, 1), :], (width, width)).T
        matches, scaled = [], []
        for k in range(slots):
            row = jnp.clip(neighbours[k, p] - first_row, 0, 3 * pairs - 1)
            weight = jnp.where(k < counts[p], couplings[k, p], 0.0)
            match = jnp.where(mine == doms[pl.ds(row, 1), :], 1.0, 0.0).astype(BF16)
            picked = contract(match, pao[row], 1, 0)
            matches.append(match)
            scaled.append((weight * picked).astype(BF16))
        total = contract(jnp.concatenate(scaled, axis=1), jnp.concatenate(matches, axis=1), 1, 1)
        c = coeffs[p]
        right_half = contract(total.astype(BF16), c, 1, 0).astype(BF16)
        acc[p] = contract(c, right_half, 0, 0)
        return carry

    lax.fori_loop(0, pairs, couple, 0)

    own_load.wait()
    stores = []
    for c in range(chunks):
        for side in (0, 1):
            near[c * 2 + side].wait_recv()
            sums[c * 2 + side].wait_recv()
            first = side * half + c * CHUNK

            def finish(i, carry, first=first):
                p = first + i
                block = own[p]
                acc[p] += contract(block[:, :width], block[:, width:], 0, 0) + arrived[p].astype(F32)
                return carry

            lax.fori_loop(0, CHUNK, finish, 0)
            copy = pltpu.make_async_copy(acc.at[rows(first)], out.at[rows(first)], out_sem.at[side, c])
            copy.start()
            stores.append(copy)

    for copy in raw + near + sums:
        copy.wait_send()
    for copy in stores:
        copy.wait()


def per_device(
    integrals,
    amplitudes,
    coeffs,
    domains,
    neighbours,
    counts,
    couplings,
    pno_energies,
    occ_energies,
):
    pairs, width, _ = amplitudes.shape
    depth = integrals.shape[1]
    half = pairs // 2
    chunks = half // CHUNK
    anywhere = pl.BlockSpec(memory_space=pl.ANY)
    scalars = pl.BlockSpec(memory_space=pltpu.SMEM)
    dma = pltpu.SemaphoreType.DMA
    gathered = pl.pallas_call(
        kernel,
        out_shape=jax.ShapeDtypeStruct((pairs, width, width), F32),
        in_specs=[anywhere] * 4 + [scalars] * 3,
        out_specs=anywhere,
        scratch_shapes=[
            pltpu.VMEM((pairs, width, width), BF16),
            pltpu.VMEM((pairs, width, width), BF16),
            pltpu.VMEM((3 * pairs, width, width), BF16),
            pltpu.VMEM((3 * pairs, width), jnp.int32),
            pltpu.VMEM((pairs, 2 * depth, 2 * width), BF16),
            pltpu.VMEM((2, half, 2 * depth, 2 * width), BF16),
            pltpu.VMEM((2, half, width, width), BF16),
            pltpu.VMEM((pairs, width, width), BF16),
            pltpu.VMEM((pairs, width, width), F32),
            dma((3,)),
            dma(()),
            dma((2,)),
            dma((2, chunks)),
            dma((2, chunks)),
            dma((2, chunks)),
            dma((2, chunks)),
            dma((2, chunks)),
            dma((2, chunks)),
            dma((2, 2 * chunks)),
            dma((2, 2 * chunks)),
            dma((2,)),
            dma((2,)),
            dma((2, chunks)),
        ],
        compiler_params=pltpu.CompilerParams(
            collective_id=0, has_side_effects=True, vmem_limit_bytes=32 * 1024 * 1024
        ),
        name="contract_and_couple",
    )(integrals, amplitudes, coeffs, domains, neighbours.T, counts, couplings.T)
    denominator = pno_energies[:, :, None] + pno_energies[:, None, :] + occ_energies[:, None, None]
    amps_wide = amplitudes.astype(F32)
    residual = gathered + denominator * amps_wide
    updated = (amps_wide - residual / denominator).astype(BF16)
    return (residual, updated)


def solution(mesh):
    in_specs = (
        P("pair", "aux", None),
        P(("pair", "aux"), None, None),
        P(("pair", "aux"), None, None),
        P(("pair", "aux"), None),
        P(("pair", "aux"), None),
        P(("pair", "aux")),
        P(("pair", "aux"), None),
        P(("pair", "aux"), None),
        P(("pair", "aux")),
    )
    out_specs = (P(("pair", "aux"), None, None), P(("pair", "aux"), None, None))
    return jax.shard_map(
        per_device, mesh=mesh, in_specs=in_specs, out_specs=out_specs, check_vma=False
    )
```

```python
import jax
import jax.numpy as jnp
from jax import lax
from jax.experimental import pallas as pl
from jax.experimental.pallas import tpu as pltpu
from jax.sharding import PartitionSpec as P

MESH = pl.DeviceIdType.MESH
F32 = jnp.float32
BF16 = jnp.bfloat16
CHUNK = 4


def contract(a, b, dim_a, dim_b):
    return lax.dot_general(a, b, (((dim_a,), (dim_b,)), ((), ())), preferred_element_type=F32)


def kernel(
    ints, amps_in, coeffs_in, domains_in, neighbours_in, counts_in, couplings_in,
    out,
    amps, coeffs, pao, doms, neighbours, counts, couplings, own, via, summed, arrived, acc,
    load_sem, own_sem, via_sem, raw_send, raw_recv, near_send, near_recv,
    summed_send, summed_recv, halo_send, halo_recv, dom_send, dom_recv, out_sem,
):
    n_pair, n_aux = lax.axis_size("pair"), lax.axis_size("aux")
    pair, aux = lax.axis_index("pair"), lax.axis_index("aux")
    pairs = amps.shape[0]
    half = pairs // 2
    depth = ints.shape[1]
    width = amps.shape[1]
    slots = neighbours.shape[0]
    chunks = half // CHUNK

    up, down, far = (aux + 1) % n_aux, (aux + n_aux - 1) % n_aux, (aux + 2) % n_aux
    to_up, to_down = (pair, up), (pair, down)
    to_right = ((pair + (aux + 1) // n_aux) % n_pair, up)
    to_left = ((pair + n_pair - (n_aux - aux) // n_aux) % n_pair, down)

    barrier = pltpu.get_barrier_semaphore()
    for device in (to_up, to_down, to_right, to_left):
        pl.semaphore_signal(barrier, inc=1, device_id=device, device_id_type=MESH)

    def remote(src, dst, send, recv, device):
        return pltpu.make_async_remote_copy(
            src_ref=src, dst_ref=dst, send_sem=send, recv_sem=recv, device_id=device, device_id_type=MESH
        )

    def rows(first, count=CHUNK):
        return pl.ds(first, count)

    loads = [
        pltpu.make_async_copy(coeffs_in, coeffs, load_sem.at[0]),
        pltpu.make_async_copy(amps_in, amps, load_sem.at[1]),
        pltpu.make_async_copy(domains_in, doms.at[rows(pairs, pairs)], load_sem.at[2]),
    ]
    scalar_loads = [
        pltpu.make_async_copy(neighbours_in, neighbours, load_sem.at[3]),
        pltpu.make_async_copy(counts_in, counts, load_sem.at[4]),
        pltpu.make_async_copy(couplings_in, couplings, load_sem.at[5]),
    ]
    via_loads = [
        pltpu.make_async_copy(
            ints.at[rows(down * pairs, half)], via.at[0, :, pl.ds(0, depth)], via_sem.at[0]
        ),
        pltpu.make_async_copy(
            ints.at[rows(up * pairs + half, half)], via.at[1, :, pl.ds(0, depth)], via_sem.at[1]
        ),
    ]
    own_load = pltpu.make_async_copy(ints.at[rows(aux * pairs, pairs)], own.at[:, pl.ds(0, depth)], own_sem)
    for copy in loads + via_loads + [own_load] + scalar_loads:
        copy.start()

    pl.semaphore_wait(barrier, 4)

    raw = []
    for c in range(chunks):
        for side, device in ((0, to_down), (1, to_up)):
            copy = remote(
                ints.at[rows(far * pairs + side * half + c * CHUNK)],
                via.at[side, rows(c * CHUNK), pl.ds(depth, depth)],
                raw_send.at[side, c],
                raw_recv.at[side, c],
                device,
            )
            copy.start()
            raw.append(copy)

    for copy in loads:
        copy.wait()

    halo = []
    for side, device in ((0, to_right), (1, to_left)):
        copy = remote(
            doms.at[rows(pairs, pairs)],
            doms.at[rows(side * 2 * pairs, pairs)],
            dom_send.at[side],
            dom_recv.at[side],
            device,
        )
        copy.start()
        halo.append(copy)
    for c in range(pairs // CHUNK):

        def to_pao(i, carry, c=c):
            p = c * CHUNK + i
            block = coeffs[p]
            left_half = contract(block, amps[p], 1, 0).astype(BF16)
            pao[pairs + p] = contract(left_half, block, 1, 1).astype(BF16)
            return carry

        lax.fori_loop(0, CHUNK, to_pao, 0)
        for side, device in ((0, to_right), (1, to_left)):
            copy = remote(
                pao.at[rows(pairs + c * CHUNK)],
                pao.at[rows(side * 2 * pairs + c * CHUNK)],
                halo_send.at[side, c],
                halo_recv.at[side, c],
                device,
            )
            copy.start()
            halo.append(copy)

    for copy in via_loads:
        copy.wait()
    sums = []
    for c in range(chunks):
        for side, device in ((0, to_down), (1, to_up)):
            raw[c * 2 + side].wait_recv()

            def add_up(i, carry, side=side, c=c):
                p = c * CHUNK + i
                block = via[side, p]
                summed[side, p] = contract(block[:, :width], block[:, width:], 0, 0).astype(BF16)
                return carry

            lax.fori_loop(0, CHUNK, add_up, 0)
            copy = remote(
                summed.at[side, rows(c * CHUNK)],
                arrived.at[rows(side * half + c * CHUNK)],
                summed_send.at[side, c],
                summed_recv.at[side, c],
                device,
            )
            copy.start()
            sums.append(copy)

    for copy in halo[:-2]:
        copy.wait_send()

    near = []
    for c in range(chunks):
        for side, device, there in ((0, to_up, up), (1, to_down, down)):
            copy = remote(
                ints.at[rows(there * pairs + side * half + c * CHUNK)],
                own.at[rows(side * half + c * CHUNK), pl.ds(depth, depth)],
                near_send.at[side, c],
                near_recv.at[side, c],
                device,
            )
            copy.start()
            near.append(copy)

    halo[-2].wait_send()
    halo[-1].wait_send()
    for copy in halo:
        copy.wait_recv()
    for copy in scalar_loads:
        copy.wait()

    first_row = ((pair * n_aux + aux) - 1) * pairs

    def couple(p, carry):
        mine = jnp.broadcast_to(doms[pl.ds(pairs + p, 1), :], (width, width)).T
        matches, scaled = [], []
        for k in range(slots):
            row = jnp.clip(neighbours[k, p] - first_row, 0, 3 * pairs - 1)
            weight = jnp.where(k < counts[p], couplings[k, p], 0.0)
            match = jnp.where(mine == doms[pl.ds(row, 1), :], 1.0, 0.0).astype(BF16)
            picked = contract(match, pao[row], 1, 0)
            matches.append(match)
            scaled.append((weight * picked).astype(BF16))
        total = contract(jnp.concatenate(scaled, axis=1), jnp.concatenate(matches, axis=1), 1, 1)
        c = coeffs[p]
        right_half = contract(total.astype(BF16), c, 1, 0).astype(BF16)
        acc[p] = contract(c, right_half, 0, 0)
        return carry

    lax.fori_loop(0, pairs, couple, 0)

    own_load.wait()
    stores = []
    for c in range(chunks):
        for side in (0, 1):
            near[c * 2 + side].wait_recv()
            sums[c * 2 + side].wait_recv()
            first = side * half + c * CHUNK

            def finish(i, carry, first=first):
                p = first + i
                block = own[p]
                acc[p] += contract(block[:, :width], block[:, width:], 0, 0) + arrived[p].astype(F32)
                return carry

            lax.fori_loop(0, CHUNK, finish, 0)
            copy = pltpu.make_async_copy(acc.at[rows(first)], out.at[rows(first)], out_sem.at[side, c])
            copy.start()
            stores.append(copy)

    for copy in raw + near + sums:
        copy.wait_send()
    for copy in stores:
        copy.wait()


def per_device(
    integrals,
    amplitudes,
    coeffs,
    domains,
    neighbours,
    counts,
    couplings,
    pno_energies,
    occ_energies,
):
    pairs, width, _ = amplitudes.shape
    depth = integrals.shape[1]
    half = pairs // 2
    chunks = half // CHUNK
    anywhere = pl.BlockSpec(memory_space=pl.ANY)
    in_hbm = pl.BlockSpec(memory_space=pltpu.HBM)
    dma = pltpu.SemaphoreType.DMA
    gathered = pl.pallas_call(
        kernel,
        out_shape=jax.ShapeDtypeStruct((pairs, width, width), F32),
        in_specs=[in_hbm] * 7,
        out_specs=anywhere,
        scratch_shapes=[
            pltpu.VMEM((pairs, width, width), BF16),
            pltpu.VMEM((pairs, width, width), BF16),
            pltpu.VMEM((3 * pairs, width, width), BF16),
            pltpu.VMEM((3 * pairs, width), jnp.int32),
            pltpu.SMEM(neighbours.shape[::-1], jnp.int32),
            pltpu.SMEM(counts.shape, jnp.int32),
            pltpu.SMEM(couplings.shape[::-1], F32),
            pltpu.VMEM((pairs, 2 * depth, 2 * width), BF16),
            pltpu.VMEM((2, half, 2 * depth, 2 * width), BF16),
            pltpu.VMEM((2, half, width, width), BF16),
            pltpu.VMEM((pairs, width, width), BF16),
            pltpu.VMEM((pairs, width, width), F32),
            dma((6,)),
            dma(()),
            dma((2,)),
            dma((2, chunks)),
            dma((2, chunks)),
            dma((2, chunks)),
            dma((2, chunks)),
            dma((2, chunks)),
            dma((2, chunks)),
            dma((2, 2 * chunks)),
            dma((2, 2 * chunks)),
            dma((2,)),
            dma((2,)),
            dma((2, chunks)),
        ],
        compiler_params=pltpu.CompilerParams(
            collective_id=0, has_side_effects=True, vmem_limit_bytes=32 * 1024 * 1024
        ),
        name="contract_and_couple",
    )(
        *(
            pltpu.with_memory_space_constraint(operand, pltpu.HBM)
            for operand in (integrals, amplitudes, coeffs, domains, neighbours.T, counts, couplings.T)
        )
    )
    denominator = pno_energies[:, :, None] + pno_energies[:, None, :] + occ_energies[:, None, None]
    amps_wide = amplitudes.astype(F32)
    residual = gathered + denominator * amps_wide
    updated = (amps_wide - residual / denominator).astype(BF16)
    return (residual, updated)


def solution(mesh):
    in_specs = (
        P("pair", "aux", None),
        P(("pair", "aux"), None, None),
        P(("pair", "aux"), None, None),
        P(("pair", "aux"), None),
        P(("pair", "aux"), None),
        P(("pair", "aux")),
        P(("pair", "aux"), None),
        P(("pair", "aux"), None),
        P(("pair", "aux")),
    )
    out_specs = (P(("pair", "aux"), None, None), P(("pair", "aux"), None, None))
    return jax.shard_map(
        per_device, mesh=mesh, in_specs=in_specs, out_specs=out_specs, check_vma=False
    )
```

```python
import jax
import jax.numpy as jnp
from jax import lax
from jax.experimental import pallas as pl
from jax.experimental.pallas import tpu as pltpu
from jax.sharding import PartitionSpec as P

MESH = pl.DeviceIdType.MESH
F32 = jnp.float32
BF16 = jnp.bfloat16
CHUNK = 4
TOGETHER = 4


def contract(a, b, dim_a, dim_b):
    return lax.dot_general(a, b, (((dim_a,), (dim_b,)), ((), ())), preferred_element_type=F32)


def kernel(
    ints, amps_in, coeffs_in, domains_in, neighbours_in, counts_in, couplings_in, pno_in, occ_in,
    residual, updated,
    amps, coeffs, pao, doms, neighbours, counts, couplings, pno, occ, own, via, summed, arrived, acc,
    load_sem, own_sem, via_sem, raw_send, raw_recv, near_send, near_recv,
    summed_send, summed_recv, halo_send, halo_recv, dom_send, dom_recv, pass_send, pass_dom_send,
):
    n_pair, n_aux = lax.axis_size("pair"), lax.axis_size("aux")
    pair, aux = lax.axis_index("pair"), lax.axis_index("aux")
    pairs = amps.shape[0]
    half = pairs // 2
    depth = ints.shape[1]
    width = amps.shape[1]
    slots = neighbours.shape[0]
    chunks = half // CHUNK
    all_chunks = pairs // CHUNK

    up, down, far = (aux + 1) % n_aux, (aux + n_aux - 1) % n_aux, (aux + 2) % n_aux
    to_up, to_down = (pair, up), (pair, down)
    next_pair, last_pair = ((pair + 1) % n_pair, aux), ((pair + n_pair - 1) % n_pair, aux)
    first_end, last_end = aux == 0, aux == n_aux - 1
    at_end = jnp.logical_or(first_end, last_end)

    barrier = pltpu.get_barrier_semaphore()

    def greet(device):
        pl.semaphore_signal(barrier, inc=1, device_id=device, device_id_type=MESH)

    greet(to_up)
    greet(to_down)

    @pl.when(at_end)
    def _():
        greet(next_pair)
        greet(last_pair)

    def remote(src, dst, send, recv, device):
        return pltpu.make_async_remote_copy(
            src_ref=src, dst_ref=dst, send_sem=send, recv_sem=recv, device_id=device, device_id_type=MESH
        )

    def rows(first, count=CHUNK):
        return pl.ds(first, count)

    loads = [
        pltpu.make_async_copy(coeffs_in, coeffs, load_sem.at[0]),
        pltpu.make_async_copy(amps_in, amps, load_sem.at[1]),
        pltpu.make_async_copy(domains_in, doms.at[rows(pairs, pairs)], load_sem.at[2]),
    ]
    small_loads = [
        pltpu.make_async_copy(neighbours_in, neighbours, load_sem.at[3]),
        pltpu.make_async_copy(counts_in, counts, load_sem.at[4]),
        pltpu.make_async_copy(couplings_in, couplings, load_sem.at[5]),
        pltpu.make_async_copy(pno_in, pno, load_sem.at[6]),
        pltpu.make_async_copy(occ_in, occ, load_sem.at[7]),
    ]
    via_loads = [
        pltpu.make_async_copy(
            ints.at[rows(down * pairs, half)], via.at[0, :, pl.ds(0, depth)], via_sem.at[0]
        ),
        pltpu.make_async_copy(
            ints.at[rows(up * pairs + half, half)], via.at[1, :, pl.ds(0, depth)], via_sem.at[1]
        ),
    ]
    own_load = pltpu.make_async_copy(ints.at[rows(aux * pairs, pairs)], own.at[:, pl.ds(0, depth)], own_sem)
    for copy in loads + via_loads + [own_load] + small_loads:
        copy.start()

    pl.semaphore_wait(barrier, jnp.where(at_end, 4, 2))

    raw = []
    for c in range(chunks):
        for side, device in ((0, to_down), (1, to_up)):
            copy = remote(
                ints.at[rows(far * pairs + side * half + c * CHUNK)],
                via.at[side, rows(c * CHUNK), pl.ds(depth, depth)],
                raw_send.at[side, c],
                raw_recv.at[side, c],
                device,
            )
            copy.start()
            raw.append(copy)

    for copy in loads:
        copy.wait()

    targets = (
        (0, to_up, jnp.where(last_end, 3, 0)),
        (1, to_down, jnp.where(first_end, 3, 2)),
    )
    halo = []
    for side, device, part in targets:
        copy = remote(
            doms.at[rows(pairs, pairs)],
            doms.at[rows(part * pairs, pairs)],
            dom_send.at[side],
            dom_recv.at[part],
            device,
        )
        copy.start()
        halo.append(copy)
    for c in range(all_chunks):
        here = [c * CHUNK + i for i in range(CHUNK)]
        left_half = [contract(coeffs[p], amps[p], 1, 0).astype(BF16) for p in here]
        for p, block in zip(here, left_half):
            pao[pairs + p] = contract(block, coeffs[p], 1, 1).astype(BF16)
        for side, device, part in targets:
            copy = remote(
                pao.at[rows(pairs + c * CHUNK)],
                pao.at[rows(part * pairs + c * CHUNK)],
                halo_send.at[side, c],
                halo_recv.at[part, c],
                device,
            )
            copy.start()
            halo.append(copy)

    for copy in via_loads:
        copy.wait()
    sums = []
    for c in range(chunks):
        for side, device in ((0, to_down), (1, to_up)):
            raw[c * 2 + side].wait_recv()
            for p in range(c * CHUNK, c * CHUNK + CHUNK):
                block = via[side, p]
                summed[side, p] = contract(block[:, :width], block[:, width:], 0, 0).astype(BF16)
            copy = remote(
                summed.at[side, rows(c * CHUNK)],
                arrived.at[rows(side * half + c * CHUNK)],
                summed_send.at[side, c],
                summed_recv.at[side, c],
                device,
            )
            copy.start()
            sums.append(copy)

    def pass_on(device, part):
        passed = [
            remote(
                doms.at[rows(3 * pairs, pairs)],
                doms.at[rows(part * pairs, pairs)],
                pass_dom_send,
                dom_recv.at[part],
                device,
            )
        ]
        passed[0].start()
        for c in range(all_chunks):
            arrival(3, c).wait_recv()
            copy = remote(
                pao.at[rows(3 * pairs + c * CHUNK)],
                pao.at[rows(part * pairs + c * CHUNK)],
                pass_send.at[c],
                halo_recv.at[part, c],
                device,
            )
            copy.start()
            passed.append(copy)
        return passed

    def arrival(part, c):
        return remote(
            pao.at[rows(pairs + c * CHUNK)],
            pao.at[rows(part * pairs + c * CHUNK)],
            halo_send.at[0, c],
            halo_recv.at[part, c],
            to_up,
        )

    def domain_arrival(part):
        return remote(
            doms.at[rows(pairs, pairs)], doms.at[rows(part * pairs, pairs)], dom_send.at[0], dom_recv.at[part], to_up
        )

    @pl.when(first_end)
    def _():
        domain_arrival(3).wait_recv()
        pass_on(next_pair, 0)

    @pl.when(last_end)
    def _():
        domain_arrival(3).wait_recv()
        pass_on(last_pair, 2)

    for copy in halo[:-2]:
        copy.wait_send()

    near = []
    for c in range(chunks):
        for side, device, there in ((0, to_up, up), (1, to_down, down)):
            copy = remote(
                ints.at[rows(there * pairs + side * half + c * CHUNK)],
                own.at[rows(side * half + c * CHUNK), pl.ds(depth, depth)],
                near_send.at[side, c],
                near_recv.at[side, c],
                device,
            )
            copy.start()
            near.append(copy)

    halo[-2].wait_send()
    halo[-1].wait_send()
    for copy in small_loads:
        copy.wait()
    for part in (0, 2):
        domain_arrival(part).wait_recv()
        for c in range(all_chunks):
            arrival(part, c).wait_recv()

    first_row = ((pair * n_aux + aux) - 1) * pairs

    def couple(step, carry):
        here = [step * TOGETHER + i for i in range(TOGETHER)]
        totals = []
        for p in here:
            mine = jnp.broadcast_to(doms[pl.ds(pairs + p, 1), :], (width, width)).T
            matches, scaled = [], []
            for k in range(slots):
                row = jnp.clip(neighbours[k, p] - first_row, 0, 3 * pairs - 1)
                weight = jnp.where(k < counts[p], couplings[k, p], 0.0)
                match = jnp.where(mine == doms[pl.ds(row, 1), :], 1.0, 0.0).astype(BF16)
                picked = contract(match, pao[row], 1, 0)
                matches.append(match)
                scaled.append((weight * picked).astype(BF16))
            total = contract(jnp.concatenate(scaled, axis=1), jnp.concatenate(matches, axis=1), 1, 1)
            totals.append(total.astype(BF16))
        halves = [contract(total, coeffs[p], 1, 0).astype(BF16) for p, total in zip(here, totals)]
        for p, right_half in zip(here, halves):
            acc[p] = contract(coeffs[p], right_half, 0, 0)
        return carry

    lax.fori_loop(0, pairs // TOGETHER, couple, 0)

    own_load.wait()
    for c in range(chunks):
        for side in (0, 1):
            near[c * 2 + side].wait_recv()
            sums[c * 2 + side].wait_recv()
            first = side * half + c * CHUNK
            for p in range(first, first + CHUNK):
                block = own[p]
                exchange = contract(block[:, :width], block[:, width:], 0, 0) + arrived[p].astype(F32)
                energies = jnp.broadcast_to(pno[pl.ds(p, 1), :], (width, width))
                denominator = energies.T + energies + occ[p]
                wide = amps[p].astype(F32)
                result = exchange + denominator * wide + acc[p]
                residual[p] = result
                updated[p] = (wide - result / denominator).astype(BF16)

    for copy in raw + near + sums:
        copy.wait_send()

    @pl.when(at_end)
    def _():
        domain_pass = remote(
            doms.at[rows(3 * pairs, pairs)], doms.at[rows(0, pairs)], pass_dom_send, dom_recv.at[0], next_pair
        )
        domain_pass.wait_send()
        for c in range(all_chunks):
            remote(
                pao.at[rows(3 * pairs + c * CHUNK)],
                pao.at[rows(c * CHUNK)],
                pass_send.at[c],
                halo_recv.at[0, c],
                next_pair,
            ).wait_send()


def per_device(
    integrals,
    amplitudes,
    coeffs,
    domains,
    neighbours,
    counts,
    couplings,
    pno_energies,
    occ_energies,
):
    pairs, width, _ = amplitudes.shape
    depth = integrals.shape[1]
    half = pairs // 2
    chunks = half // CHUNK
    in_hbm = pl.BlockSpec(memory_space=pltpu.HBM)
    in_vmem = pl.BlockSpec(memory_space=pltpu.VMEM)
    dma = pltpu.SemaphoreType.DMA
    operands = (
        integrals, amplitudes, coeffs, domains, neighbours.T, counts, couplings.T, pno_energies, occ_energies,
    )
    residual, updated = pl.pallas_call(
        kernel,
        out_shape=(
            pltpu.VMEM((pairs, width, width), F32),
            pltpu.VMEM((pairs, width, width), BF16),
        ),
        in_specs=[in_hbm] * len(operands),
        out_specs=(in_vmem, in_vmem),
        scratch_shapes=[
            pltpu.VMEM((pairs, width, width), BF16),
            pltpu.VMEM((pairs, width, width), BF16),
            pltpu.VMEM((4 * pairs, width, width), BF16),
            pltpu.VMEM((4 * pairs, width), jnp.int32),
            pltpu.SMEM(neighbours.shape[::-1], jnp.int32),
            pltpu.SMEM(counts.shape, jnp.int32),
            pltpu.SMEM(couplings.shape[::-1], F32),
            pltpu.VMEM(pno_energies.shape, F32),
            pltpu.SMEM(occ_energies.shape, F32),
            pltpu.VMEM((pairs, 2 * depth, 2 * width), BF16),
            pltpu.VMEM((2, half, 2 * depth, 2 * width), BF16),
            pltpu.VMEM((2, half, width, width), BF16),
            pltpu.VMEM((pairs, width, width), BF16),
            pltpu.VMEM((pairs, width, width), F32),
            dma((8,)),
            dma(()),
            dma((2,)),
            dma((2, chunks)),
            dma((2, chunks)),
            dma((2, chunks)),
            dma((2, chunks)),
            dma((2, chunks)),
            dma((2, chunks)),
            dma((2, 2 * chunks)),
            dma((4, 2 * chunks)),
            dma((2,)),
            dma((4,)),
            dma((2 * chunks,)),
            dma(()),
        ],
        compiler_params=pltpu.CompilerParams(
            collective_id=0, has_side_effects=True, vmem_limit_bytes=32 * 1024 * 1024
        ),
        name="doubles_residual",
    )(*(pltpu.with_memory_space_constraint(operand, pltpu.HBM) for operand in operands))
    return (residual, updated)


def solution(mesh):
    in_specs = (
        P("pair", "aux", None),
        P(("pair", "aux"), None, None),
        P(("pair", "aux"), None, None),
        P(("pair", "aux"), None),
        P(("pair", "aux"), None),
        P(("pair", "aux")),
        P(("pair", "aux"), None),
        P(("pair", "aux"), None),
        P(("pair", "aux")),
    )
    out_specs = (P(("pair", "aux"), None, None), P(("pair", "aux"), None, None))
    return jax.shard_map(
        per_device, mesh=mesh, in_specs=in_specs, out_specs=out_specs, check_vma=False
    )
```

```python
import jax
import jax.numpy as jnp
from jax import lax
from jax.experimental import pallas as pl
from jax.experimental.pallas import tpu as pltpu
from jax.sharding import PartitionSpec as P

MESH = pl.DeviceIdType.MESH
F32 = jnp.float32
BF16 = jnp.bfloat16
CHUNK = 4
TOGETHER = 4


def contract(a, b, dim_a, dim_b):
    return lax.dot_general(a, b, (((dim_a,), (dim_b,)), ((), ())), preferred_element_type=F32)


def kernel(
    ints, amps_in, coeffs_in, domains_in, neighbours_in, counts_in, couplings_in, pno_in, occ_in,
    residual, updated,
    amps, coeffs, pao, doms, neighbours, counts, couplings, pno, occ, own, via, summed, arrived,
    acc, inverse, mine, flipped,
    amps_sem, coeffs_sem, load_sem, own_sem, via_sem, raw_send, raw_recv, near_send, near_recv,
    summed_send, summed_recv, halo_send, halo_recv, dom_send, dom_recv, pass_send, pass_dom_send, ready,
):
    n_pair, n_aux = lax.axis_size("pair"), lax.axis_size("aux")
    pair, aux = lax.axis_index("pair"), lax.axis_index("aux")
    pairs = amps.shape[0]
    half = pairs // 2
    depth = ints.shape[1]
    width = amps.shape[1]
    slots = neighbours.shape[0]
    chunks = half // CHUNK
    all_chunks = pairs // CHUNK

    up, down, far = (aux + 1) % n_aux, (aux + n_aux - 1) % n_aux, (aux + 2) % n_aux
    to_up, to_down = (pair, up), (pair, down)
    next_pair, last_pair = ((pair + 1) % n_pair, aux), ((pair + n_pair - 1) % n_pair, aux)
    first_end, last_end = aux == 0, aux == n_aux - 1
    at_end = jnp.logical_or(first_end, last_end)
    no_left = jnp.logical_and(first_end, pair == 0)
    no_right = jnp.logical_and(last_end, pair == n_pair - 1)
    passes = jnp.logical_or(
        jnp.logical_and(first_end, pair < n_pair - 1), jnp.logical_and(last_end, pair > 0)
    )

    barrier = pltpu.get_barrier_semaphore()

    def greet(semaphore, device):
        pl.semaphore_signal(semaphore, inc=1, device_id=device, device_id_type=MESH)

    greet(barrier, to_up)
    greet(barrier, to_down)

    @pl.when(at_end)
    def _():
        greet(barrier, last_pair)

    def remote(src, dst, send, recv, device):
        return pltpu.make_async_remote_copy(
            src_ref=src, dst_ref=dst, send_sem=send, recv_sem=recv, device_id=device, device_id_type=MESH
        )

    def rows(first, count=CHUNK):
        return pl.ds(first, count)

    matrix_loads = []
    for c in range(all_chunks):
        part = rows(c * CHUNK)
        matrix_loads.append(
            [
                pltpu.make_async_copy(coeffs_in.at[part], coeffs.at[part], coeffs_sem.at[c]),
                pltpu.make_async_copy(amps_in.at[part], amps.at[part], amps_sem.at[c]),
            ]
        )
    domain_load = pltpu.make_async_copy(domains_in, doms.at[rows(pairs, pairs)], load_sem.at[0])
    small_loads = [
        pltpu.make_async_copy(neighbours_in, neighbours, load_sem.at[1]),
        pltpu.make_async_copy(counts_in, counts, load_sem.at[2]),
        pltpu.make_async_copy(couplings_in, couplings, load_sem.at[3]),
        pltpu.make_async_copy(pno_in, pno, load_sem.at[4]),
        pltpu.make_async_copy(occ_in, occ, load_sem.at[5]),
    ]
    via_loads = [
        pltpu.make_async_copy(
            ints.at[rows(down * pairs, half)], via.at[0, :, pl.ds(0, depth)], via_sem.at[0]
        ),
        pltpu.make_async_copy(
            ints.at[rows(up * pairs + half, half)], via.at[1, :, pl.ds(0, depth)], via_sem.at[1]
        ),
    ]
    own_load = pltpu.make_async_copy(ints.at[rows(aux * pairs, pairs)], own.at[:, pl.ds(0, depth)], own_sem)
    for copy in sum(matrix_loads, []) + [domain_load] + small_loads + [own_load] + via_loads:
        copy.start()

    def to_pao(c):
        for copy in matrix_loads[c]:
            copy.wait()
        here = [c * CHUNK + i for i in range(CHUNK)]
        left_half = [contract(coeffs[p], amps[p], 1, 0).astype(BF16) for p in here]
        for p, block in zip(here, left_half):
            pao[pairs + p] = contract(block, coeffs[p], 1, 1).astype(BF16)

    early = all_chunks // 2
    for c in range(early):
        to_pao(c)
    domain_load.wait()

    pl.semaphore_wait(barrier, jnp.where(at_end, 3, 2))

    @pl.when(jnp.logical_and(last_end, pair < n_pair - 1))
    def _():
        greet(ready, next_pair)

    targets = (
        (0, to_up, jnp.where(last_end, 3, 0)),
        (1, to_down, jnp.where(first_end, 3, 2)),
    )
    domain_halo = [
        remote(
            doms.at[rows(pairs, pairs)],
            doms.at[rows(part * pairs, pairs)],
            dom_send.at[side],
            dom_recv.at[part],
            device,
        )
        for side, device, part in targets
    ]
    for copy in domain_halo:
        copy.start()
    halo = []
    for c in range(all_chunks):
        if c >= early:
            to_pao(c)
        halo.append(
            [
                remote(
                    pao.at[rows(pairs + c * CHUNK)],
                    pao.at[rows(part * pairs + c * CHUNK)],
                    halo_send.at[side, c],
                    halo_recv.at[part, c],
                    device,
                )
                for side, device, part in targets
            ]
        )
        for copy in halo[c]:
            copy.start()

    def arrival(part, c):
        return remote(
            pao.at[rows(pairs + c * CHUNK)],
            pao.at[rows(part * pairs + c * CHUNK)],
            halo_send.at[0, c],
            halo_recv.at[part, c],
            to_up,
        )

    def domain_arrival(part):
        return remote(
            doms.at[rows(pairs, pairs)], doms.at[rows(part * pairs, pairs)], dom_send.at[0], dom_recv.at[part], to_up
        )

    pass_to = (jnp.where(first_end, next_pair[0], last_pair[0]), aux)
    pass_part = jnp.where(first_end, 0, 2)
    domain_pass = remote(
        doms.at[rows(3 * pairs, pairs)],
        doms.at[rows(pass_part * pairs, pairs)],
        pass_dom_send,
        dom_recv.at[pass_part],
        pass_to,
    )
    passed = [
        remote(
            pao.at[rows(3 * pairs + c * CHUNK)],
            pao.at[rows(pass_part * pairs + c * CHUNK)],
            pass_send.at[c],
            halo_recv.at[pass_part, c],
            pass_to,
        )
        for c in range(all_chunks)
    ]

    def halo_sent(c):
        for copy in halo[c]:
            copy.wait_send()

        @pl.when(at_end)
        def _():
            if c == 0:
                domain_arrival(3).wait_recv()
            arrival(3, c).wait_recv()

        if c == 0:

            @pl.when(jnp.logical_and(last_end, pair > 0))
            def _():
                pl.semaphore_wait(ready, 1)

        @pl.when(passes)
        def _():
            if c == 0:
                domain_pass.start()
            passed[c].start()

    def prepare(first, count):
        for p in range(first, first + count):
            energies = jnp.broadcast_to(pno[pl.ds(p, 1), :], (width, width))
            denominator = energies.T + energies + occ[p]
            inverse[p] = 1.0 / denominator
            block = own[p, pl.ds(0, depth), :]
            exchange = contract(block[:, :width], block[:, width:], 0, 0)
            acc[p] = exchange + denominator * amps[p].astype(F32)
            mine[p] = jnp.broadcast_to(doms[pl.ds(pairs + p, 1), :], (width, width)).T
            flipped[p] = coeffs[p].T

    for copy in small_loads:
        copy.wait()
    own_load.wait()
    prepare(0, half)
    for c in range(early):
        halo_sent(c)

    raw = []
    for c in range(chunks):
        for side, device in ((0, to_down), (1, to_up)):
            copy = remote(
                ints.at[rows(far * pairs + side * half + c * CHUNK)],
                via.at[side, rows(c * CHUNK), pl.ds(depth, depth)],
                raw_send.at[side, c],
                raw_recv.at[side, c],
                device,
            )
            copy.start()
            raw.append(copy)

    prepare(half, pairs - half)
    for c in range(early, all_chunks):
        halo_sent(c)

    for copy in via_loads:
        copy.wait()
    near, sums = [], []
    for c in range(chunks):
        for side, device, there in ((0, to_up, up), (1, to_down, down)):
            copy = remote(
                ints.at[rows(there * pairs + side * half + c * CHUNK)],
                own.at[rows(side * half + c * CHUNK), pl.ds(depth, depth)],
                near_send.at[side, c],
                near_recv.at[side, c],
                device,
            )
            copy.start()
            near.append(copy)
        for side, device in ((0, to_down), (1, to_up)):
            raw[c * 2 + side].wait_recv()
            for p in range(c * CHUNK, c * CHUNK + CHUNK):
                block = via[side, p]
                summed[side, p] = contract(block[:, :width], block[:, width:], 0, 0).astype(BF16)
            copy = remote(
                summed.at[side, rows(c * CHUNK)],
                arrived.at[rows(side * half + c * CHUNK)],
                summed_send.at[side, c],
                summed_recv.at[side, c],
                device,
            )
            copy.start()
            sums.append(copy)

    for part, none in ((0, no_left), (2, no_right)):

        @pl.when(jnp.logical_not(none))
        def _():
            domain_arrival(part).wait_recv()
            for c in range(all_chunks):
                arrival(part, c).wait_recv()

        @pl.when(none)
        def _():
            doms[pl.ds(part * pairs, pairs), :] = jnp.full((pairs, width), -1, jnp.int32)
            pao[pl.ds(part * pairs, pairs)] = jnp.zeros((pairs, width, width), BF16)

    first_row = ((pair * n_aux + aux) - 1) * pairs

    def couple(step, carry):
        here = [step * TOGETHER + i for i in range(TOGETHER)]
        totals = []
        for p in here:
            column = mine[p]
            matches, scaled = [], []
            for k in range(slots):
                row = jnp.clip(neighbours[k, p] - first_row, 0, 3 * pairs - 1)
                weight = jnp.where(k < counts[p], couplings[k, p], 0.0)
                match = jnp.where(column == doms[pl.ds(row, 1), :], 1.0, 0.0).astype(BF16)
                picked = contract(match, pao[row], 1, 0)
                matches.append(match)
                scaled.append((weight * picked).astype(BF16))
            total = contract(jnp.concatenate(scaled, axis=1), jnp.concatenate(matches, axis=1), 1, 1)
            totals.append(total.astype(BF16))
        halves = [contract(total, coeffs[p], 1, 0).astype(BF16) for p, total in zip(here, totals)]
        for p, right_half in zip(here, halves):
            acc[p] += contract(flipped[p], right_half, 1, 0)
        return carry

    lax.fori_loop(0, pairs // TOGETHER, couple, 0)

    for c in range(chunks):
        for side in (0, 1):
            near[c * 2 + side].wait_recv()
            sums[c * 2 + side].wait_recv()
            first = side * half + c * CHUNK
            for p in range(first, first + CHUNK):
                block = own[p, pl.ds(depth, depth), :]
                exchange = contract(block[:, :width], block[:, width:], 0, 0) + arrived[p].astype(F32)
                result = acc[p] + exchange
                residual[p] = result
                updated[p] = (amps[p].astype(F32) - result * inverse[p]).astype(BF16)

    for copy in raw + near + sums + domain_halo:
        copy.wait_send()

    @pl.when(passes)
    def _():
        for copy in [domain_pass] + passed:
            copy.wait_send()


def per_device(
    integrals,
    amplitudes,
    coeffs,
    domains,
    neighbours,
    counts,
    couplings,
    pno_energies,
    occ_energies,
):
    pairs, width, _ = amplitudes.shape
    depth = integrals.shape[1]
    half = pairs // 2
    chunks = half // CHUNK
    in_hbm = pl.BlockSpec(memory_space=pltpu.HBM)
    in_vmem = pl.BlockSpec(memory_space=pltpu.VMEM)
    dma = pltpu.SemaphoreType.DMA
    operands = (
        integrals, amplitudes, coeffs, domains, neighbours.T, counts, couplings.T, pno_energies, occ_energies,
    )
    residual, updated = pl.pallas_call(
        kernel,
        out_shape=(
            pltpu.VMEM((pairs, width, width), F32),
            pltpu.VMEM((pairs, width, width), BF16),
        ),
        in_specs=[in_hbm] * len(operands),
        out_specs=(in_vmem, in_vmem),
        scratch_shapes=[
            pltpu.VMEM((pairs, width, width), BF16),
            pltpu.VMEM((pairs, width, width), BF16),
            pltpu.VMEM((4 * pairs, width, width), BF16),
            pltpu.VMEM((4 * pairs, width), jnp.int32),
            pltpu.SMEM(neighbours.shape[::-1], jnp.int32),
            pltpu.SMEM(counts.shape, jnp.int32),
            pltpu.SMEM(couplings.shape[::-1], F32),
            pltpu.VMEM(pno_energies.shape, F32),
            pltpu.SMEM(occ_energies.shape, F32),
            pltpu.VMEM((pairs, 2 * depth, 2 * width), BF16),
            pltpu.VMEM((2, half, 2 * depth, 2 * width), BF16),
            pltpu.VMEM((2, half, width, width), BF16),
            pltpu.VMEM((pairs, width, width), BF16),
            pltpu.VMEM((pairs, width, width), F32),
            pltpu.VMEM((pairs, width, width), F32),
            pltpu.VMEM((pairs, width, width), jnp.int32),
            pltpu.VMEM((pairs, width, width), BF16),
            dma((2 * chunks,)),
            dma((2 * chunks,)),
            dma((6,)),
            dma(()),
            dma((2,)),
            dma((2, chunks)),
            dma((2, chunks)),
            dma((2, chunks)),
            dma((2, chunks)),
            dma((2, chunks)),
            dma((2, chunks)),
            dma((2, 2 * chunks)),
            dma((4, 2 * chunks)),
            dma((2,)),
            dma((4,)),
            dma((2 * chunks,)),
            dma(()),
            pltpu.SemaphoreType.REGULAR,
        ],
        compiler_params=pltpu.CompilerParams(
            collective_id=0, has_side_effects=True, vmem_limit_bytes=32 * 1024 * 1024
        ),
        name="doubles_residual",
    )(*(pltpu.with_memory_space_constraint(operand, pltpu.HBM) for operand in operands))
    return (residual, updated)


def solution(mesh):
    in_specs = (
        P("pair", "aux", None),
        P(("pair", "aux"), None, None),
        P(("pair", "aux"), None, None),
        P(("pair", "aux"), None),
        P(("pair", "aux"), None),
        P(("pair", "aux")),
        P(("pair", "aux"), None),
        P(("pair", "aux"), None),
        P(("pair", "aux")),
    )
    out_specs = (P(("pair", "aux"), None, None), P(("pair", "aux"), None, None))
    return jax.shard_map(
        per_device, mesh=mesh, in_specs=in_specs, out_specs=out_specs, check_vma=False
    )
```

```python
import jax
import jax.numpy as jnp
from jax import lax
from jax.experimental import pallas as pl
from jax.experimental.pallas import tpu as pltpu
from jax.sharding import PartitionSpec as P

MESH = pl.DeviceIdType.MESH
F32 = jnp.float32
BF16 = jnp.bfloat16
CHUNK = 4
TOGETHER = 4


def contract(a, b, dim_a, dim_b):
    return lax.dot_general(a, b, (((dim_a,), (dim_b,)), ((), ())), preferred_element_type=F32)


def kernel(
    ints, amps_in, coeffs_in, domains_in, neighbours_in, counts_in, couplings_in, pno_in, occ_in,
    residual, updated,
    amps, coeffs, pao, doms, neighbours, counts, couplings, pno, occ, own, via, summed, arrived,
    acc, inverse, mine, flipped,
    amps_sem, coeffs_sem, load_sem, own_sem, via_sem, raw_send, raw_recv, near_send, near_recv,
    summed_send, summed_recv, halo_send, halo_recv, dom_send, dom_recv, pass_send, pass_dom_send, ready,
):
    n_pair, n_aux = lax.axis_size("pair"), lax.axis_size("aux")
    pair, aux = lax.axis_index("pair"), lax.axis_index("aux")
    pairs = amps.shape[0]
    half = pairs // 2
    depth = ints.shape[1]
    width = amps.shape[1]
    slots = neighbours.shape[0]
    chunks = half // CHUNK
    all_chunks = pairs // CHUNK

    up, down, far = (aux + 1) % n_aux, (aux + n_aux - 1) % n_aux, (aux + 2) % n_aux
    to_up, to_down = (pair, up), (pair, down)
    next_pair, last_pair = ((pair + 1) % n_pair, aux), ((pair + n_pair - 1) % n_pair, aux)
    first_end, last_end = aux == 0, aux == n_aux - 1
    at_end = jnp.logical_or(first_end, last_end)
    no_left = jnp.logical_and(first_end, pair == 0)
    no_right = jnp.logical_and(last_end, pair == n_pair - 1)
    passes = jnp.logical_or(
        jnp.logical_and(first_end, pair < n_pair - 1), jnp.logical_and(last_end, pair > 0)
    )

    barrier = pltpu.get_barrier_semaphore()

    def greet(semaphore, device):
        pl.semaphore_signal(semaphore, inc=1, device_id=device, device_id_type=MESH)

    greet(barrier, to_up)
    greet(barrier, to_down)

    @pl.when(at_end)
    def _():
        greet(barrier, last_pair)

    def remote(src, dst, send, recv, device):
        return pltpu.make_async_remote_copy(
            src_ref=src, dst_ref=dst, send_sem=send, recv_sem=recv, device_id=device, device_id_type=MESH
        )

    def rows(first, count=CHUNK):
        return pl.ds(first, count)

    matrix_loads = []
    for c in range(all_chunks):
        part = rows(c * CHUNK)
        matrix_loads.append(
            [
                pltpu.make_async_copy(coeffs_in.at[part], coeffs.at[part], coeffs_sem.at[c]),
                pltpu.make_async_copy(amps_in.at[part], amps.at[part], amps_sem.at[c]),
            ]
        )
    domain_load = pltpu.make_async_copy(domains_in, doms.at[rows(pairs, pairs)], load_sem.at[0])
    small_loads = [
        pltpu.make_async_copy(neighbours_in, neighbours, load_sem.at[1]),
        pltpu.make_async_copy(counts_in, counts, load_sem.at[2]),
        pltpu.make_async_copy(couplings_in, couplings, load_sem.at[3]),
        pltpu.make_async_copy(pno_in, pno, load_sem.at[4]),
        pltpu.make_async_copy(occ_in, occ, load_sem.at[5]),
    ]
    via_loads = [
        pltpu.make_async_copy(
            ints.at[rows(down * pairs, half)], via.at[0, :, pl.ds(0, depth)], via_sem.at[0]
        ),
        pltpu.make_async_copy(
            ints.at[rows(up * pairs + half, half)], via.at[1, :, pl.ds(0, depth)], via_sem.at[1]
        ),
    ]
    own_load = pltpu.make_async_copy(ints.at[rows(aux * pairs, pairs)], own.at[:, pl.ds(0, depth)], own_sem)
    for copy in sum(matrix_loads, []) + [domain_load] + small_loads + [own_load] + via_loads:
        copy.start()

    def to_pao(c):
        for copy in matrix_loads[c]:
            copy.wait()
        here = [c * CHUNK + i for i in range(CHUNK)]
        left_half = [contract(coeffs[p], amps[p], 1, 0).astype(BF16) for p in here]
        for p, block in zip(here, left_half):
            pao[pairs + p] = contract(block, coeffs[p], 1, 1).astype(BF16)

    early = all_chunks // 2
    for c in range(early):
        to_pao(c)
    domain_load.wait()

    pl.semaphore_wait(barrier, jnp.where(at_end, 3, 2))

    @pl.when(jnp.logical_and(last_end, pair < n_pair - 1))
    def _():
        greet(ready, next_pair)

    targets = (
        (0, to_up, jnp.where(last_end, 3, 0)),
        (1, to_down, jnp.where(first_end, 3, 2)),
    )
    domain_halo = [
        remote(
            doms.at[rows(pairs, pairs)],
            doms.at[rows(part * pairs, pairs)],
            dom_send.at[side],
            dom_recv.at[part],
            device,
        )
        for side, device, part in targets
    ]
    for copy in domain_halo:
        copy.start()
    halo = [
        [
            remote(
                pao.at[rows(pairs + c * CHUNK)],
                pao.at[rows(part * pairs + c * CHUNK)],
                halo_send.at[side, c],
                halo_recv.at[part, c],
                device,
            )
            for side, device, part in targets
        ]
        for c in range(all_chunks)
    ]

    def send_halo(c):
        for copy in halo[c]:
            copy.start()

    for c in range(early):
        send_halo(c)
    for c in range(early, all_chunks):
        to_pao(c)

    def arrival(part, c):
        return remote(
            pao.at[rows(pairs + c * CHUNK)],
            pao.at[rows(part * pairs + c * CHUNK)],
            halo_send.at[0, c],
            halo_recv.at[part, c],
            to_up,
        )

    def domain_arrival(part):
        return remote(
            doms.at[rows(pairs, pairs)], doms.at[rows(part * pairs, pairs)], dom_send.at[0], dom_recv.at[part], to_up
        )

    pass_to = (jnp.where(first_end, next_pair[0], last_pair[0]), aux)
    pass_part = jnp.where(first_end, 0, 2)
    domain_pass = remote(
        doms.at[rows(3 * pairs, pairs)],
        doms.at[rows(pass_part * pairs, pairs)],
        pass_dom_send,
        dom_recv.at[pass_part],
        pass_to,
    )
    passed = [
        remote(
            pao.at[rows(3 * pairs + c * CHUNK)],
            pao.at[rows(pass_part * pairs + c * CHUNK)],
            pass_send.at[c],
            halo_recv.at[pass_part, c],
            pass_to,
        )
        for c in range(all_chunks)
    ]

    def halo_sent(c):
        for copy in halo[c]:
            copy.wait_send()

        @pl.when(at_end)
        def _():
            if c == 0:
                domain_arrival(3).wait_recv()
            arrival(3, c).wait_recv()

        if c == 0:

            @pl.when(jnp.logical_and(last_end, pair > 0))
            def _():
                pl.semaphore_wait(ready, 1)

        @pl.when(passes)
        def _():
            if c == 0:
                domain_pass.start()
            passed[c].start()

    def prepare(first, count):
        for p in range(first, first + count):
            energies = jnp.broadcast_to(pno[pl.ds(p, 1), :], (width, width))
            denominator = energies.T + energies + occ[p]
            inverse[p] = 1.0 / denominator
            block = own[p, pl.ds(0, depth), :]
            exchange = contract(block[:, :width], block[:, width:], 0, 0)
            acc[p] = exchange + denominator * amps[p].astype(F32)
            mine[p] = jnp.broadcast_to(doms[pl.ds(pairs + p, 1), :], (width, width)).T
            flipped[p] = coeffs[p].T

    raw = [
        remote(
            ints.at[rows(far * pairs + side * half + c * CHUNK)],
            via.at[side, rows(c * CHUNK), pl.ds(depth, depth)],
            raw_send.at[side, c],
            raw_recv.at[side, c],
            device,
        )
        for c in range(chunks)
        for side, device in ((0, to_down), (1, to_up))
    ]
    near = [
        remote(
            ints.at[rows(there * pairs + side * half + c * CHUNK)],
            own.at[rows(side * half + c * CHUNK), pl.ds(depth, depth)],
            near_send.at[side, c],
            near_recv.at[side, c],
            device,
        )
        for c in range(chunks)
        for side, device, there in ((0, to_up, up), (1, to_down, down))
    ]
    sums = [
        remote(
            summed.at[side, rows(c * CHUNK)],
            arrived.at[rows(side * half + c * CHUNK)],
            summed_send.at[side, c],
            summed_recv.at[side, c],
            device,
        )
        for c in range(chunks)
        for side, device in ((0, to_down), (1, to_up))
    ]

    for copy in small_loads:
        copy.wait()
    own_load.wait()
    for c in range(all_chunks):
        prepare(c * CHUNK, CHUNK)
        halo_sent(c)
        if c + early < all_chunks:
            send_halo(c + early)
        if c == all_chunks - 2:
            for copy in raw:
                copy.start()

    for part, none in ((0, no_left), (2, no_right)):

        @pl.when(jnp.logical_not(none))
        def _():
            domain_arrival(part).wait_recv()
            for c in range(all_chunks):
                arrival(part, c).wait_recv()

        @pl.when(none)
        def _():
            doms[pl.ds(part * pairs, pairs), :] = jnp.full((pairs, width), -1, jnp.int32)
            pao[pl.ds(part * pairs, pairs)] = jnp.zeros((pairs, width, width), BF16)

    first_row = ((pair * n_aux + aux) - 1) * pairs

    def couple(step, carry):
        here = [step * TOGETHER + i for i in range(TOGETHER)]
        totals = []
        for p in here:
            column = mine[p]
            matches, scaled = [], []
            for k in range(slots):
                row = jnp.clip(neighbours[k, p] - first_row, 0, 3 * pairs - 1)
                weight = jnp.where(k < counts[p], couplings[k, p], 0.0)
                match = jnp.where(column == doms[pl.ds(row, 1), :], 1.0, 0.0).astype(BF16)
                picked = contract(match, pao[row], 1, 0)
                matches.append(match)
                scaled.append((weight * picked).astype(BF16))
            total = contract(jnp.concatenate(scaled, axis=1), jnp.concatenate(matches, axis=1), 1, 1)
            totals.append(total.astype(BF16))
        halves = [contract(total, coeffs[p], 1, 0).astype(BF16) for p, total in zip(here, totals)]
        for p, right_half in zip(here, halves):
            acc[p] += contract(flipped[p], right_half, 1, 0)
        return carry

    steps = pairs // TOGETHER
    lax.fori_loop(0, steps // 4, couple, 0)
    for copy in raw[:2]:
        copy.wait_send()
    for copy in near:
        copy.start()
    lax.fori_loop(steps // 4, steps // 2, couple, 0)

    for copy in via_loads:
        copy.wait()
    for c in range(chunks):
        for side in (0, 1):
            raw[c * 2 + side].wait_recv()
            for p in range(c * CHUNK, c * CHUNK + CHUNK):
                block = via[side, p]
                summed[side, p] = contract(block[:, :width], block[:, width:], 0, 0).astype(BF16)
            sums[c * 2 + side].start()

    lax.fori_loop(steps // 2, steps, couple, 0)

    for c in range(chunks):
        for side in (0, 1):
            near[c * 2 + side].wait_recv()
            sums[c * 2 + side].wait_recv()
            first = side * half + c * CHUNK
            for p in range(first, first + CHUNK):
                block = own[p, pl.ds(depth, depth), :]
                exchange = contract(block[:, :width], block[:, width:], 0, 0) + arrived[p].astype(F32)
                result = acc[p] + exchange
                residual[p] = result
                updated[p] = (amps[p].astype(F32) - result * inverse[p]).astype(BF16)

    for copy in raw[2:] + near + sums + domain_halo:
        copy.wait_send()

    @pl.when(passes)
    def _():
        for copy in [domain_pass] + passed:
            copy.wait_send()


def per_device(
    integrals,
    amplitudes,
    coeffs,
    domains,
    neighbours,
    counts,
    couplings,
    pno_energies,
    occ_energies,
):
    pairs, width, _ = amplitudes.shape
    depth = integrals.shape[1]
    half = pairs // 2
    chunks = half // CHUNK
    in_hbm = pl.BlockSpec(memory_space=pltpu.HBM)
    in_vmem = pl.BlockSpec(memory_space=pltpu.VMEM)
    dma = pltpu.SemaphoreType.DMA
    operands = (
        integrals, amplitudes, coeffs, domains, neighbours.T, counts, couplings.T, pno_energies, occ_energies,
    )
    residual, updated = pl.pallas_call(
        kernel,
        out_shape=(
            pltpu.VMEM((pairs, width, width), F32),
            pltpu.VMEM((pairs, width, width), BF16),
        ),
        in_specs=[in_hbm] * len(operands),
        out_specs=(in_vmem, in_vmem),
        scratch_shapes=[
            pltpu.VMEM((pairs, width, width), BF16),
            pltpu.VMEM((pairs, width, width), BF16),
            pltpu.VMEM((4 * pairs, width, width), BF16),
            pltpu.VMEM((4 * pairs, width), jnp.int32),
            pltpu.SMEM(neighbours.shape[::-1], jnp.int32),
            pltpu.SMEM(counts.shape, jnp.int32),
            pltpu.SMEM(couplings.shape[::-1], F32),
            pltpu.VMEM(pno_energies.shape, F32),
            pltpu.SMEM(occ_energies.shape, F32),
            pltpu.VMEM((pairs, 2 * depth, 2 * width), BF16),
            pltpu.VMEM((2, half, 2 * depth, 2 * width), BF16),
            pltpu.VMEM((2, half, width, width), BF16),
            pltpu.VMEM((pairs, width, width), BF16),
            pltpu.VMEM((pairs, width, width), F32),
            pltpu.VMEM((pairs, width, width), F32),
            pltpu.VMEM((pairs, width, width), jnp.int32),
            pltpu.VMEM((pairs, width, width), BF16),
            dma((2 * chunks,)),
            dma((2 * chunks,)),
            dma((6,)),
            dma(()),
            dma((2,)),
            dma((2, chunks)),
            dma((2, chunks)),
            dma((2, chunks)),
            dma((2, chunks)),
            dma((2, chunks)),
            dma((2, chunks)),
            dma((2, 2 * chunks)),
            dma((4, 2 * chunks)),
            dma((2,)),
            dma((4,)),
            dma((2 * chunks,)),
            dma(()),
            pltpu.SemaphoreType.REGULAR,
        ],
        compiler_params=pltpu.CompilerParams(
            collective_id=0, has_side_effects=True, vmem_limit_bytes=32 * 1024 * 1024
        ),
        name="doubles_residual",
    )(*(pltpu.with_memory_space_constraint(operand, pltpu.HBM) for operand in operands))
    return (residual, updated)


def solution(mesh):
    in_specs = (
        P("pair", "aux", None),
        P(("pair", "aux"), None, None),
        P(("pair", "aux"), None, None),
        P(("pair", "aux"), None),
        P(("pair", "aux"), None),
        P(("pair", "aux")),
        P(("pair", "aux"), None),
        P(("pair", "aux"), None),
        P(("pair", "aux")),
    )
    out_specs = (P(("pair", "aux"), None, None), P(("pair", "aux"), None, None))
    return jax.shard_map(
        per_device, mesh=mesh, in_specs=in_specs, out_specs=out_specs, check_vma=False
    )
```

```python
import jax
import jax.numpy as jnp
from jax import lax
from jax.experimental import pallas as pl
from jax.experimental.pallas import tpu as pltpu
from jax.sharding import PartitionSpec as P

MESH = pl.DeviceIdType.MESH
F32 = jnp.float32
BF16 = jnp.bfloat16
CHUNK = 4
TOGETHER = 4


def contract(a, b, dim_a, dim_b):
    return lax.dot_general(a, b, (((dim_a,), (dim_b,)), ((), ())), preferred_element_type=F32)


def kernel(
    ints, amps_in, coeffs_in, domains_in, neighbours_in, counts_in, couplings_in, pno_in, occ_in,
    residual, updated,
    amps, coeffs, pao, doms, neighbours, counts, couplings, pno, occ, own, via, summed, arrived,
    acc, inverse, mine, flipped,
    amps_sem, coeffs_sem, load_sem, own_sem, via_sem, raw_send, raw_recv, near_send, near_recv,
    summed_send, summed_recv, halo_send, halo_recv, dom_send, dom_recv, pass_send, pass_dom_send, ready,
):
    n_pair, n_aux = lax.axis_size("pair"), lax.axis_size("aux")
    pair, aux = lax.axis_index("pair"), lax.axis_index("aux")
    pairs = amps.shape[0]
    half = pairs // 2
    depth = ints.shape[1]
    width = amps.shape[1]
    slots = neighbours.shape[0]
    chunks = half // CHUNK
    all_chunks = pairs // CHUNK

    up, down, far = (aux + 1) % n_aux, (aux + n_aux - 1) % n_aux, (aux + 2) % n_aux
    to_up, to_down = (pair, up), (pair, down)
    next_pair, last_pair = ((pair + 1) % n_pair, aux), ((pair + n_pair - 1) % n_pair, aux)
    first_end, last_end = aux == 0, aux == n_aux - 1
    at_end = jnp.logical_or(first_end, last_end)
    no_left = jnp.logical_and(first_end, pair == 0)
    no_right = jnp.logical_and(last_end, pair == n_pair - 1)
    passes = jnp.logical_or(
        jnp.logical_and(first_end, pair < n_pair - 1), jnp.logical_and(last_end, pair > 0)
    )

    barrier = pltpu.get_barrier_semaphore()

    def greet(semaphore, device):
        pl.semaphore_signal(semaphore, inc=1, device_id=device, device_id_type=MESH)

    greet(barrier, to_up)
    greet(barrier, to_down)

    @pl.when(at_end)
    def _():
        greet(barrier, last_pair)

    def remote(src, dst, send, recv, device):
        return pltpu.make_async_remote_copy(
            src_ref=src, dst_ref=dst, send_sem=send, recv_sem=recv, device_id=device, device_id_type=MESH
        )

    def rows(first, count=CHUNK):
        return pl.ds(first, count)

    matrix_loads = []
    for c in range(all_chunks):
        part = rows(c * CHUNK)
        matrix_loads.append(
            [
                pltpu.make_async_copy(coeffs_in.at[part], coeffs.at[part], coeffs_sem.at[c]),
                pltpu.make_async_copy(amps_in.at[part], amps.at[part], amps_sem.at[c]),
            ]
        )
    domain_load = pltpu.make_async_copy(domains_in, doms.at[rows(pairs, pairs)], load_sem.at[0])
    small_loads = [
        pltpu.make_async_copy(neighbours_in, neighbours, load_sem.at[1]),
        pltpu.make_async_copy(counts_in, counts, load_sem.at[2]),
        pltpu.make_async_copy(couplings_in, couplings, load_sem.at[3]),
        pltpu.make_async_copy(pno_in, pno, load_sem.at[4]),
        pltpu.make_async_copy(occ_in, occ, load_sem.at[5]),
    ]
    via_loads = [
        pltpu.make_async_copy(
            ints.at[rows(down * pairs, half)], via.at[0, :, pl.ds(0, depth)], via_sem.at[0]
        ),
        pltpu.make_async_copy(
            ints.at[rows(up * pairs + half, half)], via.at[1, :, pl.ds(0, depth)], via_sem.at[1]
        ),
    ]
    own_load = pltpu.make_async_copy(ints.at[rows(aux * pairs, pairs)], own.at[:, pl.ds(0, depth)], own_sem)
    for copy in sum(matrix_loads, []) + [domain_load] + small_loads + [own_load] + via_loads:
        copy.start()

    def to_pao(c):
        for copy in matrix_loads[c]:
            copy.wait()
        here = [c * CHUNK + i for i in range(CHUNK)]
        left_half = [contract(coeffs[p], amps[p], 1, 0).astype(BF16) for p in here]
        for p, block in zip(here, left_half):
            pao[pairs + p] = contract(block, coeffs[p], 1, 1).astype(BF16)

    to_pao(0)
    domain_load.wait()

    pl.semaphore_wait(barrier, jnp.where(at_end, 3, 2))

    @pl.when(jnp.logical_and(last_end, pair < n_pair - 1))
    def _():
        greet(ready, next_pair)

    raw = [
        remote(
            ints.at[rows(far * pairs + side * half + c * CHUNK)],
            via.at[side, rows(c * CHUNK), pl.ds(depth, depth)],
            raw_send.at[side, c],
            raw_recv.at[side, c],
            device,
        )
        for c in range(chunks)
        for side, device in ((0, to_down), (1, to_up))
    ]
    for copy in raw:
        copy.start()

    targets = (
        (0, to_up, jnp.where(last_end, 3, 0)),
        (1, to_down, jnp.where(first_end, 3, 2)),
    )
    domain_halo = [
        remote(
            doms.at[rows(pairs, pairs)],
            doms.at[rows(part * pairs, pairs)],
            dom_send.at[side],
            dom_recv.at[part],
            device,
        )
        for side, device, part in targets
    ]
    for copy in domain_halo:
        copy.start()
    halo = [
        [
            remote(
                pao.at[rows(pairs + c * CHUNK)],
                pao.at[rows(part * pairs + c * CHUNK)],
                halo_send.at[side, c],
                halo_recv.at[part, c],
                device,
            )
            for side, device, part in targets
        ]
        for c in range(all_chunks)
    ]

    for c in range(all_chunks):
        if c > 0:
            to_pao(c)
        for copy in halo[c]:
            copy.start()

    def arrival(part, c):
        return remote(
            pao.at[rows(pairs + c * CHUNK)],
            pao.at[rows(part * pairs + c * CHUNK)],
            halo_send.at[0, c],
            halo_recv.at[part, c],
            to_up,
        )

    def domain_arrival(part):
        return remote(
            doms.at[rows(pairs, pairs)], doms.at[rows(part * pairs, pairs)], dom_send.at[0], dom_recv.at[part], to_up
        )

    pass_to = (jnp.where(first_end, next_pair[0], last_pair[0]), aux)
    pass_part = jnp.where(first_end, 0, 2)
    domain_pass = remote(
        doms.at[rows(3 * pairs, pairs)],
        doms.at[rows(pass_part * pairs, pairs)],
        pass_dom_send,
        dom_recv.at[pass_part],
        pass_to,
    )
    passed = [
        remote(
            pao.at[rows(3 * pairs + c * CHUNK)],
            pao.at[rows(pass_part * pairs + c * CHUNK)],
            pass_send.at[c],
            halo_recv.at[pass_part, c],
            pass_to,
        )
        for c in range(all_chunks)
    ]

    def pass_on():
        @pl.when(at_end)
        def _():
            domain_arrival(3).wait_recv()

        @pl.when(jnp.logical_and(last_end, pair > 0))
        def _():
            pl.semaphore_wait(ready, 1)

        @pl.when(passes)
        def _():
            domain_pass.start()

        for c in range(all_chunks):

            @pl.when(at_end)
            def _():
                arrival(3, c).wait_recv()

            @pl.when(passes)
            def _():
                passed[c].start()

    def prepare(first, count):
        for p in range(first, first + count):
            energies = jnp.broadcast_to(pno[pl.ds(p, 1), :], (width, width))
            denominator = energies.T + energies + occ[p]
            inverse[p] = 1.0 / denominator
            block = own[p, pl.ds(0, depth), :]
            exchange = contract(block[:, :width], block[:, width:], 0, 0)
            acc[p] = exchange + denominator * amps[p].astype(F32)
            mine[p] = jnp.broadcast_to(doms[pl.ds(pairs + p, 1), :], (width, width)).T
            flipped[p] = coeffs[p].T

    near = [
        remote(
            ints.at[rows(there * pairs + side * half + c * CHUNK)],
            own.at[rows(side * half + c * CHUNK), pl.ds(depth, depth)],
            near_send.at[side, c],
            near_recv.at[side, c],
            device,
        )
        for c in range(chunks)
        for side, device, there in ((0, to_up, up), (1, to_down, down))
    ]
    sums = [
        remote(
            summed.at[side, rows(c * CHUNK)],
            arrived.at[rows(side * half + c * CHUNK)],
            summed_send.at[side, c],
            summed_recv.at[side, c],
            device,
        )
        for c in range(chunks)
        for side, device in ((0, to_down), (1, to_up))
    ]

    for copy in small_loads:
        copy.wait()
    own_load.wait()
    prepare(0, half)

    for copy in via_loads:
        copy.wait()
    for c in range(chunks):
        for side in (0, 1):
            raw[c * 2 + side].wait_recv()
            for p in range(c * CHUNK, c * CHUNK + CHUNK):
                block = via[side, p]
                summed[side, p] = contract(block[:, :width], block[:, width:], 0, 0).astype(BF16)
            sums[c * 2 + side].start()
    for copy in near:
        copy.start()

    prepare(half, pairs - half)
    pass_on()

    for part, none in ((0, no_left), (2, no_right)):

        @pl.when(jnp.logical_not(none))
        def _():
            domain_arrival(part).wait_recv()
            for c in range(all_chunks):
                arrival(part, c).wait_recv()

        @pl.when(none)
        def _():
            doms[pl.ds(part * pairs, pairs), :] = jnp.full((pairs, width), -1, jnp.int32)
            pao[pl.ds(part * pairs, pairs)] = jnp.zeros((pairs, width, width), BF16)

    first_row = ((pair * n_aux + aux) - 1) * pairs

    def couple(step, carry):
        here = [step * TOGETHER + i for i in range(TOGETHER)]
        totals = []
        for p in here:
            column = mine[p]
            matches, scaled = [], []
            for k in range(slots):
                row = jnp.clip(neighbours[k, p] - first_row, 0, 3 * pairs - 1)
                weight = jnp.where(k < counts[p], couplings[k, p], 0.0)
                match = jnp.where(column == doms[pl.ds(row, 1), :], 1.0, 0.0).astype(BF16)
                picked = contract(match, pao[row], 1, 0)
                matches.append(match)
                scaled.append((weight * picked).astype(BF16))
            total = contract(jnp.concatenate(scaled, axis=1), jnp.concatenate(matches, axis=1), 1, 1)
            totals.append(total.astype(BF16))
        halves = [contract(total, coeffs[p], 1, 0).astype(BF16) for p, total in zip(here, totals)]
        for p, right_half in zip(here, halves):
            acc[p] += contract(flipped[p], right_half, 1, 0)
        return carry

    lax.fori_loop(0, pairs // TOGETHER, couple, 0)

    for c in range(chunks):
        for side in (0, 1):
            near[c * 2 + side].wait_recv()
            sums[c * 2 + side].wait_recv()
            first = side * half + c * CHUNK
            for p in range(first, first + CHUNK):
                block = own[p, pl.ds(depth, depth), :]
                exchange = contract(block[:, :width], block[:, width:], 0, 0) + arrived[p].astype(F32)
                result = acc[p] + exchange
                residual[p] = result
                updated[p] = (amps[p].astype(F32) - result * inverse[p]).astype(BF16)

    for copy in raw + near + sums + domain_halo + sum(halo, []):
        copy.wait_send()

    @pl.when(passes)
    def _():
        for copy in [domain_pass] + passed:
            copy.wait_send()


def hand_over(residual_in, updated_in, residual, updated, sems):
    copies = [
        pltpu.make_async_copy(residual_in, residual, sems.at[0]),
        pltpu.make_async_copy(updated_in, updated, sems.at[1]),
    ]
    for copy in copies:
        copy.start()
    for copy in copies:
        copy.wait()


def per_device(
    integrals,
    amplitudes,
    coeffs,
    domains,
    neighbours,
    counts,
    couplings,
    pno_energies,
    occ_energies,
):
    pairs, width, _ = amplitudes.shape
    depth = integrals.shape[1]
    half = pairs // 2
    chunks = half // CHUNK
    in_hbm = pl.BlockSpec(memory_space=pltpu.HBM)
    in_vmem = pl.BlockSpec(memory_space=pltpu.VMEM)
    dma = pltpu.SemaphoreType.DMA
    operands = (
        integrals, amplitudes, coeffs, domains, neighbours.T, counts, couplings.T, pno_energies, occ_energies,
    )
    residual, updated = pl.pallas_call(
        kernel,
        out_shape=(
            pltpu.VMEM((pairs, width, width), F32),
            pltpu.VMEM((pairs, width, width), BF16),
        ),
        in_specs=[in_hbm] * len(operands),
        out_specs=(in_vmem, in_vmem),
        scratch_shapes=[
            pltpu.VMEM((pairs, width, width), BF16),
            pltpu.VMEM((pairs, width, width), BF16),
            pltpu.VMEM((4 * pairs, width, width), BF16),
            pltpu.VMEM((4 * pairs, width), jnp.int32),
            pltpu.SMEM(neighbours.shape[::-1], jnp.int32),
            pltpu.SMEM(counts.shape, jnp.int32),
            pltpu.SMEM(couplings.shape[::-1], F32),
            pltpu.VMEM(pno_energies.shape, F32),
            pltpu.SMEM(occ_energies.shape, F32),
            pltpu.VMEM((pairs, 2 * depth, 2 * width), BF16),
            pltpu.VMEM((2, half, 2 * depth, 2 * width), BF16),
            pltpu.VMEM((2, half, width, width), BF16),
            pltpu.VMEM((pairs, width, width), BF16),
            pltpu.VMEM((pairs, width, width), F32),
            pltpu.VMEM((pairs, width, width), F32),
            pltpu.VMEM((pairs, width, width), jnp.int32),
            pltpu.VMEM((pairs, width, width), BF16),
            dma((2 * chunks,)),
            dma((2 * chunks,)),
            dma((6,)),
            dma(()),
            dma((2,)),
            dma((2, chunks)),
            dma((2, chunks)),
            dma((2, chunks)),
            dma((2, chunks)),
            dma((2, chunks)),
            dma((2, chunks)),
            dma((2, 2 * chunks)),
            dma((4, 2 * chunks)),
            dma((2,)),
            dma((4,)),
            dma((2 * chunks,)),
            dma(()),
            pltpu.SemaphoreType.REGULAR,
        ],
        compiler_params=pltpu.CompilerParams(
            collective_id=0, has_side_effects=True, vmem_limit_bytes=32 * 1024 * 1024
        ),
        name="doubles_residual",
    )(*(pltpu.with_memory_space_constraint(operand, pltpu.HBM) for operand in operands))
    return pl.pallas_call(
        hand_over,
        out_shape=(
            jax.ShapeDtypeStruct((pairs, width, width), F32),
            jax.ShapeDtypeStruct((pairs, width, width), BF16),
        ),
        in_specs=(in_vmem, in_vmem),
        out_specs=(in_hbm, in_hbm),
        scratch_shapes=[dma((2,))],
        compiler_params=pltpu.CompilerParams(vmem_limit_bytes=16 * 1024 * 1024),
        name="hand_over",
    )(residual, updated)


def solution(mesh):
    in_specs = (
        P("pair", "aux", None),
        P(("pair", "aux"), None, None),
        P(("pair", "aux"), None, None),
        P(("pair", "aux"), None),
        P(("pair", "aux"), None),
        P(("pair", "aux")),
        P(("pair", "aux"), None),
        P(("pair", "aux"), None),
        P(("pair", "aux")),
    )
    out_specs = (P(("pair", "aux"), None, None), P(("pair", "aux"), None, None))
    return jax.shard_map(
        per_device, mesh=mesh, in_specs=in_specs, out_specs=out_specs, check_vma=False
    )
```

```python
import jax
import jax.numpy as jnp
from jax import lax
from jax.experimental import pallas as pl
from jax.experimental.pallas import tpu as pltpu
from jax.sharding import PartitionSpec as P

MESH = pl.DeviceIdType.MESH
F32 = jnp.float32
BF16 = jnp.bfloat16
CHUNK = 4
TOGETHER = 4


def contract(a, b, dim_a, dim_b):
    return lax.dot_general(a, b, (((dim_a,), (dim_b,)), ((), ())), preferred_element_type=F32)


def kernel(
    ints, amps_in, coeffs_in, domains_in, neighbours_in, counts_in, couplings_in, pno_in, occ_in,
    residual, updated,
    amps, coeffs, pao, doms, neighbours, counts, couplings, pno, occ, own, via, summed, arrived,
    acc, inverse, mine, flipped,
    amps_sem, coeffs_sem, load_sem, own_sem, via_sem, raw_send, raw_recv, near_send, near_recv,
    summed_send, summed_recv, halo_send, halo_recv, dom_send, dom_recv, pass_send, pass_dom_send, ready,
):
    n_pair, n_aux = lax.axis_size("pair"), lax.axis_size("aux")
    pair, aux = lax.axis_index("pair"), lax.axis_index("aux")
    pairs = amps.shape[0]
    half = pairs // 2
    depth = ints.shape[1]
    width = amps.shape[1]
    slots = neighbours.shape[0]
    chunks = half // CHUNK
    all_chunks = pairs // CHUNK

    up, down, far = (aux + 1) % n_aux, (aux + n_aux - 1) % n_aux, (aux + 2) % n_aux
    to_up, to_down = (pair, up), (pair, down)
    next_pair, last_pair = ((pair + 1) % n_pair, aux), ((pair + n_pair - 1) % n_pair, aux)
    first_end, last_end = aux == 0, aux == n_aux - 1
    at_end = jnp.logical_or(first_end, last_end)
    no_left = jnp.logical_and(first_end, pair == 0)
    no_right = jnp.logical_and(last_end, pair == n_pair - 1)
    passes = jnp.logical_or(
        jnp.logical_and(first_end, pair < n_pair - 1), jnp.logical_and(last_end, pair > 0)
    )

    barrier = pltpu.get_barrier_semaphore()

    def greet(semaphore, device):
        pl.semaphore_signal(semaphore, inc=1, device_id=device, device_id_type=MESH)

    greet(barrier, to_up)
    greet(barrier, to_down)

    @pl.when(at_end)
    def _():
        greet(barrier, last_pair)

    def remote(src, dst, send, recv, device):
        return pltpu.make_async_remote_copy(
            src_ref=src, dst_ref=dst, send_sem=send, recv_sem=recv, device_id=device, device_id_type=MESH
        )

    def rows(first, count=CHUNK):
        return pl.ds(first, count)

    matrix_loads = []
    for c in range(all_chunks):
        part = rows(c * CHUNK)
        matrix_loads.append(
            [
                pltpu.make_async_copy(coeffs_in.at[part], coeffs.at[part], coeffs_sem.at[c]),
                pltpu.make_async_copy(amps_in.at[part], amps.at[part], amps_sem.at[c]),
            ]
        )
    domain_load = pltpu.make_async_copy(domains_in, doms.at[rows(pairs, pairs)], load_sem.at[0])
    small_loads = [
        pltpu.make_async_copy(neighbours_in, neighbours, load_sem.at[1]),
        pltpu.make_async_copy(counts_in, counts, load_sem.at[2]),
        pltpu.make_async_copy(couplings_in, couplings, load_sem.at[3]),
        pltpu.make_async_copy(pno_in, pno, load_sem.at[4]),
        pltpu.make_async_copy(occ_in, occ, load_sem.at[5]),
    ]
    via_loads = [
        pltpu.make_async_copy(
            ints.at[rows(down * pairs, half)], via.at[0, :, pl.ds(0, depth)], via_sem.at[0]
        ),
        pltpu.make_async_copy(
            ints.at[rows(up * pairs + half, half)], via.at[1, :, pl.ds(0, depth)], via_sem.at[1]
        ),
    ]
    own_load = pltpu.make_async_copy(ints.at[rows(aux * pairs, pairs)], own.at[:, pl.ds(0, depth)], own_sem)
    for copy in sum(matrix_loads, []) + [domain_load] + small_loads + [own_load] + via_loads:
        copy.start()

    def to_pao(c):
        for copy in matrix_loads[c]:
            copy.wait()
        here = [c * CHUNK + i for i in range(CHUNK)]
        left_half = [contract(coeffs[p], amps[p], 1, 0).astype(BF16) for p in here]
        for p, block in zip(here, left_half):
            pao[pairs + p] = contract(block, coeffs[p], 1, 1).astype(BF16)

    to_pao(0)
    domain_load.wait()
    early = all_chunks // 2

    pl.semaphore_wait(barrier, jnp.where(at_end, 3, 2))

    @pl.when(jnp.logical_and(last_end, pair < n_pair - 1))
    def _():
        greet(ready, next_pair)

    raw = [
        remote(
            ints.at[rows(far * pairs + side * half + c * CHUNK)],
            via.at[side, rows(c * CHUNK), pl.ds(depth, depth)],
            raw_send.at[side, c],
            raw_recv.at[side, c],
            device,
        )
        for c in range(chunks)
        for side, device in ((0, to_down), (1, to_up))
    ]
    targets = (
        (0, to_up, jnp.where(last_end, 3, 0)),
        (1, to_down, jnp.where(first_end, 3, 2)),
    )
    domain_halo = [
        remote(
            doms.at[rows(pairs, pairs)],
            doms.at[rows(part * pairs, pairs)],
            dom_send.at[side],
            dom_recv.at[part],
            device,
        )
        for side, device, part in targets
    ]
    for copy in domain_halo:
        copy.start()
    halo = [
        [
            remote(
                pao.at[rows(pairs + c * CHUNK)],
                pao.at[rows(part * pairs + c * CHUNK)],
                halo_send.at[side, c],
                halo_recv.at[part, c],
                device,
            )
            for side, device, part in targets
        ]
        for c in range(all_chunks)
    ]

    for c in range(all_chunks):
        if c > 0:
            to_pao(c)
        if c < early:
            for copy in halo[c]:
                copy.start()

    def arrival(part, c):
        return remote(
            pao.at[rows(pairs + c * CHUNK)],
            pao.at[rows(part * pairs + c * CHUNK)],
            halo_send.at[0, c],
            halo_recv.at[part, c],
            to_up,
        )

    def domain_arrival(part):
        return remote(
            doms.at[rows(pairs, pairs)], doms.at[rows(part * pairs, pairs)], dom_send.at[0], dom_recv.at[part], to_up
        )

    pass_to = (jnp.where(first_end, next_pair[0], last_pair[0]), aux)
    pass_part = jnp.where(first_end, 0, 2)
    domain_pass = remote(
        doms.at[rows(3 * pairs, pairs)],
        doms.at[rows(pass_part * pairs, pairs)],
        pass_dom_send,
        dom_recv.at[pass_part],
        pass_to,
    )
    passed = [
        remote(
            pao.at[rows(3 * pairs + c * CHUNK)],
            pao.at[rows(pass_part * pairs + c * CHUNK)],
            pass_send.at[c],
            halo_recv.at[pass_part, c],
            pass_to,
        )
        for c in range(all_chunks)
    ]

    def halo_sent(c):
        for copy in halo[c]:
            copy.wait_send()
        if c + early < all_chunks:
            for copy in halo[c + early]:
                copy.start()

    def pass_on(c):
        @pl.when(at_end)
        def _():
            if c == 0:
                domain_arrival(3).wait_recv()
            arrival(3, c).wait_recv()

        if c == 0:

            @pl.when(jnp.logical_and(last_end, pair > 0))
            def _():
                pl.semaphore_wait(ready, 1)

        @pl.when(passes)
        def _():
            if c == 0:
                domain_pass.start()
            passed[c].start()

    def prepare(first, count):
        for p in range(first, first + count):
            energies = jnp.broadcast_to(pno[pl.ds(p, 1), :], (width, width))
            denominator = energies.T + energies + occ[p]
            inverse[p] = 1.0 / denominator
            block = own[p, pl.ds(0, depth), :]
            exchange = contract(block[:, :width], block[:, width:], 0, 0)
            acc[p] = exchange + denominator * amps[p].astype(F32)
            mine[p] = jnp.broadcast_to(doms[pl.ds(pairs + p, 1), :], (width, width)).T
            flipped[p] = coeffs[p].T

    near = [
        remote(
            ints.at[rows(there * pairs + side * half + c * CHUNK)],
            own.at[rows(side * half + c * CHUNK), pl.ds(depth, depth)],
            near_send.at[side, c],
            near_recv.at[side, c],
            device,
        )
        for c in range(chunks)
        for side, device, there in ((0, to_up, up), (1, to_down, down))
    ]
    sums = [
        remote(
            summed.at[side, rows(c * CHUNK)],
            arrived.at[rows(side * half + c * CHUNK)],
            summed_send.at[side, c],
            summed_recv.at[side, c],
            device,
        )
        for c in range(chunks)
        for side, device in ((0, to_down), (1, to_up))
    ]

    for copy in small_loads:
        copy.wait()
    own_load.wait()
    for c in range(all_chunks):
        prepare(c * CHUNK, CHUNK)
        halo_sent(c)
        if c == early - 1:
            for copy in raw:
                copy.start()
        if c >= early:
            for copy in near[(c - early) * 2 : (c - early) * 2 + 2]:
                copy.start()
        pass_on(c)

    for copy in via_loads:
        copy.wait()
    for c in range(chunks):
        for side in (0, 1):
            raw[c * 2 + side].wait_recv()
            for p in range(c * CHUNK, c * CHUNK + CHUNK):
                block = via[side, p]
                summed[side, p] = contract(block[:, :width], block[:, width:], 0, 0).astype(BF16)
            sums[c * 2 + side].start()

    for part, none in ((0, no_left), (2, no_right)):

        @pl.when(jnp.logical_not(none))
        def _():
            domain_arrival(part).wait_recv()
            for c in range(all_chunks):
                arrival(part, c).wait_recv()

        @pl.when(none)
        def _():
            doms[pl.ds(part * pairs, pairs), :] = jnp.full((pairs, width), -1, jnp.int32)
            pao[pl.ds(part * pairs, pairs)] = jnp.zeros((pairs, width, width), BF16)

    first_row = ((pair * n_aux + aux) - 1) * pairs

    def couple(step, carry):
        here = [step * TOGETHER + i for i in range(TOGETHER)]
        totals = []
        for p in here:
            column = mine[p]
            matches, scaled = [], []
            for k in range(slots):
                row = jnp.clip(neighbours[k, p] - first_row, 0, 3 * pairs - 1)
                weight = jnp.where(k < counts[p], couplings[k, p], 0.0)
                match = jnp.where(column == doms[pl.ds(row, 1), :], 1.0, 0.0).astype(BF16)
                picked = contract(match, pao[row], 1, 0)
                matches.append(match)
                scaled.append((weight * picked).astype(BF16))
            total = contract(jnp.concatenate(scaled, axis=1), jnp.concatenate(matches, axis=1), 1, 1)
            totals.append(total.astype(BF16))
        halves = [contract(total, coeffs[p], 1, 0).astype(BF16) for p, total in zip(here, totals)]
        for p, right_half in zip(here, halves):
            acc[p] += contract(flipped[p], right_half, 1, 0)
        return carry

    lax.fori_loop(0, pairs // TOGETHER, couple, 0)

    for c in range(chunks):
        for side in (0, 1):
            near[c * 2 + side].wait_recv()
            sums[c * 2 + side].wait_recv()
            first = side * half + c * CHUNK
            for p in range(first, first + CHUNK):
                block = own[p, pl.ds(depth, depth), :]
                exchange = contract(block[:, :width], block[:, width:], 0, 0) + arrived[p].astype(F32)
                result = acc[p] + exchange
                residual[p] = result
                updated[p] = (amps[p].astype(F32) - result * inverse[p]).astype(BF16)

    for copy in raw + near + sums + domain_halo:
        copy.wait_send()

    @pl.when(passes)
    def _():
        for copy in [domain_pass] + passed:
            copy.wait_send()


def hand_over(residual_in, updated_in, residual, updated, sems):
    copies = [
        pltpu.make_async_copy(residual_in, residual, sems.at[0]),
        pltpu.make_async_copy(updated_in, updated, sems.at[1]),
    ]
    for copy in copies:
        copy.start()
    for copy in copies:
        copy.wait()


def per_device(
    integrals,
    amplitudes,
    coeffs,
    domains,
    neighbours,
    counts,
    couplings,
    pno_energies,
    occ_energies,
):
    pairs, width, _ = amplitudes.shape
    depth = integrals.shape[1]
    half = pairs // 2
    chunks = half // CHUNK
    in_hbm = pl.BlockSpec(memory_space=pltpu.HBM)
    in_vmem = pl.BlockSpec(memory_space=pltpu.VMEM)
    dma = pltpu.SemaphoreType.DMA
    operands = (
        integrals, amplitudes, coeffs, domains, neighbours.T, counts, couplings.T, pno_energies, occ_energies,
    )
    residual, updated = pl.pallas_call(
        kernel,
        out_shape=(
            pltpu.VMEM((pairs, width, width), F32),
            pltpu.VMEM((pairs, width, width), BF16),
        ),
        in_specs=[in_hbm] * len(operands),
        out_specs=(in_vmem, in_vmem),
        scratch_shapes=[
            pltpu.VMEM((pairs, width, width), BF16),
            pltpu.VMEM((pairs, width, width), BF16),
            pltpu.VMEM((4 * pairs, width, width), BF16),
            pltpu.VMEM((4 * pairs, width), jnp.int32),
            pltpu.SMEM(neighbours.shape[::-1], jnp.int32),
            pltpu.SMEM(counts.shape, jnp.int32),
            pltpu.SMEM(couplings.shape[::-1], F32),
            pltpu.VMEM(pno_energies.shape, F32),
            pltpu.SMEM(occ_energies.shape, F32),
            pltpu.VMEM((pairs, 2 * depth, 2 * width), BF16),
            pltpu.VMEM((2, half, 2 * depth, 2 * width), BF16),
            pltpu.VMEM((2, half, width, width), BF16),
            pltpu.VMEM((pairs, width, width), BF16),
            pltpu.VMEM((pairs, width, width), F32),
            pltpu.VMEM((pairs, width, width), F32),
            pltpu.VMEM((pairs, width, width), jnp.int32),
            pltpu.VMEM((pairs, width, width), BF16),
            dma((2 * chunks,)),
            dma((2 * chunks,)),
            dma((6,)),
            dma(()),
            dma((2,)),
            dma((2, chunks)),
            dma((2, chunks)),
            dma((2, chunks)),
            dma((2, chunks)),
            dma((2, chunks)),
            dma((2, chunks)),
            dma((2, 2 * chunks)),
            dma((4, 2 * chunks)),
            dma((2,)),
            dma((4,)),
            dma((2 * chunks,)),
            dma(()),
            pltpu.SemaphoreType.REGULAR,
        ],
        compiler_params=pltpu.CompilerParams(
            collective_id=0, has_side_effects=True, vmem_limit_bytes=32 * 1024 * 1024
        ),
        name="doubles_residual",
    )(*(pltpu.with_memory_space_constraint(operand, pltpu.HBM) for operand in operands))
    return pl.pallas_call(
        hand_over,
        out_shape=(
            jax.ShapeDtypeStruct((pairs, width, width), F32),
            jax.ShapeDtypeStruct((pairs, width, width), BF16),
        ),
        in_specs=(in_vmem, in_vmem),
        out_specs=(in_hbm, in_hbm),
        scratch_shapes=[dma((2,))],
        compiler_params=pltpu.CompilerParams(vmem_limit_bytes=16 * 1024 * 1024),
        name="hand_over",
    )(residual, updated)


def solution(mesh):
    in_specs = (
        P("pair", "aux", None),
        P(("pair", "aux"), None, None),
        P(("pair", "aux"), None, None),
        P(("pair", "aux"), None),
        P(("pair", "aux"), None),
        P(("pair", "aux")),
        P(("pair", "aux"), None),
        P(("pair", "aux"), None),
        P(("pair", "aux")),
    )
    out_specs = (P(("pair", "aux"), None, None), P(("pair", "aux"), None, None))
    return jax.shard_map(
        per_device, mesh=mesh, in_specs=in_specs, out_specs=out_specs, check_vma=False
    )
```

```python
import jax
import jax.numpy as jnp
from jax import lax
from jax.experimental import pallas as pl
from jax.experimental.pallas import tpu as pltpu
from jax.sharding import PartitionSpec as P

MESH = pl.DeviceIdType.MESH
F32 = jnp.float32
BF16 = jnp.bfloat16
CHUNK = 4
TOGETHER = 4


def contract(a, b, dim_a, dim_b):
    return lax.dot_general(a, b, (((dim_a,), (dim_b,)), ((), ())), preferred_element_type=F32)


def kernel(
    ints, amps_in, coeffs_in, domains_in, neighbours_in, counts_in, couplings_in, pno_in, occ_in,
    residual, updated,
    amps, coeffs, pao, doms, neighbours, counts, couplings, pno, occ, own, via, summed, arrived,
    acc, inverse, mine, flipped,
    amps_sem, coeffs_sem, load_sem, own_sem, via_sem, raw_send, raw_recv, near_send, near_recv,
    summed_send, summed_recv, halo_send, halo_recv, dom_send, dom_recv, pass_send, pass_dom_send, ready,
):
    n_pair, n_aux = lax.axis_size("pair"), lax.axis_size("aux")
    pair, aux = lax.axis_index("pair"), lax.axis_index("aux")
    pairs = amps.shape[0]
    half = pairs // 2
    depth = ints.shape[1]
    width = amps.shape[1]
    slots = neighbours.shape[0]
    chunks = half // CHUNK
    all_chunks = pairs // CHUNK

    up, down, far = (aux + 1) % n_aux, (aux + n_aux - 1) % n_aux, (aux + 2) % n_aux
    to_up, to_down = (pair, up), (pair, down)
    next_pair, last_pair = ((pair + 1) % n_pair, aux), ((pair + n_pair - 1) % n_pair, aux)
    first_end, last_end = aux == 0, aux == n_aux - 1
    at_end = jnp.logical_or(first_end, last_end)
    no_left = jnp.logical_and(first_end, pair == 0)
    no_right = jnp.logical_and(last_end, pair == n_pair - 1)
    passes = jnp.logical_or(
        jnp.logical_and(first_end, pair < n_pair - 1), jnp.logical_and(last_end, pair > 0)
    )

    barrier = pltpu.get_barrier_semaphore()

    def greet(semaphore, device):
        pl.semaphore_signal(semaphore, inc=1, device_id=device, device_id_type=MESH)

    greet(barrier, to_up)
    greet(barrier, to_down)

    @pl.when(at_end)
    def _():
        greet(barrier, last_pair)

    def remote(src, dst, send, recv, device):
        return pltpu.make_async_remote_copy(
            src_ref=src, dst_ref=dst, send_sem=send, recv_sem=recv, device_id=device, device_id_type=MESH
        )

    def rows(first, count=CHUNK):
        return pl.ds(first, count)

    matrix_loads = []
    for c in range(all_chunks):
        part = rows(c * CHUNK)
        matrix_loads.append(
            [
                pltpu.make_async_copy(coeffs_in.at[part], coeffs.at[part], coeffs_sem.at[c]),
                pltpu.make_async_copy(amps_in.at[part], amps.at[part], amps_sem.at[c]),
            ]
        )
    domain_load = pltpu.make_async_copy(domains_in, doms.at[rows(pairs, pairs)], load_sem.at[0])
    small_loads = [
        pltpu.make_async_copy(neighbours_in, neighbours, load_sem.at[1]),
        pltpu.make_async_copy(counts_in, counts, load_sem.at[2]),
        pltpu.make_async_copy(couplings_in, couplings, load_sem.at[3]),
        pltpu.make_async_copy(pno_in, pno, load_sem.at[4]),
        pltpu.make_async_copy(occ_in, occ, load_sem.at[5]),
    ]
    via_loads = [
        pltpu.make_async_copy(
            ints.at[rows(down * pairs, half)], via.at[0, :, pl.ds(0, depth)], via_sem.at[0]
        ),
        pltpu.make_async_copy(
            ints.at[rows(up * pairs + half, half)], via.at[1, :, pl.ds(0, depth)], via_sem.at[1]
        ),
    ]
    own_load = pltpu.make_async_copy(ints.at[rows(aux * pairs, pairs)], own.at[:, pl.ds(0, depth)], own_sem)
    for copy in sum(matrix_loads, []) + [domain_load] + small_loads + [own_load] + via_loads:
        copy.start()

    def to_pao(c):
        for copy in matrix_loads[c]:
            copy.wait()
        here = [c * CHUNK + i for i in range(CHUNK)]
        left_half = [contract(coeffs[p], amps[p], 1, 0).astype(BF16) for p in here]
        for p, block in zip(here, left_half):
            pao[pairs + p] = contract(block, coeffs[p], 1, 1).astype(BF16)

    to_pao(0)
    domain_load.wait()
    early = all_chunks // 2

    pl.semaphore_wait(barrier, jnp.where(at_end, 3, 2))

    @pl.when(jnp.logical_and(last_end, pair < n_pair - 1))
    def _():
        greet(ready, next_pair)

    raw = [
        remote(
            ints.at[rows(far * pairs + side * half + c * CHUNK)],
            via.at[side, rows(c * CHUNK), pl.ds(depth, depth)],
            raw_send.at[side, c],
            raw_recv.at[side, c],
            device,
        )
        for c in range(chunks)
        for side, device in ((0, to_down), (1, to_up))
    ]
    targets = (
        (0, to_up, jnp.where(last_end, 3, 0)),
        (1, to_down, jnp.where(first_end, 3, 2)),
    )
    domain_halo = [
        remote(
            doms.at[rows(pairs, pairs)],
            doms.at[rows(part * pairs, pairs)],
            dom_send.at[side],
            dom_recv.at[part],
            device,
        )
        for side, device, part in targets
    ]
    for copy in domain_halo:
        copy.start()
    halo = [
        [
            remote(
                pao.at[rows(pairs + c * CHUNK)],
                pao.at[rows(part * pairs + c * CHUNK)],
                halo_send.at[side, c],
                halo_recv.at[part, c],
                device,
            )
            for side, device, part in targets
        ]
        for c in range(all_chunks)
    ]

    for c in range(all_chunks):
        if c > 0:
            to_pao(c)
        for copy in halo[c]:
            copy.start()

    def arrival(part, c):
        return remote(
            pao.at[rows(pairs + c * CHUNK)],
            pao.at[rows(part * pairs + c * CHUNK)],
            halo_send.at[0, c],
            halo_recv.at[part, c],
            to_up,
        )

    def domain_arrival(part):
        return remote(
            doms.at[rows(pairs, pairs)], doms.at[rows(part * pairs, pairs)], dom_send.at[0], dom_recv.at[part], to_up
        )

    pass_to = (jnp.where(first_end, next_pair[0], last_pair[0]), aux)
    pass_part = jnp.where(first_end, 0, 2)
    domain_pass = remote(
        doms.at[rows(3 * pairs, pairs)],
        doms.at[rows(pass_part * pairs, pairs)],
        pass_dom_send,
        dom_recv.at[pass_part],
        pass_to,
    )
    passed = [
        remote(
            pao.at[rows(3 * pairs + c * CHUNK)],
            pao.at[rows(pass_part * pairs + c * CHUNK)],
            pass_send.at[c],
            halo_recv.at[pass_part, c],
            pass_to,
        )
        for c in range(all_chunks)
    ]

    def halo_sent(c):
        for copy in halo[c]:
            copy.wait_send()

    def pass_on(c):
        @pl.when(at_end)
        def _():
            if c == 0:
                domain_arrival(3).wait_recv()
            arrival(3, c).wait_recv()

        if c == 0:

            @pl.when(jnp.logical_and(last_end, pair > 0))
            def _():
                pl.semaphore_wait(ready, 1)

        @pl.when(passes)
        def _():
            if c == 0:
                domain_pass.start()
            passed[c].start()

    def prepare(first, count):
        for p in range(first, first + count):
            energies = jnp.broadcast_to(pno[pl.ds(p, 1), :], (width, width))
            denominator = energies.T + energies + occ[p]
            inverse[p] = 1.0 / denominator
            block = own[p, pl.ds(0, depth), :]
            exchange = contract(block[:, :width], block[:, width:], 0, 0)
            acc[p] = exchange + denominator * amps[p].astype(F32)
            mine[p] = jnp.broadcast_to(doms[pl.ds(pairs + p, 1), :], (width, width)).T
            flipped[p] = coeffs[p].T

    near = [
        remote(
            ints.at[rows(there * pairs + side * half + c * CHUNK)],
            own.at[rows(side * half + c * CHUNK), pl.ds(depth, depth)],
            near_send.at[side, c],
            near_recv.at[side, c],
            device,
        )
        for c in range(chunks)
        for side, device, there in ((0, to_up, up), (1, to_down, down))
    ]
    sums = [
        remote(
            summed.at[side, rows(c * CHUNK)],
            arrived.at[rows(side * half + c * CHUNK)],
            summed_send.at[side, c],
            summed_recv.at[side, c],
            device,
        )
        for c in range(chunks)
        for side, device in ((0, to_down), (1, to_up))
    ]

    for copy in small_loads:
        copy.wait()
    own_load.wait()
    for c in range(all_chunks):
        prepare(c * CHUNK, CHUNK)
        halo_sent(c)
        if c == early - 1:
            for copy in raw:
                copy.start()
        if c >= early:
            for copy in near[(c - early) * 2 : (c - early) * 2 + 2]:
                copy.start()
        pass_on(c)

    for part, none in ((0, no_left), (2, no_right)):

        @pl.when(jnp.logical_not(none))
        def _():
            domain_arrival(part).wait_recv()
            for c in range(all_chunks):
                arrival(part, c).wait_recv()

        @pl.when(none)
        def _():
            doms[pl.ds(part * pairs, pairs), :] = jnp.full((pairs, width), -1, jnp.int32)
            pao[pl.ds(part * pairs, pairs)] = jnp.zeros((pairs, width, width), BF16)

    first_row = ((pair * n_aux + aux) - 1) * pairs

    def couple(step, carry):
        here = [step * TOGETHER + i for i in range(TOGETHER)]
        totals = []
        for p in here:
            column = mine[p]
            matches, scaled = [], []
            for k in range(slots):
                row = jnp.clip(neighbours[k, p] - first_row, 0, 3 * pairs - 1)
                weight = jnp.where(k < counts[p], couplings[k, p], 0.0)
                match = jnp.where(column == doms[pl.ds(row, 1), :], 1.0, 0.0).astype(BF16)
                picked = contract(match, pao[row], 1, 0)
                matches.append(match)
                scaled.append((weight * picked).astype(BF16))
            total = contract(jnp.concatenate(scaled, axis=1), jnp.concatenate(matches, axis=1), 1, 1)
            totals.append(total.astype(BF16))
        halves = [contract(total, coeffs[p], 1, 0).astype(BF16) for p, total in zip(here, totals)]
        for p, right_half in zip(here, halves):
            acc[p] += contract(flipped[p], right_half, 1, 0)
        return carry

    steps = pairs // TOGETHER
    lax.fori_loop(0, steps // 2, couple, 0)

    for copy in via_loads:
        copy.wait()
    for c in range(chunks):
        for side in (0, 1):
            raw[c * 2 + side].wait_recv()
            for p in range(c * CHUNK, c * CHUNK + CHUNK):
                block = via[side, p]
                summed[side, p] = contract(block[:, :width], block[:, width:], 0, 0).astype(BF16)
            sums[c * 2 + side].start()

    lax.fori_loop(steps // 2, steps, couple, 0)

    for c in range(chunks):
        for side in (0, 1):
            near[c * 2 + side].wait_recv()
            sums[c * 2 + side].wait_recv()
            first = side * half + c * CHUNK
            for p in range(first, first + CHUNK):
                block = own[p, pl.ds(depth, depth), :]
                exchange = contract(block[:, :width], block[:, width:], 0, 0) + arrived[p].astype(F32)
                result = acc[p] + exchange
                residual[p] = result
                updated[p] = (amps[p].astype(F32) - result * inverse[p]).astype(BF16)

    for copy in raw + near + sums + domain_halo:
        copy.wait_send()

    @pl.when(passes)
    def _():
        for copy in [domain_pass] + passed:
            copy.wait_send()


def hand_over(residual_in, updated_in, residual, updated, sems):
    copies = [
        pltpu.make_async_copy(residual_in, residual, sems.at[0]),
        pltpu.make_async_copy(updated_in, updated, sems.at[1]),
    ]
    for copy in copies:
        copy.start()
    for copy in copies:
        copy.wait()


def per_device(
    integrals,
    amplitudes,
    coeffs,
    domains,
    neighbours,
    counts,
    couplings,
    pno_energies,
    occ_energies,
):
    pairs, width, _ = amplitudes.shape
    depth = integrals.shape[1]
    half = pairs // 2
    chunks = half // CHUNK
    in_hbm = pl.BlockSpec(memory_space=pltpu.HBM)
    in_vmem = pl.BlockSpec(memory_space=pltpu.VMEM)
    dma = pltpu.SemaphoreType.DMA
    operands = (
        integrals, amplitudes, coeffs, domains, neighbours.T, counts, couplings.T, pno_energies, occ_energies,
    )
    residual, updated = pl.pallas_call(
        kernel,
        out_shape=(
            pltpu.VMEM((pairs, width, width), F32),
            pltpu.VMEM((pairs, width, width), BF16),
        ),
        in_specs=[in_hbm] * len(operands),
        out_specs=(in_vmem, in_vmem),
        scratch_shapes=[
            pltpu.VMEM((pairs, width, width), BF16),
            pltpu.VMEM((pairs, width, width), BF16),
            pltpu.VMEM((4 * pairs, width, width), BF16),
            pltpu.VMEM((4 * pairs, width), jnp.int32),
            pltpu.SMEM(neighbours.shape[::-1], jnp.int32),
            pltpu.SMEM(counts.shape, jnp.int32),
            pltpu.SMEM(couplings.shape[::-1], F32),
            pltpu.VMEM(pno_energies.shape, F32),
            pltpu.SMEM(occ_energies.shape, F32),
            pltpu.VMEM((pairs, 2 * depth, 2 * width), BF16),
            pltpu.VMEM((2, half, 2 * depth, 2 * width), BF16),
            pltpu.VMEM((2, half, width, width), BF16),
            pltpu.VMEM((pairs, width, width), BF16),
            pltpu.VMEM((pairs, width, width), F32),
            pltpu.VMEM((pairs, width, width), F32),
            pltpu.VMEM((pairs, width, width), jnp.int32),
            pltpu.VMEM((pairs, width, width), BF16),
            dma((2 * chunks,)),
            dma((2 * chunks,)),
            dma((6,)),
            dma(()),
            dma((2,)),
            dma((2, chunks)),
            dma((2, chunks)),
            dma((2, chunks)),
            dma((2, chunks)),
            dma((2, chunks)),
            dma((2, chunks)),
            dma((2, 2 * chunks)),
            dma((4, 2 * chunks)),
            dma((2,)),
            dma((4,)),
            dma((2 * chunks,)),
            dma(()),
            pltpu.SemaphoreType.REGULAR,
        ],
        compiler_params=pltpu.CompilerParams(
            collective_id=0, has_side_effects=True, vmem_limit_bytes=32 * 1024 * 1024
        ),
        name="doubles_residual",
    )(*(pltpu.with_memory_space_constraint(operand, pltpu.HBM) for operand in operands))
    return pl.pallas_call(
        hand_over,
        out_shape=(
            jax.ShapeDtypeStruct((pairs, width, width), F32),
            jax.ShapeDtypeStruct((pairs, width, width), BF16),
        ),
        in_specs=(in_vmem, in_vmem),
        out_specs=(in_hbm, in_hbm),
        scratch_shapes=[dma((2,))],
        compiler_params=pltpu.CompilerParams(vmem_limit_bytes=16 * 1024 * 1024),
        name="hand_over",
    )(residual, updated)


def solution(mesh):
    in_specs = (
        P("pair", "aux", None),
        P(("pair", "aux"), None, None),
        P(("pair", "aux"), None, None),
        P(("pair", "aux"), None),
        P(("pair", "aux"), None),
        P(("pair", "aux")),
        P(("pair", "aux"), None),
        P(("pair", "aux"), None),
        P(("pair", "aux")),
    )
    out_specs = (P(("pair", "aux"), None, None), P(("pair", "aux"), None, None))
    return jax.shard_map(
        per_device, mesh=mesh, in_specs=in_specs, out_specs=out_specs, check_vma=False
    )
```

```python
import jax
import jax.numpy as jnp
from jax import lax
from jax.experimental import pallas as pl
from jax.experimental.pallas import tpu as pltpu
from jax.sharding import PartitionSpec as P

MESH = pl.DeviceIdType.MESH
F32 = jnp.float32
BF16 = jnp.bfloat16
CHUNK = 4
TOGETHER = 4


def contract(a, b, dim_a, dim_b):
    return lax.dot_general(a, b, (((dim_a,), (dim_b,)), ((), ())), preferred_element_type=F32)


def kernel(
    ints, amps_in, coeffs_in, domains_in, neighbours_in, counts_in, couplings_in, pno_in, occ_in,
    residual, updated,
    amps, coeffs, pao, doms, neighbours, counts, couplings, pno, occ, own, via, summed, arrived,
    acc, inverse, mine, flipped,
    amps_sem, coeffs_sem, load_sem, own_sem, via_sem, raw_send, raw_recv, near_send, near_recv,
    summed_send, summed_recv, halo_send, halo_recv, dom_send, dom_recv, pass_send, pass_dom_send, ready,
):
    n_pair, n_aux = lax.axis_size("pair"), lax.axis_size("aux")
    pair, aux = lax.axis_index("pair"), lax.axis_index("aux")
    pairs = amps.shape[0]
    half = pairs // 2
    depth = ints.shape[1]
    width = amps.shape[1]
    slots = neighbours.shape[0]
    chunks = half // CHUNK
    all_chunks = pairs // CHUNK

    up, down, far = (aux + 1) % n_aux, (aux + n_aux - 1) % n_aux, (aux + 2) % n_aux
    to_up, to_down = (pair, up), (pair, down)
    next_pair, last_pair = ((pair + 1) % n_pair, aux), ((pair + n_pair - 1) % n_pair, aux)
    first_end, last_end = aux == 0, aux == n_aux - 1
    at_end = jnp.logical_or(first_end, last_end)
    no_left = jnp.logical_and(first_end, pair == 0)
    no_right = jnp.logical_and(last_end, pair == n_pair - 1)
    passes = jnp.logical_or(
        jnp.logical_and(first_end, pair < n_pair - 1), jnp.logical_and(last_end, pair > 0)
    )

    barrier = pltpu.get_barrier_semaphore()

    def greet(semaphore, device):
        pl.semaphore_signal(semaphore, inc=1, device_id=device, device_id_type=MESH)

    greet(barrier, to_up)
    greet(barrier, to_down)

    @pl.when(at_end)
    def _():
        greet(barrier, last_pair)

    def remote(src, dst, send, recv, device):
        return pltpu.make_async_remote_copy(
            src_ref=src, dst_ref=dst, send_sem=send, recv_sem=recv, device_id=device, device_id_type=MESH
        )

    def rows(first, count=CHUNK):
        return pl.ds(first, count)

    matrix_loads = []
    for c in range(all_chunks):
        part = rows(c * CHUNK)
        matrix_loads.append(
            [
                pltpu.make_async_copy(coeffs_in.at[part], coeffs.at[part], coeffs_sem.at[c]),
                pltpu.make_async_copy(amps_in.at[part], amps.at[part], amps_sem.at[c]),
            ]
        )
    domain_load = pltpu.make_async_copy(domains_in, doms.at[rows(pairs, pairs)], load_sem.at[0])
    small_loads = [
        pltpu.make_async_copy(neighbours_in, neighbours, load_sem.at[1]),
        pltpu.make_async_copy(counts_in, counts, load_sem.at[2]),
        pltpu.make_async_copy(couplings_in, couplings, load_sem.at[3]),
        pltpu.make_async_copy(pno_in, pno, load_sem.at[4]),
        pltpu.make_async_copy(occ_in, occ, load_sem.at[5]),
    ]
    via_loads = [
        pltpu.make_async_copy(
            ints.at[rows(down * pairs, half)], via.at[0, :, pl.ds(0, depth)], via_sem.at[0]
        ),
        pltpu.make_async_copy(
            ints.at[rows(up * pairs + half, half)], via.at[1, :, pl.ds(0, depth)], via_sem.at[1]
        ),
    ]
    own_load = pltpu.make_async_copy(ints.at[rows(aux * pairs, pairs)], own.at[:, pl.ds(0, depth)], own_sem)
    for copy in sum(matrix_loads, []) + [domain_load] + small_loads + [own_load] + via_loads:
        copy.start()

    def to_pao(c):
        for copy in matrix_loads[c]:
            copy.wait()
        here = [c * CHUNK + i for i in range(CHUNK)]
        left_half = [contract(coeffs[p], amps[p], 1, 0).astype(BF16) for p in here]
        for p, block in zip(here, left_half):
            pao[pairs + p] = contract(block, coeffs[p], 1, 1).astype(BF16)

    early = all_chunks // 2

    pl.semaphore_wait(barrier, jnp.where(at_end, 3, 2))

    @pl.when(jnp.logical_and(last_end, pair < n_pair - 1))
    def _():
        greet(ready, next_pair)

    raw = [
        remote(
            ints.at[rows(far * pairs + side * half + c * CHUNK)],
            via.at[side, rows(c * CHUNK), pl.ds(depth, depth)],
            raw_send.at[side, c],
            raw_recv.at[side, c],
            device,
        )
        for c in range(chunks)
        for side, device in ((0, to_down), (1, to_up))
    ]
    near = [
        remote(
            ints.at[rows(there * pairs + side * half + c * CHUNK)],
            own.at[rows(side * half + c * CHUNK), pl.ds(depth, depth)],
            near_send.at[side, c],
            near_recv.at[side, c],
            device,
        )
        for c in range(chunks)
        for side, device, there in ((0, to_up, up), (1, to_down, down))
    ]
    for copy in near[:2]:
        copy.start()

    targets = (
        (0, to_up, jnp.where(last_end, 3, 0)),
        (1, to_down, jnp.where(first_end, 3, 2)),
    )
    domain_halo = [
        remote(
            doms.at[rows(pairs, pairs)],
            doms.at[rows(part * pairs, pairs)],
            dom_send.at[side],
            dom_recv.at[part],
            device,
        )
        for side, device, part in targets
    ]
    domain_load.wait()
    for copy in domain_halo:
        copy.start()
    halo = [
        [
            remote(
                pao.at[rows(pairs + c * CHUNK)],
                pao.at[rows(part * pairs + c * CHUNK)],
                halo_send.at[side, c],
                halo_recv.at[part, c],
                device,
            )
            for side, device, part in targets
        ]
        for c in range(all_chunks)
    ]

    for c in range(all_chunks):
        to_pao(c)
        for copy in halo[c]:
            copy.start()

    def arrival(part, c):
        return remote(
            pao.at[rows(pairs + c * CHUNK)],
            pao.at[rows(part * pairs + c * CHUNK)],
            halo_send.at[0, c],
            halo_recv.at[part, c],
            to_up,
        )

    def domain_arrival(part):
        return remote(
            doms.at[rows(pairs, pairs)], doms.at[rows(part * pairs, pairs)], dom_send.at[0], dom_recv.at[part], to_up
        )

    pass_to = (jnp.where(first_end, next_pair[0], last_pair[0]), aux)
    pass_part = jnp.where(first_end, 0, 2)
    domain_pass = remote(
        doms.at[rows(3 * pairs, pairs)],
        doms.at[rows(pass_part * pairs, pairs)],
        pass_dom_send,
        dom_recv.at[pass_part],
        pass_to,
    )
    passed = [
        remote(
            pao.at[rows(3 * pairs + c * CHUNK)],
            pao.at[rows(pass_part * pairs + c * CHUNK)],
            pass_send.at[c],
            halo_recv.at[pass_part, c],
            pass_to,
        )
        for c in range(all_chunks)
    ]

    def halo_sent(c):
        for copy in halo[c]:
            copy.wait_send()

    def pass_on(c):
        @pl.when(at_end)
        def _():
            if c == 0:
                domain_arrival(3).wait_recv()
            arrival(3, c).wait_recv()

        if c == 0:

            @pl.when(jnp.logical_and(last_end, pair > 0))
            def _():
                pl.semaphore_wait(ready, 1)

        @pl.when(passes)
        def _():
            if c == 0:
                domain_pass.start()
            passed[c].start()

    def prepare(first, count):
        for p in range(first, first + count):
            energies = jnp.broadcast_to(pno[pl.ds(p, 1), :], (width, width))
            denominator = energies.T + energies + occ[p]
            inverse[p] = 1.0 / denominator
            block = own[p, pl.ds(0, depth), :]
            exchange = contract(block[:, :width], block[:, width:], 0, 0)
            acc[p] = exchange + denominator * amps[p].astype(F32)
            mine[p] = jnp.broadcast_to(doms[pl.ds(pairs + p, 1), :], (width, width)).T
            flipped[p] = coeffs[p].T

    sums = [
        remote(
            summed.at[side, rows(c * CHUNK)],
            arrived.at[rows(side * half + c * CHUNK)],
            summed_send.at[side, c],
            summed_recv.at[side, c],
            device,
        )
        for c in range(chunks)
        for side, device in ((0, to_down), (1, to_up))
    ]

    for copy in small_loads:
        copy.wait()
    own_load.wait()
    for c in range(all_chunks):
        prepare(c * CHUNK, CHUNK)
        halo_sent(c)
        if c == early - 1:
            for copy in raw:
                copy.start()
        if c == early:
            for copy in near[2:]:
                copy.start()
        pass_on(c)

    for copy in via_loads:
        copy.wait()
    for c in range(chunks):
        for side in (0, 1):
            raw[c * 2 + side].wait_recv()
            for p in range(c * CHUNK, c * CHUNK + CHUNK):
                block = via[side, p]
                summed[side, p] = contract(block[:, :width], block[:, width:], 0, 0).astype(BF16)
            sums[c * 2 + side].start()

    for part, none in ((0, no_left), (2, no_right)):

        @pl.when(jnp.logical_not(none))
        def _():
            domain_arrival(part).wait_recv()
            for c in range(all_chunks):
                arrival(part, c).wait_recv()

        @pl.when(none)
        def _():
            doms[pl.ds(part * pairs, pairs), :] = jnp.full((pairs, width), -1, jnp.int32)
            pao[pl.ds(part * pairs, pairs)] = jnp.zeros((pairs, width, width), BF16)

    first_row = ((pair * n_aux + aux) - 1) * pairs

    def couple(step, carry):
        here = [step * TOGETHER + i for i in range(TOGETHER)]
        totals = []
        for p in here:
            column = mine[p]
            matches, scaled = [], []
            for k in range(slots):
                row = jnp.clip(neighbours[k, p] - first_row, 0, 3 * pairs - 1)
                weight = jnp.where(k < counts[p], couplings[k, p], 0.0)
                match = jnp.where(column == doms[pl.ds(row, 1), :], 1.0, 0.0).astype(BF16)
                picked = contract(match, pao[row], 1, 0)
                matches.append(match)
                scaled.append((weight * picked).astype(BF16))
            total = contract(jnp.concatenate(scaled, axis=1), jnp.concatenate(matches, axis=1), 1, 1)
            totals.append(total.astype(BF16))
        halves = [contract(total, coeffs[p], 1, 0).astype(BF16) for p, total in zip(here, totals)]
        for p, right_half in zip(here, halves):
            acc[p] += contract(flipped[p], right_half, 1, 0)
        return carry

    lax.fori_loop(0, pairs // TOGETHER, couple, 0)

    for c in range(chunks):
        for side in (0, 1):
            near[c * 2 + side].wait_recv()
            first = side * half + c * CHUNK
            for p in range(first, first + CHUNK):
                block = own[p, pl.ds(depth, depth), :]
                acc[p] += contract(block[:, :width], block[:, width:], 0, 0)
    for c in range(chunks):
        for side in (0, 1):
            sums[c * 2 + side].wait_recv()
            first = side * half + c * CHUNK
            for p in range(first, first + CHUNK):
                result = acc[p] + arrived[p].astype(F32)
                residual[p] = result
                updated[p] = (amps[p].astype(F32) - result * inverse[p]).astype(BF16)

    for copy in raw + near + sums + domain_halo:
        copy.wait_send()

    @pl.when(passes)
    def _():
        for copy in [domain_pass] + passed:
            copy.wait_send()


def hand_over(residual_in, updated_in, residual, updated, sems):
    copies = [
        pltpu.make_async_copy(residual_in, residual, sems.at[0]),
        pltpu.make_async_copy(updated_in, updated, sems.at[1]),
    ]
    for copy in copies:
        copy.start()
    for copy in copies:
        copy.wait()


def per_device(
    integrals,
    amplitudes,
    coeffs,
    domains,
    neighbours,
    counts,
    couplings,
    pno_energies,
    occ_energies,
):
    pairs, width, _ = amplitudes.shape
    depth = integrals.shape[1]
    half = pairs // 2
    chunks = half // CHUNK
    in_hbm = pl.BlockSpec(memory_space=pltpu.HBM)
    in_vmem = pl.BlockSpec(memory_space=pltpu.VMEM)
    dma = pltpu.SemaphoreType.DMA
    operands = (
        integrals, amplitudes, coeffs, domains, neighbours.T, counts, couplings.T, pno_energies, occ_energies,
    )
    residual, updated = pl.pallas_call(
        kernel,
        out_shape=(
            pltpu.VMEM((pairs, width, width), F32),
            pltpu.VMEM((pairs, width, width), BF16),
        ),
        in_specs=[in_hbm] * len(operands),
        out_specs=(in_vmem, in_vmem),
        scratch_shapes=[
            pltpu.VMEM((pairs, width, width), BF16),
            pltpu.VMEM((pairs, width, width), BF16),
            pltpu.VMEM((4 * pairs, width, width), BF16),
            pltpu.VMEM((4 * pairs, width), jnp.int32),
            pltpu.SMEM(neighbours.shape[::-1], jnp.int32),
            pltpu.SMEM(counts.shape, jnp.int32),
            pltpu.SMEM(couplings.shape[::-1], F32),
            pltpu.VMEM(pno_energies.shape, F32),
            pltpu.SMEM(occ_energies.shape, F32),
            pltpu.VMEM((pairs, 2 * depth, 2 * width), BF16),
            pltpu.VMEM((2, half, 2 * depth, 2 * width), BF16),
            pltpu.VMEM((2, half, width, width), BF16),
            pltpu.VMEM((pairs, width, width), BF16),
            pltpu.VMEM((pairs, width, width), F32),
            pltpu.VMEM((pairs, width, width), F32),
            pltpu.VMEM((pairs, width, width), jnp.int32),
            pltpu.VMEM((pairs, width, width), BF16),
            dma((2 * chunks,)),
            dma((2 * chunks,)),
            dma((6,)),
            dma(()),
            dma((2,)),
            dma((2, chunks)),
            dma((2, chunks)),
            dma((2, chunks)),
            dma((2, chunks)),
            dma((2, chunks)),
            dma((2, chunks)),
            dma((2, 2 * chunks)),
            dma((4, 2 * chunks)),
            dma((2,)),
            dma((4,)),
            dma((2 * chunks,)),
            dma(()),
            pltpu.SemaphoreType.REGULAR,
        ],
        compiler_params=pltpu.CompilerParams(
            collective_id=0, has_side_effects=True, vmem_limit_bytes=32 * 1024 * 1024
        ),
        name="doubles_residual",
    )(*(pltpu.with_memory_space_constraint(operand, pltpu.HBM) for operand in operands))
    return pl.pallas_call(
        hand_over,
        out_shape=(
            jax.ShapeDtypeStruct((pairs, width, width), F32),
            jax.ShapeDtypeStruct((pairs, width, width), BF16),
        ),
        in_specs=(in_vmem, in_vmem),
        out_specs=(in_hbm, in_hbm),
        scratch_shapes=[dma((2,))],
        compiler_params=pltpu.CompilerParams(vmem_limit_bytes=16 * 1024 * 1024),
        name="hand_over",
    )(residual, updated)


def solution(mesh):
    in_specs = (
        P("pair", "aux", None),
        P(("pair", "aux"), None, None),
        P(("pair", "aux"), None, None),
        P(("pair", "aux"), None),
        P(("pair", "aux"), None),
        P(("pair", "aux")),
        P(("pair", "aux"), None),
        P(("pair", "aux"), None),
        P(("pair", "aux")),
    )
    out_specs = (P(("pair", "aux"), None, None), P(("pair", "aux"), None, None))
    return jax.shard_map(
        per_device, mesh=mesh, in_specs=in_specs, out_specs=out_specs, check_vma=False
    )
```

```python
import jax
import jax.numpy as jnp
from jax import lax
from jax.experimental import pallas as pl
from jax.experimental.pallas import tpu as pltpu
from jax.sharding import PartitionSpec as P

MESH = pl.DeviceIdType.MESH
F32 = jnp.float32
BF16 = jnp.bfloat16
CHUNK = 4
TOGETHER = 8


def contract(a, b, dim_a, dim_b):
    return lax.dot_general(a, b, (((dim_a,), (dim_b,)), ((), ())), preferred_element_type=F32)


def kernel(
    ints, amps_in, coeffs_in, domains_in, neighbours_in, counts_in, couplings_in, pno_in, occ_in,
    residual, updated,
    amps, coeffs, pao, doms, neighbours, counts, couplings, pno, occ, own, via, summed, arrived,
    acc, inverse, mine, flipped,
    amps_sem, coeffs_sem, load_sem, own_sem, via_sem, raw_send, raw_recv, near_send, near_recv,
    summed_send, summed_recv, halo_send, halo_recv, dom_send, dom_recv, pass_send, pass_dom_send, ready,
):
    n_pair, n_aux = lax.axis_size("pair"), lax.axis_size("aux")
    pair, aux = lax.axis_index("pair"), lax.axis_index("aux")
    pairs = amps.shape[0]
    half = pairs // 2
    depth = ints.shape[1]
    width = amps.shape[1]
    slots = neighbours.shape[0]
    chunks = half // CHUNK
    all_chunks = pairs // CHUNK

    up, down, far = (aux + 1) % n_aux, (aux + n_aux - 1) % n_aux, (aux + 2) % n_aux
    to_up, to_down = (pair, up), (pair, down)
    next_pair, last_pair = ((pair + 1) % n_pair, aux), ((pair + n_pair - 1) % n_pair, aux)
    first_end, last_end = aux == 0, aux == n_aux - 1
    at_end = jnp.logical_or(first_end, last_end)
    no_left = jnp.logical_and(first_end, pair == 0)
    no_right = jnp.logical_and(last_end, pair == n_pair - 1)
    passes = jnp.logical_or(
        jnp.logical_and(first_end, pair < n_pair - 1), jnp.logical_and(last_end, pair > 0)
    )

    barrier = pltpu.get_barrier_semaphore()

    def greet(semaphore, device):
        pl.semaphore_signal(semaphore, inc=1, device_id=device, device_id_type=MESH)

    greet(barrier, to_up)
    greet(barrier, to_down)

    @pl.when(at_end)
    def _():
        greet(barrier, last_pair)

    def remote(src, dst, send, recv, device):
        return pltpu.make_async_remote_copy(
            src_ref=src, dst_ref=dst, send_sem=send, recv_sem=recv, device_id=device, device_id_type=MESH
        )

    def rows(first, count=CHUNK):
        return pl.ds(first, count)

    matrix_loads = []
    for c in range(all_chunks):
        part = rows(c * CHUNK)
        matrix_loads.append(
            [
                pltpu.make_async_copy(coeffs_in.at[part], coeffs.at[part], coeffs_sem.at[c]),
                pltpu.make_async_copy(amps_in.at[part], amps.at[part], amps_sem.at[c]),
            ]
        )
    domain_load = pltpu.make_async_copy(domains_in, doms.at[rows(pairs, pairs)], load_sem.at[0])
    small_loads = [
        pltpu.make_async_copy(neighbours_in, neighbours, load_sem.at[1]),
        pltpu.make_async_copy(counts_in, counts, load_sem.at[2]),
        pltpu.make_async_copy(couplings_in, couplings, load_sem.at[3]),
        pltpu.make_async_copy(pno_in, pno, load_sem.at[4]),
        pltpu.make_async_copy(occ_in, occ, load_sem.at[5]),
    ]
    via_loads = [
        pltpu.make_async_copy(
            ints.at[rows(down * pairs, half)], via.at[0, :, pl.ds(0, depth)], via_sem.at[0]
        ),
        pltpu.make_async_copy(
            ints.at[rows(up * pairs + half, half)], via.at[1, :, pl.ds(0, depth)], via_sem.at[1]
        ),
    ]
    own_load = pltpu.make_async_copy(ints.at[rows(aux * pairs, pairs)], own.at[:, pl.ds(0, depth)], own_sem)
    for copy in sum(matrix_loads, []) + [domain_load] + small_loads + [own_load] + via_loads:
        copy.start()

    def to_pao(c):
        for copy in matrix_loads[c]:
            copy.wait()
        here = [c * CHUNK + i for i in range(CHUNK)]
        left_half = [contract(coeffs[p], amps[p], 1, 0).astype(BF16) for p in here]
        for p, block in zip(here, left_half):
            pao[pairs + p] = contract(block, coeffs[p], 1, 1).astype(BF16)

    early = all_chunks // 2

    pl.semaphore_wait(barrier, jnp.where(at_end, 3, 2))

    @pl.when(jnp.logical_and(last_end, pair < n_pair - 1))
    def _():
        greet(ready, next_pair)

    raw = [
        remote(
            ints.at[rows(far * pairs + side * half + c * CHUNK)],
            via.at[side, rows(c * CHUNK), pl.ds(depth, depth)],
            raw_send.at[side, c],
            raw_recv.at[side, c],
            device,
        )
        for c in range(chunks)
        for side, device in ((0, to_down), (1, to_up))
    ]
    near = [
        remote(
            ints.at[rows(there * pairs + side * half + c * CHUNK)],
            own.at[rows(side * half + c * CHUNK), pl.ds(depth, depth)],
            near_send.at[side, c],
            near_recv.at[side, c],
            device,
        )
        for c in range(chunks)
        for side, device, there in ((0, to_up, up), (1, to_down, down))
    ]
    for copy in near[:2]:
        copy.start()

    targets = (
        (0, to_up, jnp.where(last_end, 3, 0)),
        (1, to_down, jnp.where(first_end, 3, 2)),
    )
    domain_halo = [
        remote(
            doms.at[rows(pairs, pairs)],
            doms.at[rows(part * pairs, pairs)],
            dom_send.at[side],
            dom_recv.at[part],
            device,
        )
        for side, device, part in targets
    ]
    domain_load.wait()
    for copy in domain_halo:
        copy.start()
    halo = [
        [
            remote(
                pao.at[rows(pairs + c * CHUNK)],
                pao.at[rows(part * pairs + c * CHUNK)],
                halo_send.at[side, c],
                halo_recv.at[part, c],
                device,
            )
            for side, device, part in targets
        ]
        for c in range(all_chunks)
    ]

    for c in range(all_chunks):
        to_pao(c)
        for copy in halo[c]:
            copy.start()

    def arrival(part, c):
        return remote(
            pao.at[rows(pairs + c * CHUNK)],
            pao.at[rows(part * pairs + c * CHUNK)],
            halo_send.at[0, c],
            halo_recv.at[part, c],
            to_up,
        )

    def domain_arrival(part):
        return remote(
            doms.at[rows(pairs, pairs)], doms.at[rows(part * pairs, pairs)], dom_send.at[0], dom_recv.at[part], to_up
        )

    pass_to = (jnp.where(first_end, next_pair[0], last_pair[0]), aux)
    pass_part = jnp.where(first_end, 0, 2)
    domain_pass = remote(
        doms.at[rows(3 * pairs, pairs)],
        doms.at[rows(pass_part * pairs, pairs)],
        pass_dom_send,
        dom_recv.at[pass_part],
        pass_to,
    )
    passed = [
        remote(
            pao.at[rows(3 * pairs + c * CHUNK)],
            pao.at[rows(pass_part * pairs + c * CHUNK)],
            pass_send.at[c],
            halo_recv.at[pass_part, c],
            pass_to,
        )
        for c in range(all_chunks)
    ]

    def halo_sent(c):
        for copy in halo[c]:
            copy.wait_send()

    def pass_on(c):
        @pl.when(at_end)
        def _():
            if c == 0:
                domain_arrival(3).wait_recv()
            arrival(3, c).wait_recv()

        if c == 0:

            @pl.when(jnp.logical_and(last_end, pair > 0))
            def _():
                pl.semaphore_wait(ready, 1)

        @pl.when(passes)
        def _():
            if c == 0:
                domain_pass.start()
            passed[c].start()

    def prepare(first, count):
        for p in range(first, first + count):
            energies = jnp.broadcast_to(pno[pl.ds(p, 1), :], (width, width))
            denominator = energies.T + energies + occ[p]
            inverse[p] = 1.0 / denominator
            block = own[p, pl.ds(0, depth), :]
            exchange = contract(block[:, :width], block[:, width:], 0, 0)
            acc[p] = exchange + denominator * amps[p].astype(F32)
            mine[p] = jnp.broadcast_to(doms[pl.ds(pairs + p, 1), :], (width, width)).T
            flipped[p] = coeffs[p].T

    sums = [
        remote(
            summed.at[side, rows(c * CHUNK)],
            arrived.at[rows(side * half + c * CHUNK)],
            summed_send.at[side, c],
            summed_recv.at[side, c],
            device,
        )
        for c in range(chunks)
        for side, device in ((0, to_down), (1, to_up))
    ]

    for copy in small_loads:
        copy.wait()
    own_load.wait()
    for c in range(all_chunks):
        prepare(c * CHUNK, CHUNK)
        halo_sent(c)
        if c == 0:
            for copy in raw:
                copy.start()
        if c == early:
            for copy in near[2:]:
                copy.start()
        pass_on(c)

    for copy in via_loads:
        copy.wait()
    for c in range(chunks):
        for side in (0, 1):
            raw[c * 2 + side].wait_recv()
            for p in range(c * CHUNK, c * CHUNK + CHUNK):
                block = via[side, p]
                summed[side, p] = contract(block[:, :width], block[:, width:], 0, 0).astype(BF16)
            sums[c * 2 + side].start()

    def add_near(c):
        for side in (0, 1):
            near[c * 2 + side].wait_recv()
            first = side * half + c * CHUNK
            for p in range(first, first + CHUNK):
                block = own[p, pl.ds(depth, depth), :]
                acc[p] += contract(block[:, :width], block[:, width:], 0, 0)

    add_near(0)

    for part, none in ((0, no_left), (2, no_right)):

        @pl.when(jnp.logical_not(none))
        def _():
            domain_arrival(part).wait_recv()
            for c in range(all_chunks):
                arrival(part, c).wait_recv()

        @pl.when(none)
        def _():
            doms[pl.ds(part * pairs, pairs), :] = jnp.full((pairs, width), -1, jnp.int32)
            pao[pl.ds(part * pairs, pairs)] = jnp.zeros((pairs, width, width), BF16)

    first_row = ((pair * n_aux + aux) - 1) * pairs

    def couple(step, carry):
        here = [step * TOGETHER + i for i in range(TOGETHER)]
        totals = []
        for p in here:
            column = mine[p]
            matches, scaled = [], []
            for k in range(slots):
                row = jnp.clip(neighbours[k, p] - first_row, 0, 3 * pairs - 1)
                weight = jnp.where(k < counts[p], couplings[k, p], 0.0)
                match = jnp.where(column == doms[pl.ds(row, 1), :], 1.0, 0.0).astype(BF16)
                picked = contract(match, pao[row], 1, 0)
                matches.append(match)
                scaled.append((weight * picked).astype(BF16))
            total = contract(jnp.concatenate(scaled, axis=1), jnp.concatenate(matches, axis=1), 1, 1)
            totals.append(total.astype(BF16))
        halves = [contract(total, coeffs[p], 1, 0).astype(BF16) for p, total in zip(here, totals)]
        for p, right_half in zip(here, halves):
            acc[p] += contract(flipped[p], right_half, 1, 0)
        return carry

    lax.fori_loop(0, pairs // TOGETHER, couple, 0)

    for c in range(1, chunks):
        add_near(c)
    for c in range(chunks):
        for side in (0, 1):
            sums[c * 2 + side].wait_recv()
            first = side * half + c * CHUNK
            for p in range(first, first + CHUNK):
                result = acc[p] + arrived[p].astype(F32)
                residual[p] = result
                updated[p] = (amps[p].astype(F32) - result * inverse[p]).astype(BF16)

    for copy in raw + near + sums + domain_halo:
        copy.wait_send()

    @pl.when(passes)
    def _():
        for copy in [domain_pass] + passed:
            copy.wait_send()


def hand_over(residual_in, updated_in, residual, updated, sems):
    copies = [
        pltpu.make_async_copy(residual_in, residual, sems.at[0]),
        pltpu.make_async_copy(updated_in, updated, sems.at[1]),
    ]
    for copy in copies:
        copy.start()
    for copy in copies:
        copy.wait()


def per_device(
    integrals,
    amplitudes,
    coeffs,
    domains,
    neighbours,
    counts,
    couplings,
    pno_energies,
    occ_energies,
):
    pairs, width, _ = amplitudes.shape
    depth = integrals.shape[1]
    half = pairs // 2
    chunks = half // CHUNK
    in_hbm = pl.BlockSpec(memory_space=pltpu.HBM)
    in_vmem = pl.BlockSpec(memory_space=pltpu.VMEM)
    dma = pltpu.SemaphoreType.DMA
    operands = (
        integrals, amplitudes, coeffs, domains, neighbours.T, counts, couplings.T, pno_energies, occ_energies,
    )
    residual, updated = pl.pallas_call(
        kernel,
        out_shape=(
            pltpu.VMEM((pairs, width, width), F32),
            pltpu.VMEM((pairs, width, width), BF16),
        ),
        in_specs=[in_hbm] * len(operands),
        out_specs=(in_vmem, in_vmem),
        scratch_shapes=[
            pltpu.VMEM((pairs, width, width), BF16),
            pltpu.VMEM((pairs, width, width), BF16),
            pltpu.VMEM((4 * pairs, width, width), BF16),
            pltpu.VMEM((4 * pairs, width), jnp.int32),
            pltpu.SMEM(neighbours.shape[::-1], jnp.int32),
            pltpu.SMEM(counts.shape, jnp.int32),
            pltpu.SMEM(couplings.shape[::-1], F32),
            pltpu.VMEM(pno_energies.shape, F32),
            pltpu.SMEM(occ_energies.shape, F32),
            pltpu.VMEM((pairs, 2 * depth, 2 * width), BF16),
            pltpu.VMEM((2, half, 2 * depth, 2 * width), BF16),
            pltpu.VMEM((2, half, width, width), BF16),
            pltpu.VMEM((pairs, width, width), BF16),
            pltpu.VMEM((pairs, width, width), F32),
            pltpu.VMEM((pairs, width, width), F32),
            pltpu.VMEM((pairs, width, width), jnp.int32),
            pltpu.VMEM((pairs, width, width), BF16),
            dma((2 * chunks,)),
            dma((2 * chunks,)),
            dma((6,)),
            dma(()),
            dma((2,)),
            dma((2, chunks)),
            dma((2, chunks)),
            dma((2, chunks)),
            dma((2, chunks)),
            dma((2, chunks)),
            dma((2, chunks)),
            dma((2, 2 * chunks)),
            dma((4, 2 * chunks)),
            dma((2,)),
            dma((4,)),
            dma((2 * chunks,)),
            dma(()),
            pltpu.SemaphoreType.REGULAR,
        ],
        compiler_params=pltpu.CompilerParams(
            collective_id=0, has_side_effects=True, vmem_limit_bytes=32 * 1024 * 1024
        ),
        name="doubles_residual",
    )(*(pltpu.with_memory_space_constraint(operand, pltpu.HBM) for operand in operands))
    return pl.pallas_call(
        hand_over,
        out_shape=(
            jax.ShapeDtypeStruct((pairs, width, width), F32),
            jax.ShapeDtypeStruct((pairs, width, width), BF16),
        ),
        in_specs=(in_vmem, in_vmem),
        out_specs=(in_hbm, in_hbm),
        scratch_shapes=[dma((2,))],
        compiler_params=pltpu.CompilerParams(vmem_limit_bytes=16 * 1024 * 1024),
        name="hand_over",
    )(residual, updated)


def solution(mesh):
    in_specs = (
        P("pair", "aux", None),
        P(("pair", "aux"), None, None),
        P(("pair", "aux"), None, None),
        P(("pair", "aux"), None),
        P(("pair", "aux"), None),
        P(("pair", "aux")),
        P(("pair", "aux"), None),
        P(("pair", "aux"), None),
        P(("pair", "aux")),
    )
    out_specs = (P(("pair", "aux"), None, None), P(("pair", "aux"), None, None))
    return jax.shard_map(
        per_device, mesh=mesh, in_specs=in_specs, out_specs=out_specs, check_vma=False
    )
```

```python
import jax
import jax.numpy as jnp
from jax import lax
from jax.experimental import pallas as pl
from jax.experimental.pallas import tpu as pltpu
from jax.sharding import PartitionSpec as P

MESH = pl.DeviceIdType.MESH
F32 = jnp.float32
BF16 = jnp.bfloat16
CHUNK = 2
TOGETHER = 8


def contract(a, b, dim_a, dim_b):
    return lax.dot_general(a, b, (((dim_a,), (dim_b,)), ((), ())), preferred_element_type=F32)


def kernel(
    ints, amps_in, coeffs_in, domains_in, neighbours_in, counts_in, couplings_in, pno_in, occ_in,
    residual, updated,
    amps, coeffs, pao, doms, neighbours, counts, couplings, pno, occ, own, via, summed, arrived,
    acc, inverse, mine, flipped,
    amps_sem, coeffs_sem, load_sem, own_sem, via_sem, raw_send, raw_recv, near_send, near_recv,
    summed_send, summed_recv, halo_send, halo_recv, dom_send, dom_recv, pass_send, pass_dom_send, ready,
):
    n_pair, n_aux = lax.axis_size("pair"), lax.axis_size("aux")
    pair, aux = lax.axis_index("pair"), lax.axis_index("aux")
    pairs = amps.shape[0]
    half = pairs // 2
    depth = ints.shape[1]
    width = amps.shape[1]
    slots = neighbours.shape[0]
    chunks = half // CHUNK
    all_chunks = pairs // CHUNK

    up, down, far = (aux + 1) % n_aux, (aux + n_aux - 1) % n_aux, (aux + 2) % n_aux
    to_up, to_down = (pair, up), (pair, down)
    next_pair, last_pair = ((pair + 1) % n_pair, aux), ((pair + n_pair - 1) % n_pair, aux)
    first_end, last_end = aux == 0, aux == n_aux - 1
    at_end = jnp.logical_or(first_end, last_end)
    no_left = jnp.logical_and(first_end, pair == 0)
    no_right = jnp.logical_and(last_end, pair == n_pair - 1)
    passes = jnp.logical_or(
        jnp.logical_and(first_end, pair < n_pair - 1), jnp.logical_and(last_end, pair > 0)
    )

    barrier = pltpu.get_barrier_semaphore()

    def greet(semaphore, device):
        pl.semaphore_signal(semaphore, inc=1, device_id=device, device_id_type=MESH)

    greet(barrier, to_up)
    greet(barrier, to_down)

    @pl.when(at_end)
    def _():
        greet(barrier, last_pair)

    def remote(src, dst, send, recv, device):
        return pltpu.make_async_remote_copy(
            src_ref=src, dst_ref=dst, send_sem=send, recv_sem=recv, device_id=device, device_id_type=MESH
        )

    def rows(first, count=CHUNK):
        return pl.ds(first, count)

    matrix_loads = []
    for c in range(all_chunks):
        part = rows(c * CHUNK)
        matrix_loads.append(
            [
                pltpu.make_async_copy(coeffs_in.at[part], coeffs.at[part], coeffs_sem.at[c]),
                pltpu.make_async_copy(amps_in.at[part], amps.at[part], amps_sem.at[c]),
            ]
        )
    domain_load = pltpu.make_async_copy(domains_in, doms.at[rows(pairs, pairs)], load_sem.at[0])
    small_loads = [
        pltpu.make_async_copy(neighbours_in, neighbours, load_sem.at[1]),
        pltpu.make_async_copy(counts_in, counts, load_sem.at[2]),
        pltpu.make_async_copy(couplings_in, couplings, load_sem.at[3]),
        pltpu.make_async_copy(pno_in, pno, load_sem.at[4]),
        pltpu.make_async_copy(occ_in, occ, load_sem.at[5]),
    ]
    via_loads = [
        pltpu.make_async_copy(
            ints.at[rows(down * pairs, half)], via.at[0, :, pl.ds(0, depth)], via_sem.at[0]
        ),
        pltpu.make_async_copy(
            ints.at[rows(up * pairs + half, half)], via.at[1, :, pl.ds(0, depth)], via_sem.at[1]
        ),
    ]
    own_load = pltpu.make_async_copy(ints.at[rows(aux * pairs, pairs)], own.at[:, pl.ds(0, depth)], own_sem)
    for copy in sum(matrix_loads, []) + [domain_load] + small_loads + [own_load] + via_loads:
        copy.start()

    def to_pao(c):
        for copy in matrix_loads[c]:
            copy.wait()
        here = [c * CHUNK + i for i in range(CHUNK)]
        left_half = [contract(coeffs[p], amps[p], 1, 0).astype(BF16) for p in here]
        for p, block in zip(here, left_half):
            pao[pairs + p] = contract(block, coeffs[p], 1, 1).astype(BF16)

    early = all_chunks // 2

    pl.semaphore_wait(barrier, jnp.where(at_end, 3, 2))

    @pl.when(jnp.logical_and(last_end, pair < n_pair - 1))
    def _():
        greet(ready, next_pair)

    raw = [
        remote(
            ints.at[rows(far * pairs + side * half + c * CHUNK)],
            via.at[side, rows(c * CHUNK), pl.ds(depth, depth)],
            raw_send.at[side, c],
            raw_recv.at[side, c],
            device,
        )
        for c in range(chunks)
        for side, device in ((0, to_down), (1, to_up))
    ]
    near = [
        remote(
            ints.at[rows(there * pairs + side * half + c * CHUNK)],
            own.at[rows(side * half + c * CHUNK), pl.ds(depth, depth)],
            near_send.at[side, c],
            near_recv.at[side, c],
            device,
        )
        for c in range(chunks)
        for side, device, there in ((0, to_up, up), (1, to_down, down))
    ]
    for copy in near[:2]:
        copy.start()

    targets = (
        (0, to_up, jnp.where(last_end, 3, 0)),
        (1, to_down, jnp.where(first_end, 3, 2)),
    )
    domain_halo = [
        remote(
            doms.at[rows(pairs, pairs)],
            doms.at[rows(part * pairs, pairs)],
            dom_send.at[side],
            dom_recv.at[part],
            device,
        )
        for side, device, part in targets
    ]
    domain_load.wait()
    for copy in domain_halo:
        copy.start()
    halo = [
        [
            remote(
                pao.at[rows(pairs + c * CHUNK)],
                pao.at[rows(part * pairs + c * CHUNK)],
                halo_send.at[side, c],
                halo_recv.at[part, c],
                device,
            )
            for side, device, part in targets
        ]
        for c in range(all_chunks)
    ]

    for c in range(all_chunks):
        to_pao(c)
        for copy in halo[c]:
            copy.start()

    def arrival(part, c):
        return remote(
            pao.at[rows(pairs + c * CHUNK)],
            pao.at[rows(part * pairs + c * CHUNK)],
            halo_send.at[0, c],
            halo_recv.at[part, c],
            to_up,
        )

    def domain_arrival(part):
        return remote(
            doms.at[rows(pairs, pairs)], doms.at[rows(part * pairs, pairs)], dom_send.at[0], dom_recv.at[part], to_up
        )

    pass_to = (jnp.where(first_end, next_pair[0], last_pair[0]), aux)
    pass_part = jnp.where(first_end, 0, 2)
    domain_pass = remote(
        doms.at[rows(3 * pairs, pairs)],
        doms.at[rows(pass_part * pairs, pairs)],
        pass_dom_send,
        dom_recv.at[pass_part],
        pass_to,
    )
    passed = [
        remote(
            pao.at[rows(3 * pairs + c * CHUNK)],
            pao.at[rows(pass_part * pairs + c * CHUNK)],
            pass_send.at[c],
            halo_recv.at[pass_part, c],
            pass_to,
        )
        for c in range(all_chunks)
    ]

    def halo_sent(c):
        for copy in halo[c]:
            copy.wait_send()

    def pass_on(c):
        @pl.when(at_end)
        def _():
            if c == 0:
                domain_arrival(3).wait_recv()
            arrival(3, c).wait_recv()

        if c == 0:

            @pl.when(jnp.logical_and(last_end, pair > 0))
            def _():
                pl.semaphore_wait(ready, 1)

        @pl.when(passes)
        def _():
            if c == 0:
                domain_pass.start()
            passed[c].start()

    def prepare(first, count):
        for p in range(first, first + count):
            energies = jnp.broadcast_to(pno[pl.ds(p, 1), :], (width, width))
            denominator = energies.T + energies + occ[p]
            inverse[p] = 1.0 / denominator
            block = own[p, pl.ds(0, depth), :]
            exchange = contract(block[:, :width], block[:, width:], 0, 0)
            acc[p] = exchange + denominator * amps[p].astype(F32)
            mine[p] = jnp.broadcast_to(doms[pl.ds(pairs + p, 1), :], (width, width)).T
            flipped[p] = coeffs[p].T

    sums = [
        remote(
            summed.at[side, rows(c * CHUNK)],
            arrived.at[rows(side * half + c * CHUNK)],
            summed_send.at[side, c],
            summed_recv.at[side, c],
            device,
        )
        for c in range(chunks)
        for side, device in ((0, to_down), (1, to_up))
    ]

    for copy in small_loads:
        copy.wait()
    own_load.wait()
    for c in range(all_chunks):
        prepare(c * CHUNK, CHUNK)
        halo_sent(c)
        if c == 0:
            for copy in raw:
                copy.start()
        if c == early:
            for copy in near[2:]:
                copy.start()
        pass_on(c)

    for copy in via_loads:
        copy.wait()
    for c in range(chunks):
        for side in (0, 1):
            raw[c * 2 + side].wait_recv()
            for p in range(c * CHUNK, c * CHUNK + CHUNK):
                block = via[side, p]
                summed[side, p] = contract(block[:, :width], block[:, width:], 0, 0).astype(BF16)
            sums[c * 2 + side].start()

    def add_near(c):
        for side in (0, 1):
            near[c * 2 + side].wait_recv()
            first = side * half + c * CHUNK
            for p in range(first, first + CHUNK):
                block = own[p, pl.ds(depth, depth), :]
                acc[p] += contract(block[:, :width], block[:, width:], 0, 0)

    add_near(0)

    for part, none in ((0, no_left), (2, no_right)):

        @pl.when(jnp.logical_not(none))
        def _():
            domain_arrival(part).wait_recv()
            for c in range(all_chunks):
                arrival(part, c).wait_recv()

        @pl.when(none)
        def _():
            doms[pl.ds(part * pairs, pairs), :] = jnp.full((pairs, width), -1, jnp.int32)
            pao[pl.ds(part * pairs, pairs)] = jnp.zeros((pairs, width, width), BF16)

    first_row = ((pair * n_aux + aux) - 1) * pairs

    def couple(step, carry):
        here = [step * TOGETHER + i for i in range(TOGETHER)]
        totals = []
        for p in here:
            column = mine[p]
            matches, scaled = [], []
            for k in range(slots):
                row = jnp.clip(neighbours[k, p] - first_row, 0, 3 * pairs - 1)
                weight = jnp.where(k < counts[p], couplings[k, p], 0.0)
                match = jnp.where(column == doms[pl.ds(row, 1), :], 1.0, 0.0).astype(BF16)
                picked = contract(match, pao[row], 1, 0)
                matches.append(match)
                scaled.append((weight * picked).astype(BF16))
            total = contract(jnp.concatenate(scaled, axis=1), jnp.concatenate(matches, axis=1), 1, 1)
            totals.append(total.astype(BF16))
        halves = [contract(total, coeffs[p], 1, 0).astype(BF16) for p, total in zip(here, totals)]
        for p, right_half in zip(here, halves):
            acc[p] += contract(flipped[p], right_half, 1, 0)
        return carry

    lax.fori_loop(0, pairs // TOGETHER, couple, 0)

    for c in range(1, chunks):
        add_near(c)
    for c in range(chunks):
        for side in (0, 1):
            sums[c * 2 + side].wait_recv()
            first = side * half + c * CHUNK
            for p in range(first, first + CHUNK):
                result = acc[p] + arrived[p].astype(F32)
                residual[p] = result
                updated[p] = (amps[p].astype(F32) - result * inverse[p]).astype(BF16)

    for copy in raw + near + sums + domain_halo:
        copy.wait_send()

    @pl.when(passes)
    def _():
        for copy in [domain_pass] + passed:
            copy.wait_send()


def hand_over(residual_in, updated_in, residual, updated, sems):
    copies = [
        pltpu.make_async_copy(residual_in, residual, sems.at[0]),
        pltpu.make_async_copy(updated_in, updated, sems.at[1]),
    ]
    for copy in copies:
        copy.start()
    for copy in copies:
        copy.wait()


def per_device(
    integrals,
    amplitudes,
    coeffs,
    domains,
    neighbours,
    counts,
    couplings,
    pno_energies,
    occ_energies,
):
    pairs, width, _ = amplitudes.shape
    depth = integrals.shape[1]
    half = pairs // 2
    chunks = half // CHUNK
    in_hbm = pl.BlockSpec(memory_space=pltpu.HBM)
    in_vmem = pl.BlockSpec(memory_space=pltpu.VMEM)
    dma = pltpu.SemaphoreType.DMA
    operands = (
        integrals, amplitudes, coeffs, domains, neighbours.T, counts, couplings.T, pno_energies, occ_energies,
    )
    residual, updated = pl.pallas_call(
        kernel,
        out_shape=(
            pltpu.VMEM((pairs, width, width), F32),
            pltpu.VMEM((pairs, width, width), BF16),
        ),
        in_specs=[in_hbm] * len(operands),
        out_specs=(in_vmem, in_vmem),
        scratch_shapes=[
            pltpu.VMEM((pairs, width, width), BF16),
            pltpu.VMEM((pairs, width, width), BF16),
            pltpu.VMEM((4 * pairs, width, width), BF16),
            pltpu.VMEM((4 * pairs, width), jnp.int32),
            pltpu.SMEM(neighbours.shape[::-1], jnp.int32),
            pltpu.SMEM(counts.shape, jnp.int32),
            pltpu.SMEM(couplings.shape[::-1], F32),
            pltpu.VMEM(pno_energies.shape, F32),
            pltpu.SMEM(occ_energies.shape, F32),
            pltpu.VMEM((pairs, 2 * depth, 2 * width), BF16),
            pltpu.VMEM((2, half, 2 * depth, 2 * width), BF16),
            pltpu.VMEM((2, half, width, width), BF16),
            pltpu.VMEM((pairs, width, width), BF16),
            pltpu.VMEM((pairs, width, width), F32),
            pltpu.VMEM((pairs, width, width), F32),
            pltpu.VMEM((pairs, width, width), jnp.int32),
            pltpu.VMEM((pairs, width, width), BF16),
            dma((2 * chunks,)),
            dma((2 * chunks,)),
            dma((6,)),
            dma(()),
            dma((2,)),
            dma((2, chunks)),
            dma((2, chunks)),
            dma((2, chunks)),
            dma((2, chunks)),
            dma((2, chunks)),
            dma((2, chunks)),
            dma((2, 2 * chunks)),
            dma((4, 2 * chunks)),
            dma((2,)),
            dma((4,)),
            dma((2 * chunks,)),
            dma(()),
            pltpu.SemaphoreType.REGULAR,
        ],
        compiler_params=pltpu.CompilerParams(
            collective_id=0, has_side_effects=True, vmem_limit_bytes=32 * 1024 * 1024
        ),
        name="doubles_residual",
    )(*(pltpu.with_memory_space_constraint(operand, pltpu.HBM) for operand in operands))
    return pl.pallas_call(
        hand_over,
        out_shape=(
            jax.ShapeDtypeStruct((pairs, width, width), F32),
            jax.ShapeDtypeStruct((pairs, width, width), BF16),
        ),
        in_specs=(in_vmem, in_vmem),
        out_specs=(in_hbm, in_hbm),
        scratch_shapes=[dma((2,))],
        compiler_params=pltpu.CompilerParams(vmem_limit_bytes=16 * 1024 * 1024),
        name="hand_over",
    )(residual, updated)


def solution(mesh):
    in_specs = (
        P("pair", "aux", None),
        P(("pair", "aux"), None, None),
        P(("pair", "aux"), None, None),
        P(("pair", "aux"), None),
        P(("pair", "aux"), None),
        P(("pair", "aux")),
        P(("pair", "aux"), None),
        P(("pair", "aux"), None),
        P(("pair", "aux")),
    )
    out_specs = (P(("pair", "aux"), None, None), P(("pair", "aux"), None, None))
    return jax.shard_map(
        per_device, mesh=mesh, in_specs=in_specs, out_specs=out_specs, check_vma=False
    )
```

```python
import jax
import jax.numpy as jnp
from jax import lax
from jax.experimental import pallas as pl
from jax.experimental.pallas import tpu as pltpu
from jax.sharding import PartitionSpec as P

MESH = pl.DeviceIdType.MESH
F32 = jnp.float32
BF16 = jnp.bfloat16
CHUNK = 4
TOGETHER = 8


def contract(a, b, dim_a, dim_b):
    return lax.dot_general(a, b, (((dim_a,), (dim_b,)), ((), ())), preferred_element_type=F32)


def kernel(
    ints, amps_in, coeffs_in, domains_in, neighbours_in, counts_in, couplings_in, pno_in, occ_in,
    residual, updated,
    amps, coeffs, pao, doms, neighbours, counts, couplings, pno, occ, own, via, summed, arrived,
    acc, inverse, mine, flipped,
    amps_sem, coeffs_sem, load_sem, own_sem, via_sem, raw_send, raw_recv, near_send, near_recv,
    summed_send, summed_recv, halo_send, halo_recv, dom_send, dom_recv, pass_send, pass_dom_send, ready,
):
    n_pair, n_aux = lax.axis_size("pair"), lax.axis_size("aux")
    pair, aux = lax.axis_index("pair"), lax.axis_index("aux")
    pairs = amps.shape[0]
    half = pairs // 2
    depth = ints.shape[1]
    width = amps.shape[1]
    slots = neighbours.shape[0]
    chunks = half // CHUNK
    all_chunks = pairs // CHUNK

    up, down, far = (aux + 1) % n_aux, (aux + n_aux - 1) % n_aux, (aux + 2) % n_aux
    to_up, to_down = (pair, up), (pair, down)
    next_pair, last_pair = ((pair + 1) % n_pair, aux), ((pair + n_pair - 1) % n_pair, aux)
    first_end, last_end = aux == 0, aux == n_aux - 1
    at_end = jnp.logical_or(first_end, last_end)
    no_left = jnp.logical_and(first_end, pair == 0)
    no_right = jnp.logical_and(last_end, pair == n_pair - 1)
    passes = jnp.logical_or(
        jnp.logical_and(first_end, pair < n_pair - 1), jnp.logical_and(last_end, pair > 0)
    )

    barrier = pltpu.get_barrier_semaphore()

    def greet(semaphore, device):
        pl.semaphore_signal(semaphore, inc=1, device_id=device, device_id_type=MESH)

    greet(barrier, to_up)
    greet(barrier, to_down)

    @pl.when(at_end)
    def _():
        greet(barrier, last_pair)

    def remote(src, dst, send, recv, device):
        return pltpu.make_async_remote_copy(
            src_ref=src, dst_ref=dst, send_sem=send, recv_sem=recv, device_id=device, device_id_type=MESH
        )

    def rows(first, count=CHUNK):
        return pl.ds(first, count)

    matrix_loads = []
    for c in range(all_chunks):
        part = rows(c * CHUNK)
        matrix_loads.append(
            [
                pltpu.make_async_copy(coeffs_in.at[part], coeffs.at[part], coeffs_sem.at[c]),
                pltpu.make_async_copy(amps_in.at[part], amps.at[part], amps_sem.at[c]),
            ]
        )
    domain_load = pltpu.make_async_copy(domains_in, doms.at[rows(pairs, pairs)], load_sem.at[0])
    small_loads = [
        pltpu.make_async_copy(neighbours_in, neighbours, load_sem.at[1]),
        pltpu.make_async_copy(counts_in, counts, load_sem.at[2]),
        pltpu.make_async_copy(couplings_in, couplings, load_sem.at[3]),
        pltpu.make_async_copy(pno_in, pno, load_sem.at[4]),
        pltpu.make_async_copy(occ_in, occ, load_sem.at[5]),
    ]
    via_loads = [
        pltpu.make_async_copy(
            ints.at[rows(down * pairs, half)], via.at[0, :, pl.ds(0, depth)], via_sem.at[0]
        ),
        pltpu.make_async_copy(
            ints.at[rows(up * pairs + half, half)], via.at[1, :, pl.ds(0, depth)], via_sem.at[1]
        ),
    ]
    own_load = pltpu.make_async_copy(ints.at[rows(aux * pairs, pairs)], own.at[:, pl.ds(0, depth)], own_sem)
    for copy in sum(matrix_loads, []) + [domain_load] + small_loads + [own_load] + via_loads:
        copy.start()

    def to_pao(c):
        for copy in matrix_loads[c]:
            copy.wait()
        here = [c * CHUNK + i for i in range(CHUNK)]
        left_half = [contract(coeffs[p], amps[p], 1, 0).astype(BF16) for p in here]
        for p, block in zip(here, left_half):
            pao[pairs + p] = contract(block, coeffs[p], 1, 1).astype(BF16)

    early = all_chunks // 2

    pl.semaphore_wait(barrier, jnp.where(at_end, 3, 2))

    @pl.when(jnp.logical_and(last_end, pair < n_pair - 1))
    def _():
        greet(ready, next_pair)

    raw = [
        remote(
            ints.at[rows(far * pairs + side * half, half)],
            via.at[side, :, pl.ds(depth, depth)],
            raw_send.at[side],
            raw_recv.at[side],
            device,
        )
        for side, device in ((0, to_down), (1, to_up))
    ]
    near = [
        remote(
            ints.at[rows(there * pairs + side * half + c * CHUNK)],
            own.at[rows(side * half + c * CHUNK), pl.ds(depth, depth)],
            near_send.at[side, c],
            near_recv.at[side, c],
            device,
        )
        for c in range(chunks)
        for side, device, there in ((0, to_up, up), (1, to_down, down))
    ]
    for copy in near[:2]:
        copy.start()

    targets = (
        (0, to_up, jnp.where(last_end, 3, 0)),
        (1, to_down, jnp.where(first_end, 3, 2)),
    )
    domain_halo = [
        remote(
            doms.at[rows(pairs, pairs)],
            doms.at[rows(part * pairs, pairs)],
            dom_send.at[side],
            dom_recv.at[part],
            device,
        )
        for side, device, part in targets
    ]
    domain_load.wait()
    for copy in domain_halo:
        copy.start()
    halo = [
        [
            remote(
                pao.at[rows(pairs + c * CHUNK)],
                pao.at[rows(part * pairs + c * CHUNK)],
                halo_send.at[side, c],
                halo_recv.at[part, c],
                device,
            )
            for side, device, part in targets
        ]
        for c in range(all_chunks)
    ]

    for c in range(all_chunks):
        to_pao(c)
        for copy in halo[c]:
            copy.start()

    def arrival(part, c):
        return remote(
            pao.at[rows(pairs + c * CHUNK)],
            pao.at[rows(part * pairs + c * CHUNK)],
            halo_send.at[0, c],
            halo_recv.at[part, c],
            to_up,
        )

    def domain_arrival(part):
        return remote(
            doms.at[rows(pairs, pairs)], doms.at[rows(part * pairs, pairs)], dom_send.at[0], dom_recv.at[part], to_up
        )

    pass_to = (jnp.where(first_end, next_pair[0], last_pair[0]), aux)
    pass_part = jnp.where(first_end, 0, 2)
    domain_pass = remote(
        doms.at[rows(3 * pairs, pairs)],
        doms.at[rows(pass_part * pairs, pairs)],
        pass_dom_send,
        dom_recv.at[pass_part],
        pass_to,
    )
    passed = [
        remote(
            pao.at[rows(3 * pairs + c * CHUNK)],
            pao.at[rows(pass_part * pairs + c * CHUNK)],
            pass_send.at[c],
            halo_recv.at[pass_part, c],
            pass_to,
        )
        for c in range(all_chunks)
    ]

    def halo_sent(c):
        for copy in halo[c]:
            copy.wait_send()

    def pass_on(c):
        @pl.when(at_end)
        def _():
            if c == 0:
                domain_arrival(3).wait_recv()
            arrival(3, c).wait_recv()

        if c == 0:

            @pl.when(jnp.logical_and(last_end, pair > 0))
            def _():
                pl.semaphore_wait(ready, 1)

        @pl.when(passes)
        def _():
            if c == 0:
                domain_pass.start()
            passed[c].start()

    def prepare(first, count):
        for p in range(first, first + count):
            energies = jnp.broadcast_to(pno[pl.ds(p, 1), :], (width, width))
            denominator = energies.T + energies + occ[p]
            inverse[p] = 1.0 / denominator
            block = own[p, pl.ds(0, depth), :]
            exchange = contract(block[:, :width], block[:, width:], 0, 0)
            acc[p] = exchange + denominator * amps[p].astype(F32)
            mine[p] = jnp.broadcast_to(doms[pl.ds(pairs + p, 1), :], (width, width)).T
            flipped[p] = coeffs[p].T

    sums = [
        remote(
            summed.at[side, rows(c * CHUNK)],
            arrived.at[rows(side * half + c * CHUNK)],
            summed_send.at[side, c],
            summed_recv.at[side, c],
            device,
        )
        for c in range(chunks)
        for side, device in ((0, to_down), (1, to_up))
    ]

    for copy in small_loads:
        copy.wait()
    own_load.wait()
    for c in range(all_chunks):
        prepare(c * CHUNK, CHUNK)
        halo_sent(c)
        if c == 0:
            for copy in raw:
                copy.start()
        if c == early:
            for copy in near[2:]:
                copy.start()
        pass_on(c)

    for copy in via_loads:
        copy.wait()
    for copy in raw:
        copy.wait_recv()
    for c in range(chunks):
        for side in (1, 0):
            for p in range(c * CHUNK, c * CHUNK + CHUNK):
                block = via[side, p]
                summed[side, p] = contract(block[:, :width], block[:, width:], 0, 0).astype(BF16)
            sums[c * 2 + side].start()

    def add_near(c):
        for side in (0, 1):
            near[c * 2 + side].wait_recv()
            first = side * half + c * CHUNK
            for p in range(first, first + CHUNK):
                block = own[p, pl.ds(depth, depth), :]
                acc[p] += contract(block[:, :width], block[:, width:], 0, 0)

    add_near(0)

    for part, none in ((0, no_left), (2, no_right)):

        @pl.when(jnp.logical_not(none))
        def _():
            domain_arrival(part).wait_recv()
            for c in range(all_chunks):
                arrival(part, c).wait_recv()

        @pl.when(none)
        def _():
            doms[pl.ds(part * pairs, pairs), :] = jnp.full((pairs, width), -1, jnp.int32)
            pao[pl.ds(part * pairs, pairs)] = jnp.zeros((pairs, width, width), BF16)

    first_row = ((pair * n_aux + aux) - 1) * pairs

    def couple(step, carry):
        here = [step * TOGETHER + i for i in range(TOGETHER)]
        totals = []
        for p in here:
            column = mine[p]
            matches, scaled = [], []
            for k in range(slots):
                row = jnp.clip(neighbours[k, p] - first_row, 0, 3 * pairs - 1)
                weight = jnp.where(k < counts[p], couplings[k, p], 0.0)
                match = jnp.where(column == doms[pl.ds(row, 1), :], 1.0, 0.0).astype(BF16)
                picked = contract(match, pao[row], 1, 0)
                matches.append(match)
                scaled.append((weight * picked).astype(BF16))
            total = contract(jnp.concatenate(scaled, axis=1), jnp.concatenate(matches, axis=1), 1, 1)
            totals.append(total.astype(BF16))
        halves = [contract(total, coeffs[p], 1, 0).astype(BF16) for p, total in zip(here, totals)]
        for p, right_half in zip(here, halves):
            acc[p] += contract(flipped[p], right_half, 1, 0)
        return carry

    lax.fori_loop(0, pairs // TOGETHER, couple, 0)

    for c in range(1, chunks):
        add_near(c)
    for c in range(chunks):
        for side in (0, 1):
            sums[c * 2 + side].wait_recv()
            first = side * half + c * CHUNK
            for p in range(first, first + CHUNK):
                result = acc[p] + arrived[p].astype(F32)
                residual[p] = result
                updated[p] = (amps[p].astype(F32) - result * inverse[p]).astype(BF16)

    for copy in raw + near + sums + domain_halo:
        copy.wait_send()

    @pl.when(passes)
    def _():
        for copy in [domain_pass] + passed:
            copy.wait_send()


def hand_over(residual_in, updated_in, residual, updated, sems):
    copies = [
        pltpu.make_async_copy(residual_in, residual, sems.at[0]),
        pltpu.make_async_copy(updated_in, updated, sems.at[1]),
    ]
    for copy in copies:
        copy.start()
    for copy in copies:
        copy.wait()


def per_device(
    integrals,
    amplitudes,
    coeffs,
    domains,
    neighbours,
    counts,
    couplings,
    pno_energies,
    occ_energies,
):
    pairs, width, _ = amplitudes.shape
    depth = integrals.shape[1]
    half = pairs // 2
    chunks = half // CHUNK
    in_hbm = pl.BlockSpec(memory_space=pltpu.HBM)
    in_vmem = pl.BlockSpec(memory_space=pltpu.VMEM)
    dma = pltpu.SemaphoreType.DMA
    operands = (
        integrals, amplitudes, coeffs, domains, neighbours.T, counts, couplings.T, pno_energies, occ_energies,
    )
    residual, updated = pl.pallas_call(
        kernel,
        out_shape=(
            pltpu.VMEM((pairs, width, width), F32),
            pltpu.VMEM((pairs, width, width), BF16),
        ),
        in_specs=[in_hbm] * len(operands),
        out_specs=(in_vmem, in_vmem),
        scratch_shapes=[
            pltpu.VMEM((pairs, width, width), BF16),
            pltpu.VMEM((pairs, width, width), BF16),
            pltpu.VMEM((4 * pairs, width, width), BF16),
            pltpu.VMEM((4 * pairs, width), jnp.int32),
            pltpu.SMEM(neighbours.shape[::-1], jnp.int32),
            pltpu.SMEM(counts.shape, jnp.int32),
            pltpu.SMEM(couplings.shape[::-1], F32),
            pltpu.VMEM(pno_energies.shape, F32),
            pltpu.SMEM(occ_energies.shape, F32),
            pltpu.VMEM((pairs, 2 * depth, 2 * width), BF16),
            pltpu.VMEM((2, half, 2 * depth, 2 * width), BF16),
            pltpu.VMEM((2, half, width, width), BF16),
            pltpu.VMEM((pairs, width, width), BF16),
            pltpu.VMEM((pairs, width, width), F32),
            pltpu.VMEM((pairs, width, width), F32),
            pltpu.VMEM((pairs, width, width), jnp.int32),
            pltpu.VMEM((pairs, width, width), BF16),
            dma((2 * chunks,)),
            dma((2 * chunks,)),
            dma((6,)),
            dma(()),
            dma((2,)),
            dma((2,)),
            dma((2,)),
            dma((2, chunks)),
            dma((2, chunks)),
            dma((2, chunks)),
            dma((2, chunks)),
            dma((2, 2 * chunks)),
            dma((4, 2 * chunks)),
            dma((2,)),
            dma((4,)),
            dma((2 * chunks,)),
            dma(()),
            pltpu.SemaphoreType.REGULAR,
        ],
        compiler_params=pltpu.CompilerParams(
            collective_id=0, has_side_effects=True, vmem_limit_bytes=32 * 1024 * 1024
        ),
        name="doubles_residual",
    )(*(pltpu.with_memory_space_constraint(operand, pltpu.HBM) for operand in operands))
    return pl.pallas_call(
        hand_over,
        out_shape=(
            jax.ShapeDtypeStruct((pairs, width, width), F32),
            jax.ShapeDtypeStruct((pairs, width, width), BF16),
        ),
        in_specs=(pl.BlockSpec(memory_space=pl.ANY),) * 2,
        out_specs=(in_hbm, in_hbm),
        scratch_shapes=[dma((2,))],
        compiler_params=pltpu.CompilerParams(vmem_limit_bytes=16 * 1024 * 1024),
        name="hand_over",
    )(residual, updated)


def solution(mesh):
    in_specs = (
        P("pair", "aux", None),
        P(("pair", "aux"), None, None),
        P(("pair", "aux"), None, None),
        P(("pair", "aux"), None),
        P(("pair", "aux"), None),
        P(("pair", "aux")),
        P(("pair", "aux"), None),
        P(("pair", "aux"), None),
        P(("pair", "aux")),
    )
    out_specs = (P(("pair", "aux"), None, None), P(("pair", "aux"), None, None))
    return jax.shard_map(
        per_device, mesh=mesh, in_specs=in_specs, out_specs=out_specs, check_vma=False
    )
```

```python
import jax
import jax.numpy as jnp
from jax import lax
from jax.experimental import pallas as pl
from jax.experimental.pallas import tpu as pltpu
from jax.sharding import PartitionSpec as P

MESH = pl.DeviceIdType.MESH
F32 = jnp.float32
BF16 = jnp.bfloat16
CHUNK = 4
TOGETHER = 8


def contract(a, b, dim_a, dim_b):
    return lax.dot_general(a, b, (((dim_a,), (dim_b,)), ((), ())), preferred_element_type=F32)


def kernel(
    ints, amps_in, coeffs_in, domains_in, neighbours_in, counts_in, couplings_in, pno_in, occ_in,
    residual, updated,
    amps, coeffs, pao, doms, neighbours, counts, couplings, pno, occ, own, via, summed, arrived,
    acc, inverse, mine, flipped,
    amps_sem, coeffs_sem, load_sem, own_sem, via_sem, raw_send, raw_recv, near_send, near_recv,
    summed_send, summed_recv, halo_send, halo_recv, dom_send, dom_recv, pass_send, pass_dom_send, ready,
):
    n_pair, n_aux = lax.axis_size("pair"), lax.axis_size("aux")
    pair, aux = lax.axis_index("pair"), lax.axis_index("aux")
    pairs = amps.shape[0]
    half = pairs // 2
    depth = ints.shape[1]
    width = amps.shape[1]
    slots = neighbours.shape[0]
    chunks = half // CHUNK
    all_chunks = pairs // CHUNK

    up, down, far = (aux + 1) % n_aux, (aux + n_aux - 1) % n_aux, (aux + 2) % n_aux
    to_up, to_down = (pair, up), (pair, down)
    next_pair, last_pair = ((pair + 1) % n_pair, aux), ((pair + n_pair - 1) % n_pair, aux)
    first_end, last_end = aux == 0, aux == n_aux - 1
    at_end = jnp.logical_or(first_end, last_end)
    no_left = jnp.logical_and(first_end, pair == 0)
    no_right = jnp.logical_and(last_end, pair == n_pair - 1)
    passes = jnp.logical_or(
        jnp.logical_and(first_end, pair < n_pair - 1), jnp.logical_and(last_end, pair > 0)
    )

    barrier = pltpu.get_barrier_semaphore()

    def greet(semaphore, device):
        pl.semaphore_signal(semaphore, inc=1, device_id=device, device_id_type=MESH)

    greet(barrier, to_up)
    greet(barrier, to_down)

    @pl.when(at_end)
    def _():
        greet(barrier, last_pair)

    def remote(src, dst, send, recv, device):
        return pltpu.make_async_remote_copy(
            src_ref=src, dst_ref=dst, send_sem=send, recv_sem=recv, device_id=device, device_id_type=MESH
        )

    def rows(first, count=CHUNK):
        return pl.ds(first, count)

    matrix_loads = []
    for c in range(all_chunks):
        part = rows(c * CHUNK)
        matrix_loads.append(
            [
                pltpu.make_async_copy(coeffs_in.at[part], coeffs.at[part], coeffs_sem.at[c]),
                pltpu.make_async_copy(amps_in.at[part], amps.at[part], amps_sem.at[c]),
            ]
        )
    domain_load = pltpu.make_async_copy(domains_in, doms.at[rows(pairs, pairs)], load_sem.at[0])
    small_loads = [
        pltpu.make_async_copy(neighbours_in, neighbours, load_sem.at[1]),
        pltpu.make_async_copy(counts_in, counts, load_sem.at[2]),
        pltpu.make_async_copy(couplings_in, couplings, load_sem.at[3]),
        pltpu.make_async_copy(pno_in, pno, load_sem.at[4]),
        pltpu.make_async_copy(occ_in, occ, load_sem.at[5]),
    ]
    via_loads = [
        pltpu.make_async_copy(
            ints.at[rows(down * pairs, half)], via.at[0, :, pl.ds(0, depth)], via_sem.at[0]
        ),
        pltpu.make_async_copy(
            ints.at[rows(up * pairs + half, half)], via.at[1, :, pl.ds(0, depth)], via_sem.at[1]
        ),
    ]
    own_load = pltpu.make_async_copy(ints.at[rows(aux * pairs, pairs)], own.at[:, pl.ds(0, depth)], own_sem)
    for copy in sum(matrix_loads, []) + [domain_load] + small_loads + [own_load] + via_loads:
        copy.start()

    def to_pao(c):
        for copy in matrix_loads[c]:
            copy.wait()
        here = [c * CHUNK + i for i in range(CHUNK)]
        left_half = [contract(coeffs[p], amps[p], 1, 0).astype(BF16) for p in here]
        for p, block in zip(here, left_half):
            pao[pairs + p] = contract(block, coeffs[p], 1, 1).astype(BF16)

    early = all_chunks // 2

    pl.semaphore_wait(barrier, jnp.where(at_end, 3, 2))

    @pl.when(jnp.logical_and(last_end, pair < n_pair - 1))
    def _():
        greet(ready, next_pair)

    raw = [
        remote(
            ints.at[rows(far * pairs + side * half + c * CHUNK)],
            via.at[side, rows(c * CHUNK), pl.ds(depth, depth)],
            raw_send.at[side, c],
            raw_recv.at[side, c],
            device,
        )
        for c in range(chunks)
        for side, device in ((0, to_down), (1, to_up))
    ]
    near = [
        remote(
            ints.at[rows(there * pairs + side * half + c * CHUNK)],
            own.at[rows(side * half + c * CHUNK), pl.ds(depth, depth)],
            near_send.at[side, c],
            near_recv.at[side, c],
            device,
        )
        for c in range(chunks)
        for side, device, there in ((0, to_up, up), (1, to_down, down))
    ]
    for copy in near[:2]:
        copy.start()

    targets = (
        (0, to_up, jnp.where(last_end, 3, 0)),
        (1, to_down, jnp.where(first_end, 3, 2)),
    )
    domain_halo = [
        remote(
            doms.at[rows(pairs, pairs)],
            doms.at[rows(part * pairs, pairs)],
            dom_send.at[side],
            dom_recv.at[part],
            device,
        )
        for side, device, part in targets
    ]
    domain_load.wait()
    for copy in domain_halo:
        copy.start()
    halo = [
        [
            remote(
                pao.at[rows(pairs + c * CHUNK)],
                pao.at[rows(part * pairs + c * CHUNK)],
                halo_send.at[side, c],
                halo_recv.at[part, c],
                device,
            )
            for side, device, part in targets
        ]
        for c in range(all_chunks)
    ]

    for c in range(all_chunks):
        to_pao(c)
        for copy in halo[c]:
            copy.start()

    def arrival(part, c):
        return remote(
            pao.at[rows(pairs + c * CHUNK)],
            pao.at[rows(part * pairs + c * CHUNK)],
            halo_send.at[0, c],
            halo_recv.at[part, c],
            to_up,
        )

    def domain_arrival(part):
        return remote(
            doms.at[rows(pairs, pairs)], doms.at[rows(part * pairs, pairs)], dom_send.at[0], dom_recv.at[part], to_up
        )

    pass_to = (jnp.where(first_end, next_pair[0], last_pair[0]), aux)
    pass_part = jnp.where(first_end, 0, 2)
    domain_pass = remote(
        doms.at[rows(3 * pairs, pairs)],
        doms.at[rows(pass_part * pairs, pairs)],
        pass_dom_send,
        dom_recv.at[pass_part],
        pass_to,
    )
    passed = [
        remote(
            pao.at[rows(3 * pairs + c * CHUNK)],
            pao.at[rows(pass_part * pairs + c * CHUNK)],
            pass_send.at[c],
            halo_recv.at[pass_part, c],
            pass_to,
        )
        for c in range(all_chunks)
    ]

    def halo_sent(c):
        for copy in halo[c]:
            copy.wait_send()

    def pass_on(c):
        @pl.when(at_end)
        def _():
            if c == 0:
                domain_arrival(3).wait_recv()
            arrival(3, c).wait_recv()

        if c == 0:

            @pl.when(jnp.logical_and(last_end, pair > 0))
            def _():
                pl.semaphore_wait(ready, 1)

        @pl.when(passes)
        def _():
            if c == 0:
                domain_pass.start()
            passed[c].start()

    def prepare(first, count):
        for p in range(first, first + count):
            energies = jnp.broadcast_to(pno[pl.ds(p, 1), :], (width, width))
            denominator = energies.T + energies + occ[p]
            inverse[p] = 1.0 / denominator
            block = own[p, pl.ds(0, depth), :]
            exchange = contract(block[:, :width], block[:, width:], 0, 0)
            acc[p] = exchange + denominator * amps[p].astype(F32)
            mine[p] = jnp.broadcast_to(doms[pl.ds(pairs + p, 1), :], (width, width)).T
            flipped[p] = coeffs[p].T

    sums = [
        remote(
            summed.at[side, rows(c * CHUNK)],
            arrived.at[rows(side * half + c * CHUNK)],
            summed_send.at[side, c],
            summed_recv.at[side, c],
            device,
        )
        for c in range(chunks)
        for side, device in ((0, to_down), (1, to_up))
    ]

    for copy in small_loads:
        copy.wait()
    own_load.wait()
    for c in range(all_chunks):
        prepare(c * CHUNK, CHUNK)
        halo_sent(c)
        if c == 0:
            for copy in raw:
                copy.start()
        if c == early:
            for copy in near[2:]:
                copy.start()
        pass_on(c)

    for copy in via_loads:
        copy.wait()
    for c in range(chunks):
        for side in (1, 0):
            raw[c * 2 + side].wait_recv()
            for p in range(c * CHUNK, c * CHUNK + CHUNK):
                block = via[side, p]
                summed[side, p] = contract(block[:, :width], block[:, width:], 0, 0).astype(BF16)
            sums[c * 2 + side].start()

    def add_near(c):
        for side in (0, 1):
            near[c * 2 + side].wait_recv()
            first = side * half + c * CHUNK
            for p in range(first, first + CHUNK):
                block = own[p, pl.ds(depth, depth), :]
                acc[p] += contract(block[:, :width], block[:, width:], 0, 0)

    add_near(0)

    for part, none in ((0, no_left), (2, no_right)):

        @pl.when(jnp.logical_not(none))
        def _():
            domain_arrival(part).wait_recv()
            for c in range(all_chunks):
                arrival(part, c).wait_recv()

        @pl.when(none)
        def _():
            doms[pl.ds(part * pairs, pairs), :] = jnp.full((pairs, width), -1, jnp.int32)
            pao[pl.ds(part * pairs, pairs)] = jnp.zeros((pairs, width, width), BF16)

    first_row = ((pair * n_aux + aux) - 1) * pairs

    def couple(step, carry):
        here = [step * TOGETHER + i for i in range(TOGETHER)]
        totals = []
        for p in here:
            column = mine[p]
            matches, scaled = [], []
            for k in range(slots):
                row = jnp.clip(neighbours[k, p] - first_row, 0, 3 * pairs - 1)
                weight = jnp.where(k < counts[p], couplings[k, p], 0.0)
                match = jnp.where(column == doms[pl.ds(row, 1), :], 1.0, 0.0).astype(BF16)
                picked = contract(match, pao[row], 1, 0)
                matches.append(match)
                scaled.append((weight * picked).astype(BF16))
            total = contract(jnp.concatenate(scaled, axis=1), jnp.concatenate(matches, axis=1), 1, 1)
            totals.append(total.astype(BF16))
        halves = [contract(total, coeffs[p], 1, 0).astype(BF16) for p, total in zip(here, totals)]
        for p, right_half in zip(here, halves):
            acc[p] += contract(flipped[p], right_half, 1, 0)
        return carry

    lax.fori_loop(0, pairs // TOGETHER, couple, 0)

    for c in range(1, chunks):
        add_near(c)
    for c in range(chunks):
        for side in (1, 0):
            sums[c * 2 + side].wait_recv()
            first = side * half + c * CHUNK
            for p in range(first, first + CHUNK):
                result = acc[p] + arrived[p].astype(F32)
                residual[p] = result
                updated[p] = (amps[p].astype(F32) - result * inverse[p]).astype(BF16)

    for copy in raw + near + sums + domain_halo:
        copy.wait_send()

    @pl.when(passes)
    def _():
        for copy in [domain_pass] + passed:
            copy.wait_send()


def hand_over(residual_in, updated_in, residual, updated, sems):
    copies = [
        pltpu.make_async_copy(residual_in, residual, sems.at[0]),
        pltpu.make_async_copy(updated_in, updated, sems.at[1]),
    ]
    for copy in copies:
        copy.start()
    for copy in copies:
        copy.wait()


def per_device(
    integrals,
    amplitudes,
    coeffs,
    domains,
    neighbours,
    counts,
    couplings,
    pno_energies,
    occ_energies,
):
    pairs, width, _ = amplitudes.shape
    depth = integrals.shape[1]
    half = pairs // 2
    chunks = half // CHUNK
    in_hbm = pl.BlockSpec(memory_space=pltpu.HBM)
    in_vmem = pl.BlockSpec(memory_space=pltpu.VMEM)
    dma = pltpu.SemaphoreType.DMA
    operands = (
        integrals, amplitudes, coeffs, domains, neighbours.T, counts, couplings.T, pno_energies, occ_energies,
    )
    residual, updated = pl.pallas_call(
        kernel,
        out_shape=(
            pltpu.VMEM((pairs, width, width), F32),
            pltpu.VMEM((pairs, width, width), BF16),
        ),
        in_specs=[in_hbm] * len(operands),
        out_specs=(in_vmem, in_vmem),
        scratch_shapes=[
            pltpu.VMEM((pairs, width, width), BF16),
            pltpu.VMEM((pairs, width, width), BF16),
            pltpu.VMEM((4 * pairs, width, width), BF16),
            pltpu.VMEM((4 * pairs, width), jnp.int32),
            pltpu.SMEM(neighbours.shape[::-1], jnp.int32),
            pltpu.SMEM(counts.shape, jnp.int32),
            pltpu.SMEM(couplings.shape[::-1], F32),
            pltpu.VMEM(pno_energies.shape, F32),
            pltpu.SMEM(occ_energies.shape, F32),
            pltpu.VMEM((pairs, 2 * depth, 2 * width), BF16),
            pltpu.VMEM((2, half, 2 * depth, 2 * width), BF16),
            pltpu.VMEM((2, half, width, width), BF16),
            pltpu.VMEM((pairs, width, width), BF16),
            pltpu.VMEM((pairs, width, width), F32),
            pltpu.VMEM((pairs, width, width), F32),
            pltpu.VMEM((pairs, width, width), jnp.int32),
            pltpu.VMEM((pairs, width, width), BF16),
            dma((2 * chunks,)),
            dma((2 * chunks,)),
            dma((6,)),
            dma(()),
            dma((2,)),
            dma((2, chunks)),
            dma((2, chunks)),
            dma((2, chunks)),
            dma((2, chunks)),
            dma((2, chunks)),
            dma((2, chunks)),
            dma((2, 2 * chunks)),
            dma((4, 2 * chunks)),
            dma((2,)),
            dma((4,)),
            dma((2 * chunks,)),
            dma(()),
            pltpu.SemaphoreType.REGULAR,
        ],
        compiler_params=pltpu.CompilerParams(
            collective_id=0, has_side_effects=True, vmem_limit_bytes=32 * 1024 * 1024
        ),
        name="doubles_residual",
    )(*(pltpu.with_memory_space_constraint(operand, pltpu.HBM) for operand in operands))
    return pl.pallas_call(
        hand_over,
        out_shape=(
            jax.ShapeDtypeStruct((pairs, width, width), F32),
            jax.ShapeDtypeStruct((pairs, width, width), BF16),
        ),
        in_specs=(pl.BlockSpec(memory_space=pl.ANY),) * 2,
        out_specs=(in_hbm, in_hbm),
        scratch_shapes=[dma((2,))],
        compiler_params=pltpu.CompilerParams(vmem_limit_bytes=16 * 1024 * 1024),
        name="hand_over",
    )(residual, updated)


def solution(mesh):
    in_specs = (
        P("pair", "aux", None),
        P(("pair", "aux"), None, None),
        P(("pair", "aux"), None, None),
        P(("pair", "aux"), None),
        P(("pair", "aux"), None),
        P(("pair", "aux")),
        P(("pair", "aux"), None),
        P(("pair", "aux"), None),
        P(("pair", "aux")),
    )
    out_specs = (P(("pair", "aux"), None, None), P(("pair", "aux"), None, None))
    return jax.shard_map(
        per_device, mesh=mesh, in_specs=in_specs, out_specs=out_specs, check_vma=False
    )
```

```python
import jax
import jax.numpy as jnp
from jax import lax
from jax.experimental import pallas as pl
from jax.experimental.pallas import tpu as pltpu
from jax.sharding import PartitionSpec as P

MESH = pl.DeviceIdType.MESH
F32 = jnp.float32
BF16 = jnp.bfloat16
CHUNK = 4
TOGETHER = 8


def contract(a, b, dim_a, dim_b):
    return lax.dot_general(a, b, (((dim_a,), (dim_b,)), ((), ())), preferred_element_type=F32)


def kernel(
    ints, amps_in, coeffs_in, domains_in, neighbours_in, counts_in, couplings_in, pno_in, occ_in,
    residual, updated,
    amps, coeffs, pao, doms, neighbours, counts, couplings, pno, occ, own, via, summed, arrived,
    acc, inverse, mine, flipped,
    amps_sem, coeffs_sem, load_sem, own_sem, via_sem, raw_send, raw_recv, near_send, near_recv,
    summed_send, summed_recv, halo_send, halo_recv, dom_send, dom_recv, pass_send, pass_dom_send, ready,
):
    n_pair, n_aux = lax.axis_size("pair"), lax.axis_size("aux")
    pair, aux = lax.axis_index("pair"), lax.axis_index("aux")
    pairs = amps.shape[0]
    half = pairs // 2
    depth = ints.shape[1]
    width = amps.shape[1]
    slots = neighbours.shape[0]
    chunks = half // CHUNK
    all_chunks = pairs // CHUNK

    up, down, far = (aux + 1) % n_aux, (aux + n_aux - 1) % n_aux, (aux + 2) % n_aux
    to_up, to_down = (pair, up), (pair, down)
    next_pair, last_pair = ((pair + 1) % n_pair, aux), ((pair + n_pair - 1) % n_pair, aux)
    first_end, last_end = aux == 0, aux == n_aux - 1
    at_end = jnp.logical_or(first_end, last_end)
    no_left = jnp.logical_and(first_end, pair == 0)
    no_right = jnp.logical_and(last_end, pair == n_pair - 1)
    passes = jnp.logical_or(
        jnp.logical_and(first_end, pair < n_pair - 1), jnp.logical_and(last_end, pair > 0)
    )

    barrier = pltpu.get_barrier_semaphore()

    def greet(semaphore, device):
        pl.semaphore_signal(semaphore, inc=1, device_id=device, device_id_type=MESH)

    greet(barrier, to_up)
    greet(barrier, to_down)

    @pl.when(at_end)
    def _():
        greet(barrier, last_pair)

    def remote(src, dst, send, recv, device):
        return pltpu.make_async_remote_copy(
            src_ref=src, dst_ref=dst, send_sem=send, recv_sem=recv, device_id=device, device_id_type=MESH
        )

    def rows(first, count=CHUNK):
        return pl.ds(first, count)

    matrix_loads = []
    for c in range(all_chunks):
        part = rows(c * CHUNK)
        matrix_loads.append(
            [
                pltpu.make_async_copy(coeffs_in.at[part], coeffs.at[part], coeffs_sem.at[c]),
                pltpu.make_async_copy(amps_in.at[part], amps.at[part], amps_sem.at[c]),
            ]
        )
    domain_load = pltpu.make_async_copy(domains_in, doms.at[rows(pairs, pairs)], load_sem.at[0])
    small_loads = [
        pltpu.make_async_copy(neighbours_in, neighbours, load_sem.at[1]),
        pltpu.make_async_copy(counts_in, counts, load_sem.at[2]),
        pltpu.make_async_copy(couplings_in, couplings, load_sem.at[3]),
        pltpu.make_async_copy(pno_in, pno, load_sem.at[4]),
        pltpu.make_async_copy(occ_in, occ, load_sem.at[5]),
    ]
    via_loads = [
        pltpu.make_async_copy(
            ints.at[rows(down * pairs, half)], via.at[0, :, pl.ds(0, depth)], via_sem.at[0]
        ),
        pltpu.make_async_copy(
            ints.at[rows(up * pairs + half, half)], via.at[1, :, pl.ds(0, depth)], via_sem.at[1]
        ),
    ]
    own_load = pltpu.make_async_copy(ints.at[rows(aux * pairs, pairs)], own.at[:, pl.ds(0, depth)], own_sem)
    for copy in sum(matrix_loads, []) + [domain_load] + small_loads + [own_load] + via_loads:
        copy.start()

    def to_pao(c):
        for copy in matrix_loads[c]:
            copy.wait()
        here = [c * CHUNK + i for i in range(CHUNK)]
        left_half = [contract(coeffs[p], amps[p], 1, 0).astype(BF16) for p in here]
        for p, block in zip(here, left_half):
            pao[pairs + p] = contract(block, coeffs[p], 1, 1).astype(BF16)

    early = all_chunks // 2

    pl.semaphore_wait(barrier, jnp.where(at_end, 3, 2))

    @pl.when(jnp.logical_and(last_end, pair < n_pair - 1))
    def _():
        greet(ready, next_pair)

    raw = [
        remote(
            ints.at[rows(far * pairs + side * half, half)],
            via.at[side, :, pl.ds(depth, depth)],
            raw_send.at[side],
            raw_recv.at[side],
            device,
        )
        for side, device in ((0, to_down), (1, to_up))
    ]
    near = [
        remote(
            ints.at[rows(there * pairs + side * half + c * CHUNK)],
            own.at[rows(side * half + c * CHUNK), pl.ds(depth, depth)],
            near_send.at[side, c],
            near_recv.at[side, c],
            device,
        )
        for c in range(chunks)
        for side, device, there in ((0, to_up, up), (1, to_down, down))
    ]
    for copy in near[:2]:
        copy.start()

    targets = (
        (0, to_up, jnp.where(last_end, 3, 0)),
        (1, to_down, jnp.where(first_end, 3, 2)),
    )
    domain_halo = [
        remote(
            doms.at[rows(pairs, pairs)],
            doms.at[rows(part * pairs, pairs)],
            dom_send.at[side],
            dom_recv.at[part],
            device,
        )
        for side, device, part in targets
    ]
    domain_load.wait()
    for copy in domain_halo:
        copy.start()
    halo = [
        [
            remote(
                pao.at[rows(pairs + c * CHUNK)],
                pao.at[rows(part * pairs + c * CHUNK)],
                halo_send.at[side, c],
                halo_recv.at[part, c],
                device,
            )
            for side, device, part in targets
        ]
        for c in range(all_chunks)
    ]

    for c in range(all_chunks):
        to_pao(c)
        for copy in halo[c]:
            copy.start()

    def arrival(part, c):
        return remote(
            pao.at[rows(pairs + c * CHUNK)],
            pao.at[rows(part * pairs + c * CHUNK)],
            halo_send.at[0, c],
            halo_recv.at[part, c],
            to_up,
        )

    def domain_arrival(part):
        return remote(
            doms.at[rows(pairs, pairs)], doms.at[rows(part * pairs, pairs)], dom_send.at[0], dom_recv.at[part], to_up
        )

    pass_to = (jnp.where(first_end, next_pair[0], last_pair[0]), aux)
    pass_part = jnp.where(first_end, 0, 2)
    domain_pass = remote(
        doms.at[rows(3 * pairs, pairs)],
        doms.at[rows(pass_part * pairs, pairs)],
        pass_dom_send,
        dom_recv.at[pass_part],
        pass_to,
    )
    passed = [
        remote(
            pao.at[rows(3 * pairs + c * CHUNK)],
            pao.at[rows(pass_part * pairs + c * CHUNK)],
            pass_send.at[c],
            halo_recv.at[pass_part, c],
            pass_to,
        )
        for c in range(all_chunks)
    ]

    def halo_sent(c):
        for copy in halo[c]:
            copy.wait_send()

    def pass_on(c):
        @pl.when(at_end)
        def _():
            if c == 0:
                domain_arrival(3).wait_recv()
            arrival(3, c).wait_recv()

        if c == 0:

            @pl.when(jnp.logical_and(last_end, pair > 0))
            def _():
                pl.semaphore_wait(ready, 1)

        @pl.when(passes)
        def _():
            if c == 0:
                domain_pass.start()
            passed[c].start()

    def prepare(first, count):
        for p in range(first, first + count):
            energies = jnp.broadcast_to(pno[pl.ds(p, 1), :], (width, width))
            denominator = energies.T + energies + occ[p]
            inverse[p] = 1.0 / denominator
            block = own[p, pl.ds(0, depth), :]
            exchange = contract(block[:, :width], block[:, width:], 0, 0)
            acc[p] = exchange + denominator * amps[p].astype(F32)
            mine[p] = jnp.broadcast_to(doms[pl.ds(pairs + p, 1), :], (width, width)).T
            flipped[p] = coeffs[p].T

    sums = [
        remote(
            summed.at[side, rows(c * CHUNK)],
            arrived.at[rows(side * half + c * CHUNK)],
            summed_send.at[side, c],
            summed_recv.at[side, c],
            device,
        )
        for c in range(chunks)
        for side, device in ((0, to_down), (1, to_up))
    ]

    for copy in small_loads:
        copy.wait()
    own_load.wait()
    for c in range(all_chunks):
        prepare(c * CHUNK, CHUNK)
        halo_sent(c)
        if c == 0:
            for copy in raw:
                copy.start()
        if c == early:
            for copy in near[2:]:
                copy.start()
        pass_on(c)

    for copy in via_loads:
        copy.wait()
    for copy in raw:
        copy.wait_recv()
    for c in range(chunks):
        for side in (0, 1):
            for p in range(c * CHUNK, c * CHUNK + CHUNK):
                block = via[side, p]
                summed[side, p] = contract(block[:, :width], block[:, width:], 0, 0).astype(BF16)
            sums[c * 2 + side].start()

    def add_near(c):
        for side in (0, 1):
            near[c * 2 + side].wait_recv()
            first = side * half + c * CHUNK
            for p in range(first, first + CHUNK):
                block = own[p, pl.ds(depth, depth), :]
                acc[p] += contract(block[:, :width], block[:, width:], 0, 0)

    add_near(0)

    for part, none in ((0, no_left), (2, no_right)):

        @pl.when(jnp.logical_not(none))
        def _():
            domain_arrival(part).wait_recv()
            for c in range(all_chunks):
                arrival(part, c).wait_recv()

        @pl.when(none)
        def _():
            doms[pl.ds(part * pairs, pairs), :] = jnp.full((pairs, width), -1, jnp.int32)
            pao[pl.ds(part * pairs, pairs)] = jnp.zeros((pairs, width, width), BF16)

    first_row = ((pair * n_aux + aux) - 1) * pairs

    def couple(step, carry):
        here = [step * TOGETHER + i for i in range(TOGETHER)]
        totals = []
        for p in here:
            column = mine[p]
            matches, scaled = [], []
            for k in range(slots):
                row = jnp.clip(neighbours[k, p] - first_row, 0, 3 * pairs - 1)
                weight = jnp.where(k < counts[p], couplings[k, p], 0.0)
                match = jnp.where(column == doms[pl.ds(row, 1), :], 1.0, 0.0).astype(BF16)
                picked = contract(match, pao[row], 1, 0)
                matches.append(match)
                scaled.append((weight * picked).astype(BF16))
            total = contract(jnp.concatenate(scaled, axis=1), jnp.concatenate(matches, axis=1), 1, 1)
            totals.append(total.astype(BF16))
        halves = [contract(total, coeffs[p], 1, 0).astype(BF16) for p, total in zip(here, totals)]
        for p, right_half in zip(here, halves):
            acc[p] += contract(flipped[p], right_half, 1, 0)
        return carry

    lax.fori_loop(0, pairs // TOGETHER, couple, 0)

    for c in range(1, chunks):
        add_near(c)
    for c in range(chunks):
        for side in (0, 1):
            sums[c * 2 + side].wait_recv()
            first = side * half + c * CHUNK
            for p in range(first, first + CHUNK):
                result = acc[p] + arrived[p].astype(F32)
                residual[p] = result
                updated[p] = (amps[p].astype(F32) - result * inverse[p]).astype(BF16)

    for copy in raw + near + sums + domain_halo:
        copy.wait_send()

    @pl.when(passes)
    def _():
        for copy in [domain_pass] + passed:
            copy.wait_send()


def hand_over(residual_in, updated_in, residual, updated, sems):
    copies = [
        pltpu.make_async_copy(residual_in, residual, sems.at[0]),
        pltpu.make_async_copy(updated_in, updated, sems.at[1]),
    ]
    for copy in copies:
        copy.start()
    for copy in copies:
        copy.wait()


def per_device(
    integrals,
    amplitudes,
    coeffs,
    domains,
    neighbours,
    counts,
    couplings,
    pno_energies,
    occ_energies,
):
    pairs, width, _ = amplitudes.shape
    depth = integrals.shape[1]
    half = pairs // 2
    chunks = half // CHUNK
    in_hbm = pl.BlockSpec(memory_space=pltpu.HBM)
    in_vmem = pl.BlockSpec(memory_space=pltpu.VMEM)
    dma = pltpu.SemaphoreType.DMA
    operands = (
        integrals, amplitudes, coeffs, domains, neighbours.T, counts, couplings.T, pno_energies, occ_energies,
    )
    residual, updated = pl.pallas_call(
        kernel,
        out_shape=(
            pltpu.VMEM((pairs, width, width), F32),
            pltpu.VMEM((pairs, width, width), BF16),
        ),
        in_specs=[in_hbm] * len(operands),
        out_specs=(in_vmem, in_vmem),
        scratch_shapes=[
            pltpu.VMEM((pairs, width, width), BF16),
            pltpu.VMEM((pairs, width, width), BF16),
            pltpu.VMEM((4 * pairs, width, width), BF16),
            pltpu.VMEM((4 * pairs, width), jnp.int32),
            pltpu.SMEM(neighbours.shape[::-1], jnp.int32),
            pltpu.SMEM(counts.shape, jnp.int32),
            pltpu.SMEM(couplings.shape[::-1], F32),
            pltpu.VMEM(pno_energies.shape, F32),
            pltpu.SMEM(occ_energies.shape, F32),
            pltpu.VMEM((pairs, 2 * depth, 2 * width), BF16),
            pltpu.VMEM((2, half, 2 * depth, 2 * width), BF16),
            pltpu.VMEM((2, half, width, width), BF16),
            pltpu.VMEM((pairs, width, width), BF16),
            pltpu.VMEM((pairs, width, width), F32),
            pltpu.VMEM((pairs, width, width), F32),
            pltpu.VMEM((pairs, width, width), jnp.int32),
            pltpu.VMEM((pairs, width, width), BF16),
            dma((2 * chunks,)),
            dma((2 * chunks,)),
            dma((6,)),
            dma(()),
            dma((2,)),
            dma((2,)),
            dma((2,)),
            dma((2, chunks)),
            dma((2, chunks)),
            dma((2, chunks)),
            dma((2, chunks)),
            dma((2, 2 * chunks)),
            dma((4, 2 * chunks)),
            dma((2,)),
            dma((4,)),
            dma((2 * chunks,)),
            dma(()),
            pltpu.SemaphoreType.REGULAR,
        ],
        compiler_params=pltpu.CompilerParams(
            collective_id=0, has_side_effects=True, vmem_limit_bytes=32 * 1024 * 1024
        ),
        name="doubles_residual",
    )(*(pltpu.with_memory_space_constraint(operand, pltpu.HBM) for operand in operands))
    return pl.pallas_call(
        hand_over,
        out_shape=(
            jax.ShapeDtypeStruct((pairs, width, width), F32),
            jax.ShapeDtypeStruct((pairs, width, width), BF16),
        ),
        in_specs=(pl.BlockSpec(memory_space=pl.ANY),) * 2,
        out_specs=(in_hbm, in_hbm),
        scratch_shapes=[dma((2,))],
        compiler_params=pltpu.CompilerParams(vmem_limit_bytes=16 * 1024 * 1024),
        name="hand_over",
    )(residual, updated)


def solution(mesh):
    in_specs = (
        P("pair", "aux", None),
        P(("pair", "aux"), None, None),
        P(("pair", "aux"), None, None),
        P(("pair", "aux"), None),
        P(("pair", "aux"), None),
        P(("pair", "aux")),
        P(("pair", "aux"), None),
        P(("pair", "aux"), None),
        P(("pair", "aux")),
    )
    out_specs = (P(("pair", "aux"), None, None), P(("pair", "aux"), None, None))
    return jax.shard_map(
        per_device, mesh=mesh, in_specs=in_specs, out_specs=out_specs, check_vma=False
    )
```
